32 devices in a mesh: section: 2 (over x), seq: 4 (over z), fsdp: 4 (over y, core).
Axes of the slice: x: 2, y: 2, z: 4, core: 2. Of those that a mesh axis runs over, the one named last changes fastest.
Arguments:
- ends: bfloat16 [2, 2, 4, 1024, 1536], P('section', None, 'fsdp', 'seq'), may hold values from -6 to 6
- segment_ids: int32 [2, 4, 1024], P(None, 'fsdp'), may hold values from 0 to 3, as said below
- norm_one: bfloat16 [2, 1536], P('section', ('seq', 'fsdp')), may hold values from 0.099609375 to 1.8984375
- w_branch: bfloat16 [2, 1536, 2048], P('section', ('seq', 'fsdp')), may hold values from -0.15625 to 0.15625
- w_input: bfloat16 [2, 1536, 2048], P('section', ('seq', 'fsdp')), may hold values from -0.15625 to 0.15625
- conv_weight: bfloat16 [2, 4, 2048], P('section', None, ('seq', 'fsdp')), may hold values from -3 to 3
- conv_bias: bfloat16 [2, 2048], P('section', ('seq', 'fsdp')), may hold values from -3 to 3
- gate_a: bfloat16 [2, 16, 128, 128], P('section', None, ('seq', 'fsdp')), may hold values from -0.5 to 0.5
- gate_i: bfloat16 [2, 16, 128, 128], P('section', None, ('seq', 'fsdp')), may hold values from -0.5 to 0.5
- bias_a: bfloat16 [2, 2048], P('section', ('seq', 'fsdp')), may hold values from -4 to 4
- bias_i: bfloat16 [2, 2048], P('section', ('seq', 'fsdp')), may hold values from -4 to 4
- decay: bfloat16 [2, 2048], P('section', ('seq', 'fsdp')), may hold values from -12 to -4
- w_out: bfloat16 [2, 2048, 1536], P('section', ('seq', 'fsdp')), may hold values from -0.375 to 0.375
- norm_two: bfloat16 [2, 1536], P('section', ('seq', 'fsdp')), may hold values from 0.099609375 to 1.8984375
- w_gate: bfloat16 [2, 1536, 4608], P('section', ('seq', 'fsdp')), may hold values from -0.15625 to 0.15625
- w_up: bfloat16 [2, 1536, 4608], P('section', ('seq', 'fsdp')), may hold values from -0.15625 to 0.15625
- w_down: bfloat16 [2, 4608, 1536], P('section', ('seq', 'fsdp')), may hold values from -0.15625 to 0.15625
Outputs:
- section_outputs: bfloat16 [2, 2, 4, 1024, 1536], P('section', None, 'fsdp', 'seq')
- input_grads: bfloat16 [2, 2, 4, 1024, 1536], P('section', None, 'fsdp', 'seq')
- grad_norm_one: float32 [2, 1536], P('section', ('seq', 'fsdp'))
- grad_w_branch: float32 [2, 1536, 2048], P('section', ('seq', 'fsdp'))
- grad_w_input: float32 [2, 1536, 2048], P('section', ('seq', 'fsdp'))
- grad_conv_weight: float32 [2, 4, 2048], P('section', None, ('seq', 'fsdp'))
- grad_conv_bias: float32 [2, 2048], P('section', ('seq', 'fsdp'))
- grad_gate_a: float32 [2, 16, 128, 128], P('section', None, ('seq', 'fsdp'))
- grad_gate_i: float32 [2, 16, 128, 128], P('section', None, ('seq', 'fsdp'))
- grad_bias_a: float32 [2, 2048], P('section', ('seq', 'fsdp'))
- grad_bias_i: float32 [2, 2048], P('section', ('seq', 'fsdp'))
- grad_decay: float32 [2, 2048], P('section', ('seq', 'fsdp'))
- grad_w_out: float32 [2, 2048, 1536], P('section', ('seq', 'fsdp'))
- grad_norm_two: float32 [2, 1536], P('section', ('seq', 'fsdp'))
- grad_w_gate: float32 [2, 1536, 4608], P('section', ('seq', 'fsdp'))
- grad_w_up: float32 [2, 1536, 4608], P('section', ('seq', 'fsdp'))
- grad_w_down: float32 [2, 4608, 1536], P('section', ('seq', 'fsdp'))
The draws below stay inside these ranges and needn't reach their ends.
Inputs may be any that keep to these rules, and one draw needn't show every extreme that they name: `segment_ids`: within each sequence the ids start at 0, never fall, and rise where a document begins; for each index of the second dimension one micro-batch's sequence is a single document.
All inputs are finite; a program needn't handle non-finite values.
Results may differ from the reference program's by a relative error of at most 0.017.
Values may be sent and summed in bfloat16 or wider, within the bound.
No kernel may reach another device: no remote copies, remote signals or barrier semaphores. Data moves between devices by JAX's collectives and lax.ppermute only.
A program may use at most 448 MiB of HBM per device.

```python
import math
import jax
import jax.numpy as jnp
from jax import lax

D = 1536
FR = 2048
FF = 4608
H = 16
CONV = 4
MB = 2
BLK = 128
LEN = 1024
SEQS = 4


def draw_segment_ids(key, part):
    key = jax.random.fold_in(key, 11)
    split_keys = jax.random.split(key, 2)
    total_seqs = MB * SEQS

    def one_sequence(seq_key):
        places = jax.random.permutation(seq_key, LEN - 1)[:3] + 1
        flags = jnp.zeros((LEN,), jnp.int32).at[places].set(1)
        return jnp.cumsum(flags).astype(jnp.int32)
    seq_keys = jax.random.split(split_keys[0], total_seqs)
    numbers = jax.vmap(one_sequence)(seq_keys).reshape(MB, SEQS, LEN)
    chosen = jax.random.randint(split_keys[1], (SEQS,), 0, MB)
    whole = (jnp.arange(MB)[:, None] == chosen[None, :])[..., None]
    return jnp.where(whole, 0, numbers).astype(jnp.int32)


def draw_decay(key, part):
    key = jax.random.fold_in(key, 12)
    lowest = math.log(0.1 / LEN)
    highest = math.log(1.0 / 64.0)
    spread = jax.random.uniform(key, (2, FR), jnp.float32, lowest, highest)
    rates = jnp.exp(spread)
    return jnp.log(jnp.expm1(rates)).astype(jnp.bfloat16)


def levels(key, extent, shards, smallest, largest):
    def one(dim, blocks):
        heights = jax.random.uniform(jax.random.fold_in(jax.random.fold_in(key, 6), dim), (blocks,), jnp.float32, smallest / len(shards), largest / len(shards))
        return jnp.repeat(jnp.exp(heights), extent[dim] // blocks).reshape((-1,) + (1,) * (len(extent) - dim - 1))

    loudness = one(*shards[0])
    for cut in shards[1:]:
        loudness = loudness * one(*cut)
    return loudness


def centred(rng, shape, deviation, most, cuts=(), kind=jnp.bfloat16):
    level = levels(rng, shape, cuts, -0.22, 0.18) if cuts else 1.0
    entries = jax.random.normal(rng, shape, jnp.float32) * deviation * level
    return jnp.minimum(jnp.maximum(entries, -most), most).astype(kind)


def setup_inputs(seed: int = 0) -> dict:
    key_of = jax.random.split(jax.random.key(seed), 18)
    return {
        "ends": centred(key_of[0], (2, MB, SEQS, LEN, D), 1.0, 6.0, ((0, 2), (2, 4), (3, 4))),
        "segment_ids": draw_segment_ids(jax.random.fold_in(key_of[17], 71), 0),
        "norm_one": jnp.clip(1.0 + 0.18 * jax.random.normal(key_of[2], (2, D), jnp.float32), 0.099609375, 1.8984375).astype(jnp.bfloat16),
        "w_branch": centred(key_of[3], (2, D, FR), D ** -0.5, 0.15625, ((0, 2), (1, 16))),
        "w_input": centred(key_of[4], (2, D, FR), D ** -0.5, 0.15625, ((0, 2), (1, 16))),
        "conv_weight": centred(key_of[5], (2, CONV, FR), 0.5, 3.0, ((0, 2), (2, 16))),
        "conv_bias": centred(key_of[6], (2, FR), 0.5, 3.0, ((0, 2), (1, 16))),
        "gate_a": centred(key_of[7], (2, H, BLK, BLK), BLK ** -0.5, 0.5, ((0, 2), (2, 16))),
        "gate_i": centred(key_of[8], (2, H, BLK, BLK), BLK ** -0.5, 0.5, ((0, 2), (2, 16))),
        "bias_a": centred(key_of[9], (2, FR), 1.0, 4.0, ((0, 2), (1, 16))),
        "bias_i": centred(key_of[10], (2, FR), 1.0, 4.0, ((0, 2), (1, 16))),
        "decay": draw_decay(jax.random.fold_in(key_of[17], 71), 0),
        "w_out": centred(key_of[12], (2, FR, D), (FR // 8) ** -0.5, 0.375, ((0, 2), (1, 16))),
        "norm_two": jnp.clip(1.0 + 0.18 * jax.random.normal(key_of[13], (2, D), jnp.float32), 0.099609375, 1.8984375).astype(jnp.bfloat16),
        "w_gate": centred(key_of[14], (2, D, FF), D ** -0.5, 0.15625, ((0, 2), (1, 16))),
        "w_up": centred(key_of[15], (2, D, FF), D ** -0.5, 0.15625, ((0, 2), (1, 16))),
        "w_down": centred(key_of[16], (2, FF, D), (FF // 3) ** -0.5, 0.15625, ((0, 2), (1, 16))),
    }


@jax.custom_vjp
def low(v):
    return lax.optimization_barrier(v.astype(jnp.bfloat16)).astype(jnp.float32)

@jax.custom_vjp
def low_back(v):
    return v

def low_keep(v):
    return (low(v), None)

def low_pass(kept, grad):
    return (grad,)

def back_keep(v):
    return (v, None)

def back_low(kept, grad):
    return (low(grad),)
low.defvjp(low_keep, low_pass)
low_back.defvjp(back_keep, back_low)

def rms_norm(values, gain):
    return values * lax.rsqrt(lax.optimization_barrier(jnp.mean(values * values, axis=-1, keepdims=True)) + 1e-06) * gain

def project(left, right):
    return jnp.einsum('bld,df->blf', left, right, precision=lax.Precision.HIGHEST)

def combine(earlier, later):
    return (earlier[0] * later[0], later[0] * earlier[1] + later[1])

def gate_terms(first_pre, second_pre, conv_value, rate_bias, input_bias, decay_value, starts):
    rate_gate = jax.nn.sigmoid(first_pre + rate_bias)
    input_gate = jax.nn.sigmoid(second_pre + input_bias)
    log_keep = -8.0 * rate_gate * jax.nn.softplus(decay_value)
    keeping = jnp.where(starts, 0.0, jnp.exp(log_keep))
    scaling = jnp.sqrt(1.0 + 0.0001 - keeping * keeping)
    return (keeping, input_gate * conv_value * scaling)

def block(inputs, weights, seg_ids):
    norm_one, w_branch, w_input, conv_weight, conv_bias, gate_a, gate_i, bias_a, bias_i, decay, w_out, norm_two, w_gate, w_up, w_down = weights
    seq_len = inputs.shape[1]
    head_count = gate_a.shape[0]
    block_size = gate_a.shape[1]
    padded_ids = jnp.pad(seg_ids, ((0, 0), (CONV - 1, 0)), constant_values=-1)
    starts = (padded_ids[:, CONV - 2:CONV - 2 + seq_len] != seg_ids)[..., None]
    normed = low(rms_norm(inputs, norm_one))
    branch = low_back(project(normed, w_branch))
    conv_in = low(low_back(project(normed, w_input)))
    padded_in = jnp.pad(conv_in, ((0, 0), (CONV - 1, 0), (0, 0)))
    conv_out = conv_bias + conv_weight[0] * conv_in
    for offset in range(1, CONV):
        linked = (padded_ids[:, CONV - 1 - offset:CONV - 1 - offset + seq_len] == seg_ids)[..., None]
        earlier = padded_in[:, CONV - 1 - offset:CONV - 1 - offset + seq_len]
        conv_out = conv_out + conv_weight[offset] * jnp.where(linked, earlier, 0.0)
    rounded = low(conv_out).reshape(conv_out.shape[:2] + (head_count, block_size))
    pre_a = low_back(jnp.einsum('blhi,hij->blhj', rounded, gate_a, precision=lax.Precision.HIGHEST)).reshape(conv_out.shape)
    pre_i = low_back(jnp.einsum('blhi,hij->blhj', rounded, gate_i, precision=lax.Precision.HIGHEST)).reshape(conv_out.shape)
    keeping, driven = gate_terms(pre_a, pre_i, conv_out, bias_a, bias_i, decay, starts)
    hidden = lax.associative_scan(combine, (keeping, driven), axis=1)[1]
    mixed = low(hidden * jax.nn.gelu(branch))
    middle = inputs + low_back(project(mixed, w_out))
    normed_two = low(rms_norm(middle, norm_two))
    gate_pre = low_back(project(normed_two, w_gate))
    up_pre = low_back(project(normed_two, w_up))
    product = low(jax.nn.gelu(gate_pre) * up_pre)
    return middle + low_back(project(product, w_down))

def reference(ends, segment_ids, norm_one, w_branch, w_input, conv_weight, conv_bias, gate_a, gate_i, bias_a, bias_i, decay, w_out, norm_two, w_gate, w_up, w_down):
    stacked = tuple((weight.astype(jnp.float32) for weight in (norm_one, w_branch, w_input, conv_weight, conv_bias, gate_a, gate_i, bias_a, bias_i, decay, w_out, norm_two, w_gate, w_up, w_down)))
    first_section = tuple((weight[0] for weight in stacked))
    second_section = tuple((weight[1] for weight in stacked))

    def micro_step(totals, step_items):
        inputs, cotangent, seg_ids = step_items

        def forward(start_in, offset, first_w, second_w):
            out_first = block(start_in, first_w, seg_ids)
            passed = low_back(low(out_first)) + offset
            return (block(passed, second_w, seg_ids), out_first)
        start_value = inputs.astype(jnp.float32)
        out_second, pullback, out_first = jax.vjp(forward, start_value, jnp.zeros(start_value.shape, jnp.float32), first_section, second_section, has_aux=True)
        grad_in, grad_mid, grad_first, grad_second = pullback(cotangent.astype(jnp.float32))
        totals = jax.tree.map(lambda total, extra: total + extra, totals, (grad_first, grad_second))
        return (totals, (out_first.astype(jnp.bfloat16), out_second.astype(jnp.bfloat16), grad_in.astype(jnp.bfloat16), grad_mid.astype(jnp.bfloat16)))
    initial = jax.tree.map(jnp.zeros_like, (first_section, second_section))
    totals, results = lax.scan(micro_step, initial, (ends[0], ends[1], segment_ids))
    section_outputs = jnp.stack([results[0], results[1]])
    input_grads = jnp.stack([results[2], results[3]])
    weight_grads = [jnp.stack([section_zero, section_one]) for section_zero, section_one in zip(totals[0], totals[1])]
    return (section_outputs, input_grads, weight_grads[0], weight_grads[1], weight_grads[2], weight_grads[3], weight_grads[4], weight_grads[5], weight_grads[6], weight_grads[7], weight_grads[8], weight_grads[9], weight_grads[10], weight_grads[11], weight_grads[12], weight_grads[13], weight_grads[14])
```

```python
import functools

import jax
import jax.numpy as jnp
from jax import lax
from jax.experimental import pallas as pl
from jax.experimental.pallas import tpu as pltpu
from jax.sharding import PartitionSpec as P

CONV = 4
EPS = 1e-06
F32 = jnp.float32
BF16 = jnp.bfloat16
VMEM_BYTES = 56 << 20
LANES = 128
SUB = 8


def nn_dot(a, b):
    return lax.dot_general(a, b, (((1,), (0,)), ((), ())), preferred_element_type=F32)


def nt_dot(a, b):
    return lax.dot_general(a, b, (((1,), (1,)), ((), ())), preferred_element_type=F32)


def tn_dot(a, b):
    return lax.dot_general(a, b, (((0,), (0,)), ((), ())), preferred_element_type=F32)


def sigmoid(v):
    return 0.5 * jnp.tanh(0.5 * v) + 0.5


K0 = 0.7978845608028654
K1 = 0.044715


def gelu(v):
    return 0.5 * v * (1.0 + jnp.tanh(K0 * (v + K1 * v * v * v)))


def gelu_both(v):
    square = v * v
    t = jnp.tanh(K0 * v * (1.0 + K1 * square))
    half = 0.5 * (1.0 + t)
    slope = half + (0.5 * K0) * v * (1.0 - t * t) * (1.0 + (3.0 * K1) * square)
    return v * half, slope


def lanes(mask, width):
    return jnp.concatenate([mask] * (width // LANES), axis=1) if width > LANES else mask


def call(kernel, grid, in_specs, out_specs, out_shape, scratch, flops, bytes_accessed, args):
    return pl.pallas_call(
        kernel,
        grid=grid,
        in_specs=in_specs,
        out_specs=out_specs,
        out_shape=out_shape,
        scratch_shapes=scratch,
        compiler_params=pltpu.CompilerParams(
            dimension_semantics=("arbitrary",) * len(grid), vmem_limit_bytes=VMEM_BYTES
        ),
        cost_estimate=pl.CostEstimate(
            flops=int(flops), bytes_accessed=int(bytes_accessed), transcendentals=0
        ),
    )(*args)


def whole(shape):
    return pl.BlockSpec(shape, lambda c: (0,) * len(shape))


def columns(rows, width, offset=0):
    return pl.BlockSpec((rows, width), lambda c: (0, c + offset))


def struct(shape, dtype):
    return jax.ShapeDtypeStruct(shape, dtype)


def recur_in_kernel(
    groups, length,
    x_ref, halo_ref, gain_ref, wb_ref, wi_ref, ga_ref, gi_ref, vec_ref, mask_ref,
    normed_ref, branch_ref, ext_ref, rate_ref, igate_ref, keep_ref, local_ref, segp_ref, agg_ref,
    xn, conv, pre_a, pre_i,
):
    rows = groups * length
    steps = length // SUB
    width = wb_ref.shape[1]

    @pl.when(pl.program_id(0) == 0)
    def _():
        gain = gain_ref[...]
        for at, ref in ((0, x_ref), (rows, halo_ref)):
            v = ref[...].astype(F32)
            r = lax.rsqrt(jnp.mean(v * v, axis=-1, keepdims=True) + EPS)
            xn[at : at + ref.shape[0], :] = (v * r * gain).astype(BF16)
        normed_ref[...] = xn[0:rows, :]

    branch_ref[...] = nn_dot(xn[0:rows, :], wb_ref[...])
    conv_in = nn_dot(xn[...], wi_ref[...]).astype(BF16).astype(F32)
    sub = lax.broadcasted_iota(jnp.int32, (SUB, width), 0)
    for g in range(groups):
        base = conv_in[g * length : (g + 1) * length]
        halo = conv_in[rows + g * SUB : rows + (g + 1) * SUB]
        for k in (3, 2, 1):
            block = pltpu.roll(base[(steps - k) * SUB : (steps - k + 1) * SUB], 1, 0)
            ext_ref[g, (3 - k) * SUB : (4 - k) * SUB, :] = jnp.where(sub == 0, halo[3 - k : 4 - k], block)
        ext_ref[g, 3 * SUB : 3 * SUB + length, :] = base
    taps = [vec_ref[k : k + 1, :] for k in range(CONV)]
    for g in range(groups):
        part = slice(g * length, (g + 1) * length)
        out = vec_ref[4:5, :] + taps[0] * ext_ref[g, 3 * SUB : 3 * SUB + length, :]
        for k in range(1, CONV):
            link = lanes(mask_ref[k, part, :], width)
            out = out + taps[k] * (link * ext_ref[g, (3 - k) * SUB : (3 - k) * SUB + length, :])
        conv[part, :] = out
    rounded = conv[...].astype(BF16)
    for h in range(width // LANES):
        col = slice(h * LANES, (h + 1) * LANES)
        pre_a[:, col] = nn_dot(rounded[:, col], ga_ref[h])
        pre_i[:, col] = nn_dot(rounded[:, col], gi_ref[h])
    bias_a, bias_i, scale = vec_ref[5:6, :], vec_ref[6:7, :], vec_ref[7:8, :]
    chunk = 4

    def step(i, carry):
        out = []
        for g in range(groups):
            h, p = carry[g]
            at = pl.multiple_of(g * length + i * (chunk * SUB), chunk * SUB)
            here = pl.ds(at, chunk * SUB)
            rate = sigmoid(pre_a[here, :] + bias_a)
            igate = sigmoid(pre_i[here, :] + bias_i)
            keep = jnp.exp(scale * rate) * lanes(mask_ref[0, here, :], width)
            driven = igate * conv[here, :] * jnp.sqrt(1.0 + 0.0001 - keep * keep)
            rate_ref[here, :] = rate
            igate_ref[here, :] = igate
            keep_ref[here, :] = keep
            states = []
            for q in range(chunk):
                kq = keep[q * SUB : (q + 1) * SUB]
                h = kq * h + driven[q * SUB : (q + 1) * SUB]
                p = kq * p
                states.append(h)
            local_ref[here, :] = jnp.concatenate(states, axis=0)
            out.append((h, p))
        return tuple(out)

    start = tuple((jnp.zeros((SUB, width), F32), jnp.ones((SUB, width), F32)) for _ in range(groups))
    done = lax.fori_loop(0, steps // chunk, step, start)
    for g in range(groups):
        h, p = done[g]
        segp_ref[g * SUB : (g + 1) * SUB, :] = p
        a, b = jnp.ones((1, width), F32), jnp.zeros((1, width), F32)
        for s in range(SUB):
            b = p[s : s + 1] * b + h[s : s + 1]
            a = p[s : s + 1] * a
        agg_ref[2 * g : 2 * g + 1, :] = a
        agg_ref[2 * g + 1 : 2 * g + 2, :] = b


def recur_in(x, halo, gain, w_in, gate_a, gate_i, vec, masks, groups, length):
    rows, dim = x.shape
    recur = w_in.shape[1] // 2
    width = 256
    blocks = recur // width
    block_f32 = columns(rows, width)
    heads = width // LANES
    ext_len = length + 3 * SUB
    return call(
        functools.partial(recur_in_kernel, groups, length),
        (blocks,),
        [
            whole(x.shape), whole(halo.shape), whole(gain.shape),
            columns(dim, width), columns(dim, width, blocks),
            pl.BlockSpec((heads, LANES, LANES), lambda c: (c, 0, 0)),
            pl.BlockSpec((heads, LANES, LANES), lambda c: (c, 0, 0)),
            columns(8, width), whole(masks.shape),
        ],
        [
            whole((rows, dim)), block_f32,
            pl.BlockSpec((groups, ext_len, width), lambda c: (0, 0, c)),
            block_f32, block_f32, block_f32, block_f32,
            columns(SUB * groups, width), columns(2 * groups, width),
        ],
        [
            struct((rows, dim), BF16), struct((rows, recur), F32), struct((groups, ext_len, recur), F32),
            struct((rows, recur), F32), struct((rows, recur), F32), struct((rows, recur), F32),
            struct((rows, recur), F32), struct((SUB * groups, recur), F32), struct((2 * groups, recur), F32),
        ],
        [
            pltpu.VMEM((rows + SUB * groups, dim), BF16), pltpu.VMEM((rows, width), F32),
            pltpu.VMEM((rows, width), F32), pltpu.VMEM((rows, width), F32),
        ],
        4 * rows * dim * recur * 1.5,
        dim * recur * 4 + rows * recur * 4 * 6,
        (x, halo, gain, w_in, w_in, gate_a, gate_i, vec, masks),
    )


def recur_out_kernel(
    groups, length,
    x_ref, keep_ref, local_ref, branch_ref, segp_ref, hin_ref, wo_ref, gain_ref,
    hidden_ref, mixed_ref, middle_ref, normed_ref,
    acc,
):
    steps = length // SUB
    width = keep_ref.shape[1]
    chunk = 4
    c = pl.program_id(0)
    start = []
    for g in range(groups):
        ends = local_ref[(g + 1) * length - SUB : (g + 1) * length, :]
        prods = segp_ref[g * SUB : (g + 1) * SUB, :]
        state = hin_ref[g : g + 1, :]
        entering = []
        for s in range(SUB):
            entering.append(state)
            state = prods[s : s + 1] * state + ends[s : s + 1]
        start.append(jnp.concatenate(entering, axis=0))

    def step(i, carry):
        out = []
        for g in range(groups):
            q = carry[g]
            at = pl.multiple_of(g * length + i * (chunk * SUB), chunk * SUB)
            here = pl.ds(at, chunk * SUB)
            keep = keep_ref[here, :]
            moved = []
            for r in range(chunk):
                q = keep[r * SUB : (r + 1) * SUB] * q
                moved.append(q)
            hidden = local_ref[here, :] + jnp.concatenate(moved, axis=0)
            hidden_ref[here, :] = hidden
            mixed_ref[here, :] = (hidden * gelu(branch_ref[here, :])).astype(BF16)
            out.append(q)
        return tuple(out)

    lax.fori_loop(0, steps // chunk, step, tuple(start))
    part = nn_dot(mixed_ref[...], wo_ref[...])

    @pl.when(c == 0)
    def _():
        acc[...] = x_ref[...].astype(F32) + part

    @pl.when(c > 0)
    def _():
        acc[...] += part

    @pl.when(c == pl.num_programs(0) - 1)
    def _():
        m = acc[...]
        middle_ref[...] = m
        r = lax.rsqrt(jnp.mean(m * m, axis=-1, keepdims=True) + EPS)
        normed_ref[...] = (m * r * gain_ref[...]).astype(BF16)


def recur_out(x, keep, local, branch, segp, hin, w_out, gain, groups, length):
    rows, dim = x.shape
    recur = keep.shape[1]
    width = 256
    block = columns(rows, width)
    return call(
        functools.partial(recur_out_kernel, groups, length),
        (recur // width,),
        [
            whole(x.shape), block, block, block, columns(SUB * groups, width), columns(groups, width),
            pl.BlockSpec((width, dim), lambda c: (c, 0)), whole(gain.shape),
        ],
        [block, block, whole((rows, dim)), whole((rows, dim))],
        [
            struct((rows, recur), F32), struct((rows, recur), BF16),
            struct((rows, dim), F32), struct((rows, dim), BF16),
        ],
        [pltpu.VMEM((rows, dim), F32)],
        2 * rows * dim * recur * 1.5,
        dim * recur * 2 + rows * recur * 18,
        (x, keep, local, branch, segp, hin, w_out, gain),
    )


def ff_kernel(x_ref, mid_ref, wg_ref, wu_ref, wd_ref, gate_ref, up_ref, product_ref, out_ref, acc):
    c = pl.program_id(0)
    x = x_ref[...]
    gate = nn_dot(x, wg_ref[...])
    up = nn_dot(x, wu_ref[...])
    gate_ref[...] = gate.astype(BF16)
    up_ref[...] = up.astype(BF16)
    product = (gelu(gate) * up).astype(BF16)
    product_ref[...] = product
    part = nn_dot(product, wd_ref[...])

    @pl.when(c == 0)
    def _():
        acc[...] = mid_ref[...] + part

    @pl.when(c > 0)
    def _():
        acc[...] += part

    @pl.when(c == pl.num_programs(0) - 1)
    def _():
        out_ref[...] = acc[...].astype(BF16)


def feed_forward(x, middle, w_gu, w_down):
    rows, dim = x.shape
    hidden = w_down.shape[0]
    width = 512
    blocks = hidden // width
    block = columns(rows, width)
    return call(
        ff_kernel,
        (blocks,),
        [
            whole(x.shape), whole(middle.shape), columns(dim, width), columns(dim, width, blocks),
            pl.BlockSpec((width, dim), lambda c: (c, 0)),
        ],
        [block, block, block, whole((rows, dim))],
        [struct((rows, hidden), BF16)] * 3 + [struct((rows, dim), BF16)],
        [pltpu.VMEM((rows, dim), F32)],
        6 * rows * dim * hidden,
        6 * dim * hidden,
        (x, middle, w_gu, w_gu, w_down),
    )


def norm_back(values, gain, grad):
    q = lax.rsqrt(jnp.mean(values * values, axis=-1, keepdims=True) + EPS)
    t = gain * grad
    back = q * t - values * (q * q * q * jnp.mean(values * t, axis=-1, keepdims=True))
    return back, jnp.sum(values * q * grad, axis=0, keepdims=True)


def ff_back_kernel(
    dout_ref, mid_ref, gain_ref, gate_ref, up_ref, wg_ref, wu_ref, wd_ref,
    dgate_ref, dup_ref, dmid_ref, low_ref, dgain_ref,
    acc,
):
    c = pl.program_id(0)
    dproduct = nt_dot(dout_ref[...], wd_ref[...])
    act, slope = gelu_both(gate_ref[...].astype(F32))
    dgate = (dproduct * up_ref[...].astype(F32) * slope).astype(BF16)
    dup = (dproduct * act).astype(BF16)
    dgate_ref[...] = dgate
    dup_ref[...] = dup
    part = nt_dot(dgate, wg_ref[...]) + nt_dot(dup, wu_ref[...])

    @pl.when(c == 0)
    def _():
        acc[...] = part

    @pl.when(c > 0)
    def _():
        acc[...] += part

    @pl.when(c == pl.num_programs(0) - 1)
    def _():
        back, dgain = norm_back(mid_ref[...], gain_ref[...], acc[...])
        dmid = dout_ref[...].astype(F32) + back
        dmid_ref[...] = dmid
        low_ref[...] = dmid.astype(BF16)
        dgain_ref[...] = dgain


def feed_forward_back(dout, middle, gain, gate, up, w_gu, w_down):
    rows, dim = dout.shape
    hidden = w_down.shape[0]
    width = 512
    blocks = hidden // width
    block = columns(rows, width)
    full = whole((rows, dim))
    return call(
        ff_back_kernel,
        (blocks,),
        [
            full, full, whole(gain.shape), block, block, columns(dim, width), columns(dim, width, blocks),
            pl.BlockSpec((width, dim), lambda c: (c, 0)),
        ],
        [block, block, full, full, whole((1, dim))],
        [
            struct((rows, hidden), BF16), struct((rows, hidden), BF16), struct((rows, dim), F32),
            struct((rows, dim), BF16), struct((1, dim), F32),
        ],
        [pltpu.VMEM((rows, dim), F32)],
        6 * rows * dim * hidden * 1.2,
        6 * dim * hidden,
        (dout, middle, gain, gate, up, w_gu, w_gu, w_down),
    )


def mix_back_kernel(
    groups, length,
    low_ref, wo_ref, branch_ref, hidden_ref, keep_ref,
    dbranch_ref, local_ref, sege_ref, segf_ref, agg_ref,
    dmixed,
):
    steps = length // SUB
    width = keep_ref.shape[1]
    chunk = 4
    dmixed[...] = nt_dot(low_ref[...], wo_ref[...])

    def step(i, carry):
        out = []
        for g in range(groups):
            s, p, after = carry[g]
            at = pl.multiple_of(g * length + (steps // chunk - 1 - i) * (chunk * SUB), chunk * SUB)
            here = pl.ds(at, chunk * SUB)
            act, slope = gelu_both(branch_ref[here, :])
            d = dmixed[here, :]
            dbranch_ref[here, :] = (d * hidden_ref[here, :] * slope).astype(BF16)
            dhidden = d * act
            keep = keep_ref[here, :]
            states = [None] * chunk
            for r in reversed(range(chunk)):
                s = dhidden[r * SUB : (r + 1) * SUB] + after * s
                p = after * p
                after = keep[r * SUB : (r + 1) * SUB]
                states[r] = s
            local_ref[here, :] = jnp.concatenate(states, axis=0)
            out.append((s, p, after))
        return tuple(out)

    one = jnp.ones((SUB, width), F32)
    start = tuple((jnp.zeros((SUB, width), F32), one, one) for _ in range(groups))
    done = lax.fori_loop(0, steps // chunk, step, start)
    for g in range(groups):
        s, p, after = done[g]
        e, f = after * s, after * p
        sege_ref[g * SUB : (g + 1) * SUB, :] = e
        segf_ref[g * SUB : (g + 1) * SUB, :] = f
        a, b = jnp.ones((1, width), F32), jnp.zeros((1, width), F32)
        for r in reversed(range(SUB)):
            b = e[r : r + 1] + f[r : r + 1] * b
            a = f[r : r + 1] * a
        agg_ref[2 * g : 2 * g + 1, :] = a
        agg_ref[2 * g + 1 : 2 * g + 2, :] = b


def mix_back(low, w_out, branch, hidden, keep, groups, length):
    rows, dim = low.shape
    recur = keep.shape[1]
    width = 256
    block = columns(rows, width)
    return call(
        functools.partial(mix_back_kernel, groups, length),
        (recur // width,),
        [whole(low.shape), pl.BlockSpec((width, dim), lambda c: (c, 0)), block, block, block],
        [block, block, columns(SUB * groups, width), columns(SUB * groups, width), columns(2 * groups, width)],
        [
            struct((rows, recur), BF16), struct((rows, recur), F32), struct((SUB * groups, recur), F32),
            struct((SUB * groups, recur), F32), struct((2 * groups, recur), F32),
        ],
        [pltpu.VMEM((rows, width), F32)],
        2 * rows * dim * recur * 2,
        dim * recur * 2 + rows * recur * 18,
        (low, w_out, branch, hidden, keep),
    )


def gates_back_kernel(
    groups, length,
    local_ref, keep_ref, hidden_ref, ext_ref, rate_ref, igate_ref, sege_ref, segf_ref, gin_ref, hin_ref,
    ga_ref, gi_ref, vec_ref, mask_ref,
    din_ref, head_ref, dga_ref, dgi_ref, dvec_ref,
    dconv, low_a, low_i, rounded,
):
    steps = length // SUB
    width = keep_ref.shape[1]
    chunk = 4
    sub = lax.broadcasted_iota(jnp.int32, (SUB, width), 0)
    taps = [vec_ref[k : k + 1, :] for k in range(CONV)]
    conv_bias, scale = vec_ref[4:5, :], vec_ref[7:8, :]
    start = []
    for g in range(groups):
        e = sege_ref[g * SUB : (g + 1) * SUB, :]
        f = segf_ref[g * SUB : (g + 1) * SUB, :]
        y = gin_ref[g : g + 1, :]
        entering = [None] * SUB
        for s in reversed(range(SUB)):
            entering[s] = y
            y = e[s : s + 1] + f[s : s + 1] * y
        start.append((jnp.concatenate(entering, axis=0), jnp.ones((SUB, width), F32)))
    zero = jnp.zeros((SUB, width), F32)

    def fold(v):
        return functools.reduce(jnp.add, [v[q * SUB : (q + 1) * SUB] for q in range(v.shape[0] // SUB)])

    def step(i, carry):
        chains, sum_a, sum_i, sum_d = carry
        out = []
        j = steps // chunk - 1 - i
        for g in range(groups):
            r, after = chains[g]
            at = pl.multiple_of(g * length + j * (chunk * SUB), chunk * SUB)
            here = pl.ds(at, chunk * SUB)
            keep = keep_ref[here, :]
            parts = [None] * chunk
            for q in reversed(range(chunk)):
                r = after * r
                after = keep[q * SUB : (q + 1) * SUB]
                parts[q] = r
            state = local_ref[here, :] + jnp.concatenate(parts, axis=0)
            last = hidden_ref[(g + 1) * length - SUB : (g + 1) * length, :]
            wrapped = jnp.where(sub == 0, hin_ref[g : g + 1, :], pltpu.roll(last, 1, 0))
            before = pl.multiple_of(jnp.maximum(at - SUB, g * length), SUB)
            first = jnp.where(j == 0, wrapped, hidden_ref[pl.ds(before, SUB), :])
            rest = hidden_ref[pl.ds(at, (chunk - 1) * SUB), :]
            previous = jnp.concatenate([first, rest], axis=0)
            inner = pl.multiple_of(j * (chunk * SUB), chunk * SUB)
            conv = conv_bias + taps[0] * ext_ref[g, pl.ds(inner + 3 * SUB, chunk * SUB), :]
            for k in range(1, CONV):
                link = lanes(mask_ref[k, here, :], width)
                conv = conv + taps[k] * (link * ext_ref[g, pl.ds(inner + (3 - k) * SUB, chunk * SUB), :])
            rate, igate = rate_ref[here, :], igate_ref[here, :]
            space = 1.0 + 0.0001 - keep * keep
            inverse = lax.rsqrt(space)
            scaling = space * inverse
            both = state * igate
            dconv[here, :] = both * scaling
            with_conv = both * conv
            dlog = (state * previous - with_conv * (keep * inverse)) * keep
            dpre_a = (dlog * scale) * (rate * (1.0 - rate))
            dpre_i = (with_conv * scaling) * (1.0 - igate)
            low_a[here, :] = dpre_a.astype(BF16)
            low_i[here, :] = dpre_i.astype(BF16)
            rounded[here, :] = conv.astype(BF16)
            sum_a = sum_a + fold(dpre_a)
            sum_i = sum_i + fold(dpre_i)
            sum_d = sum_d + fold(dlog * rate)
            out.append((r, after))
        return tuple(out), sum_a, sum_i, sum_d

    _, sum_a, sum_i, sum_d = lax.fori_loop(0, steps // chunk, step, (tuple(start), zero, zero, zero))
    dvec_ref[5:6, :] = jnp.sum(sum_a, axis=0, keepdims=True)
    dvec_ref[6:7, :] = jnp.sum(sum_i, axis=0, keepdims=True)
    dvec_ref[7:8, :] = jnp.sum(sum_d, axis=0, keepdims=True)
    for h in range(width // LANES):
        col = slice(h * LANES, (h + 1) * LANES)
        dga_ref[h] = tn_dot(rounded[:, col], low_a[:, col])
        dgi_ref[h] = tn_dot(rounded[:, col], low_i[:, col])
        dconv[:, col] += nt_dot(low_a[:, col], ga_ref[h]) + nt_dot(low_i[:, col], gi_ref[h])

    sums = [zero] * (CONV + 1)
    for g in range(groups):

        def conv_step(i, carry, g=g):
            carry = list(carry)
            inner = pl.multiple_of(i * (chunk * SUB), chunk * SUB)
            here = pl.ds(pl.multiple_of(g * length + inner, chunk * SUB), chunk * SUB)
            d = dconv[here, :]
            carry[4] = carry[4] + fold(d)
            for k in range(CONV):
                masked = d if k == 0 else d * lanes(mask_ref[k, here, :], width)
                carry[k] = carry[k] + fold(masked * ext_ref[g, pl.ds(inner + (3 - k) * SUB, chunk * SUB), :])
            return tuple(carry)

        sums = list(lax.fori_loop(0, steps // chunk, conv_step, tuple(sums)))
        base = g * length
        tail = length - 3 * SUB
        total = taps[0] * dconv[base : base + tail, :]
        for k in range(1, CONV):
            there = slice(base + k * SUB, base + k * SUB + tail)
            total = total + taps[k] * (dconv[there, :] * lanes(mask_ref[k, there, :], width))
        din_ref[base : base + tail, :] = total

        def term(k, block):
            there = slice(base + block * SUB, base + (block + 1) * SUB)
            v = taps[k] * dconv[there, :]
            return v if k == 0 else v * lanes(mask_ref[k, there, :], width)

        heads = []
        for i in (3, 2, 1):
            j = steps - i
            value = term(0, j)
            head = None
            for k in range(1, CONV):
                if j + k < steps:
                    value = value + term(k, j + k)
                else:
                    t = term(k, j + k - steps)
                    value = value + jnp.where(sub == SUB - 1, 0.0, pltpu.roll(t, SUB - 1, 0))
                    head = t if head is None else head + t
            din_ref[base + j * SUB : base + (j + 1) * SUB, :] = value
            heads.append(head[0:1])
        head_ref[g * SUB : (g + 1) * SUB, :] = jnp.concatenate(heads + [jnp.zeros((SUB - 3, width), F32)], axis=0)
    for k in range(CONV + 1):
        dvec_ref[k : k + 1, :] = jnp.sum(sums[k], axis=0, keepdims=True)


def gates_back(local, keep, hidden, ext, rate, igate, sege, segf, gin, hin, gate_a, gate_i, vec, masks, groups, length):
    rows, recur = local.shape
    width = 256
    heads = width // LANES
    block = columns(rows, width)
    seg = columns(SUB * groups, width)
    gate = pl.BlockSpec((heads, LANES, LANES), lambda c: (c, 0, 0))
    return call(
        functools.partial(gates_back_kernel, groups, length),
        (recur // width,),
        [
            block, block, block, pl.BlockSpec((groups, length + 3 * SUB, width), lambda c: (0, 0, c)),
            block, block, seg, seg, columns(groups, width), columns(groups, width),
            gate, gate, columns(8, width), whole(masks.shape),
        ],
        [block, seg, gate, gate, columns(8, width)],
        [
            struct((rows, recur), F32), struct((SUB * groups, recur), F32), struct(gate_a.shape, F32),
            struct(gate_a.shape, F32), struct((8, recur), F32),
        ],
        [
            pltpu.VMEM((rows, width), F32), pltpu.VMEM((rows, width), BF16),
            pltpu.VMEM((rows, width), BF16), pltpu.VMEM((rows, width), BF16),
        ],
        rows * recur * 128 * 8 * 4,
        rows * recur * 28,
        (local, keep, hidden, ext, rate, igate, sege, segf, gin, hin, gate_a, gate_i, vec, masks),
    )


def recur_in_back_kernel(
    groups, length,
    dbranch_ref, din_ref, back_ref, wb_ref, wi_ref, x_ref, gain_ref, dmid_ref,
    low_ref, dx_ref, dgain_ref,
    acc,
):
    c = pl.program_id(0)
    width = din_ref.shape[1]
    rim = 4 * SUB
    sub = lax.broadcasted_iota(jnp.int32, (SUB, width), 0)
    for g in range(groups):
        base = g * length
        if length > rim:
            low_ref[base : base + length - rim, :] = din_ref[base : base + length - rim, :].astype(BF16)
        extra = [jnp.zeros((SUB, width), F32)]
        for i in range(3):
            extra.append(jnp.where(sub == SUB - 1, back_ref[g * SUB + i : g * SUB + i + 1, :], 0.0))
        tail = slice(base + length - rim, base + length)
        low_ref[tail, :] = (din_ref[tail, :] + jnp.concatenate(extra, axis=0)).astype(BF16)
    part = nt_dot(dbranch_ref[...], wb_ref[...]) + nt_dot(low_ref[...], wi_ref[...])

    @pl.when(c == 0)
    def _():
        acc[...] = part

    @pl.when(c > 0)
    def _():
        acc[...] += part

    @pl.when(c == pl.num_programs(0) - 1)
    def _():
        back, dgain = norm_back(x_ref[...].astype(F32), gain_ref[...], acc[...])
        dx_ref[...] = (dmid_ref[...] + back).astype(BF16)
        dgain_ref[...] = dgain


def recur_in_back(dbranch, din, back, w_in, x, gain, dmid, groups, length):
    rows, dim = x.shape
    recur = din.shape[1]
    width = 256
    blocks = recur // width
    block = columns(rows, width)
    full = whole((rows, dim))
    return call(
        functools.partial(recur_in_back_kernel, groups, length),
        (blocks,),
        [
            block, block, columns(SUB * groups, width), columns(dim, width), columns(dim, width, blocks),
            full, whole(gain.shape), full,
        ],
        [block, full, whole((1, dim))],
        [struct((rows, recur), BF16), struct((rows, dim), BF16), struct((1, dim), F32)],
        [pltpu.VMEM((rows, dim), F32)],
        4 * rows * dim * recur,
        4 * dim * recur + rows * recur * 8,
        (dbranch, din, back, w_in, w_in, x, gain, dmid),
    )


def outer_kernel(keep_a, keep_b, send_a, send_b, right_a, right_b, keep_ref, send_ref):
    a, b = right_a[...], right_b[...]
    send_ref[...] = (nn_dot(send_a[...], a) + nn_dot(send_b[...], b)).astype(BF16)
    keep_ref[...] = (nn_dot(keep_a[...], a) + nn_dot(keep_b[...], b)).astype(BF16)


def outer_block(total):
    for width in (768, 512, 384, 256, 128):
        if total % width == 0:
            return width
    return total


def outer(left, right, first, total):
    k, rows = left[0].shape
    width = outer_block(total)
    offset = first // width
    out = columns(k, width)
    return call(
        outer_kernel,
        (total // width,),
        [whole((k, rows))] * 4 + [columns(rows, width, offset)] * 2,
        [out, out],
        [struct((k, total), BF16)] * 2,
        [],
        8 * k * rows * total,
        4 * k * total + 4 * rows * total,
        (*left, *right),
    )


def shifted(value, axis, by):
    length = lax.axis_size(axis)
    pairs = [(i, i + by) for i in range(length) if 0 <= i + by < length]
    return lax.ppermute(value, axis, pairs)


def entering(agg, groups, reverse):
    n = lax.axis_size("seq")
    sign = -1 if reverse else 1
    got = {k: shifted(agg, "seq", sign * k) for k in range(1, n)}
    state = jnp.zeros((groups, agg.shape[1]), F32)
    for k in range(n - 1, 0, -1):
        part = got[k].reshape(groups, 2, -1)
        state = part[:, 0] * state + part[:, 1]
    return state


def add(*parts):
    return functools.reduce(jnp.add, [p.astype(F32) for p in parts])


def line_sum(slots, mine, n, send):
    def at(offset):
        return slots((mine + offset) % n)

    up, down = at(n - 1), at(1)
    for s in range(1, n):
        got_up = send(up, [(i, i + 1) for i in range(s)])
        got_down = send(down, [(i, i - 1) for i in range(n - s, n)])
        if s < n - 1:
            up = add(at(n - 1 - s), got_up).astype(BF16)
            down = add(at(s + 1), got_down).astype(BF16)
    return add(at(0), got_up, got_down)


class Scatter:
    def __init__(self):
        self.n, self.fs = lax.axis_size("seq"), lax.axis_size("fsdp")
        self.ny = self.fs // 2
        self.z, f = lax.axis_index("seq"), lax.axis_index("fsdp")
        self.y, self.core = f // 2, f % 2
        self.swaps = []

    def core_swap(self, value):
        return lax.ppermute(value, "fsdp", [(i, i ^ 1) for i in range(self.fs)])

    def y_send(self, value, pairs):
        return lax.ppermute(value, "fsdp", [(2 * a + c, 2 * b + c) for a, b in pairs for c in range(2)])

    def over_y(self, keep, send):
        if len(self.swaps) >= 2:
            send, _ = lax.optimization_barrier((send, self.swaps[-2]))
        got = self.y_send(send, [(0, 1), (1, 0)])
        self.swaps.append(got)
        return add(keep, got).astype(BF16)

    def over_z(self, shares):
        def slots(d):
            return lax.dynamic_index_in_dim(shares, d, 0, keepdims=False)

        if self.n == 1:
            return shares[0].astype(F32)
        return line_sum(slots, self.z, self.n, lambda v, pairs: lax.ppermute(v, "seq", pairs))

    def finish(self, keep, send):
        return self.over_z(self.over_y(keep, send))


def pick(value, index, axis):
    return lax.dynamic_index_in_dim(value, index, axis, keepdims=False)


def reorder(v):
    length, d = v.shape[-2:]
    return jnp.swapaxes(v.reshape(-1, SUB, length // SUB, d), 1, 2).reshape(-1, d)


def restore(v, shape):
    length, d = shape[-2:]
    return jnp.swapaxes(v.reshape(-1, length // SUB, SUB, d), 1, 2).reshape(shape)


def tail_rows(v, groups, length):
    d = v.shape[1]
    last = v.reshape(groups, length // SUB, SUB, d)[:, length // SUB - 3 :, SUB - 1]
    return jnp.pad(last, ((0, 0), (0, SUB - 3), (0, 0))).reshape(groups * SUB, d)


def gather(shard):
    return lax.all_gather(shard, ("seq", "fsdp"), axis=0, tiled=True)


def body(
    ends, segment_ids, norm_one, w_branch, w_input, conv_weight, conv_bias, gate_a, gate_i, bias_a, bias_i,
    decay, w_out, norm_two, w_gate, w_up, w_down,
):
    is_first = lax.axis_index("section") == 0
    z = lax.axis_index("seq")
    n, fs = lax.axis_size("seq"), lax.axis_size("fsdp")
    places = n * fs
    micro, seqs, length, dim = ends.shape[1:]
    groups = micro * seqs
    rows = groups * length
    recur = w_branch.shape[2]
    heads, part, block = gate_a.shape[1:]
    hidden_dim = w_gate.shape[2]

    small = jnp.concatenate(
        [norm_one[0].reshape(-1), norm_two[0].reshape(-1), conv_weight[0].reshape(-1), conv_bias[0], bias_a[0],
         bias_i[0], decay[0], gate_a[0].reshape(-1), gate_i[0].reshape(-1)]
    )
    count = small.shape[0]
    padded = -(-count // 2048) * 2048
    small = gather(jnp.pad(small, (0, padded - count)).reshape(1, -1, LANES)).reshape(places, padded)
    w_in = gather(jnp.concatenate([w_branch[0], w_input[0]], axis=1))
    w_out_all = gather(w_out[0])
    w_gu = gather(jnp.concatenate([w_gate[0], w_up[0]], axis=1))
    w_down_all = gather(w_down[0])

    dshare, rshare = dim // places, recur // places
    cuts = [dshare, dshare, CONV * rshare, rshare, rshare, rshare, rshare, heads * part * block, heads * part * block]
    pieces, at = [], 0
    for size in cuts:
        pieces.append(small[:, at : at + size])
        at += size
    gain_one = pieces[0].reshape(1, dim).astype(F32)
    gain_two = pieces[1].reshape(1, dim).astype(F32)
    taps = jnp.swapaxes(pieces[2].reshape(places, CONV, rshare), 0, 1).reshape(CONV, recur).astype(F32)
    decays = pieces[6].reshape(1, recur).astype(F32)
    vec = jnp.concatenate(
        [taps] + [p.reshape(1, recur).astype(F32) for p in pieces[3:6]] + [-8.0 * jax.nn.softplus(decays)], axis=0
    )
    gates_a, gates_i = [
        jnp.swapaxes(p.reshape(places, heads, part, block), 0, 1).reshape(heads, block, block) for p in pieces[7:9]
    ]

    padded_ids = jnp.pad(segment_ids, ((0, 0), (0, 0), (CONV - 1, 0)), constant_values=-1)
    window = lax.dynamic_slice_in_dim(padded_ids, z * length, length + CONV - 1, axis=2)
    current = window[:, :, CONV - 1 :]
    masks = jnp.stack(
        [window[:, :, CONV - 1 - k : CONV - 1 - k + length] == current for k in (1, 1, 2, 3)]
    ).astype(F32)
    masks = jnp.swapaxes(masks.reshape(4, groups, SUB, length // SUB), 2, 3).reshape(4, rows, 1)
    masks = jnp.broadcast_to(masks, (4, rows, LANES))

    def forward(x, halo):
        normed, branch, ext, rate, igate, keep, local, segp, agg = recur_in(
            x, halo, gain_one, w_in, gates_a, gates_i, vec, masks, groups, length
        )
        hin = entering(agg, groups, False)
        hidden, mixed, middle, normed_two = recur_out(
            x, keep, local, branch, segp, hin, w_out_all, gain_two, groups, length
        )
        gate, up, product, out = feed_forward(normed_two, middle, w_gu, w_down_all)
        saved = (normed, branch, ext, rate, igate, keep, hin, hidden, mixed, middle, normed_two, gate, up, product)
        return out, saved

    def backward(dout, x, saved):
        normed, branch, ext, rate, igate, keep, hin, hidden, mixed, middle, normed_two, gate, up, product = saved
        dgate, dup, dmid, out_low, dgain_two = feed_forward_back(
            dout, middle, gain_two, gate, up, w_gu, w_down_all
        )
        dbranch, local, sege, segf, agg = mix_back(out_low, w_out_all, branch, hidden, keep, groups, length)
        gin = entering(agg, groups, True)
        din, head, dga, dgi, dvec = gates_back(
            local, keep, hidden, ext, rate, igate, sege, segf, gin, hin, gates_a, gates_i, vec, masks, groups, length
        )
        back = shifted(head, "seq", -1)
        input_low, dx, dgain_one = recur_in_back(dbranch, din, back, w_in, x, gain_one, dmid, groups, length)
        return dx, dgate, dup, out_low, dbranch, input_low, dgain_one, dgain_two, dga, dgi, dvec

    own = reorder(ends[0])
    tails = tail_rows(own, groups, length)
    out, _ = forward(own, shifted(tails, "seq", 1))
    received = shifted(out, "section", 1)
    received_halo = lax.ppermute(
        tail_rows(out, groups, length), ("section", "seq"), [(i, n + i + 1) for i in range(n - 1)]
    )
    x = jnp.where(is_first, own, received)
    halo = jnp.where(is_first, shifted(tails, "seq", 1), received_halo)
    out, saved = forward(x, halo)
    dx = backward(own, x, saved)[0]
    dout = jnp.where(is_first, shifted(dx, "section", -1), own)
    dx, dgate, dup, out_low, dbranch, input_low, dgain_one, dgain_two, dga, dgi, dvec = backward(dout, x, saved)

    outputs = restore(out, ends.shape)
    grads = restore(dx, ends.shape)

    normed, mixed, normed_two, product = saved[0], saved[8], saved[10], saved[13]
    scatter = Scatter()

    def left(v):
        k = v.shape[1]
        t = v.T.reshape(n, scatter.ny, 2, k // places, rows)
        mine, other = pick(t, scatter.core, 2), scatter.core_swap(pick(t, 1 - scatter.core, 2))
        if scatter.ny == 2:
            keep = [pick(w, scatter.y, 1).reshape(-1, rows) for w in (mine, other)]
            send = [pick(w, 1 - scatter.y, 1).reshape(-1, rows) for w in (mine, other)]
            return tuple(keep + send)
        return mine, other

    def right(v):
        return v, scatter.core_swap(v)

    def sum_of(lefts, rights, chunks):
        total = rights[0].shape[1]
        if scatter.ny == 2:
            step = total // chunks
            parts = []
            for i in range(chunks):
                keep, send = outer(lefts, rights, i * step, step)
                parts.append(scatter.finish(keep.reshape(n, -1, step), send.reshape(n, -1, step)))
            return parts[0] if chunks == 1 else jnp.concatenate(parts, axis=1)
        mine, other = lefts
        grad = nn_dot(mine.reshape(-1, rows), rights[0]) + nn_dot(other.reshape(-1, rows), rights[1])
        grad = grad.astype(BF16).reshape(n, scatter.ny, -1, total)
        return sum_rest(grad)

    def sum_rest(grad):
        over_y = line_sum(lambda d: pick(grad, d, 1), scatter.y, scatter.ny, scatter.y_send).astype(BF16)
        return scatter.over_z(over_y)

    normed_t, mixed_t, normed_two_t, product_t = left(normed), left(mixed), left(normed_two), left(product)
    sum_down = sum_of(product_t, right(dout), 2)
    sum_gate = sum_of(normed_two_t, right(dgate), 2)
    sum_up = sum_of(normed_two_t, right(dup), 2)
    sum_out = sum_of(mixed_t, right(out_low), 1)
    sum_branch = sum_of(normed_t, right(dbranch), 1)
    sum_input = sum_of(normed_t, right(input_low), 1)

    ddecay = -8.0 * jax.nn.sigmoid(decays) * dvec[7:8]
    by_place = [
        dgain_one.reshape(places, -1), dgain_two.reshape(places, -1),
        jnp.swapaxes(dvec[:CONV].reshape(CONV, places, rshare), 0, 1).reshape(places, -1),
        dvec[4].reshape(places, -1), dvec[5].reshape(places, -1), dvec[6].reshape(places, -1),
        ddecay.reshape(places, -1),
        jnp.swapaxes(dga.reshape(heads, places, part, block), 0, 1).reshape(places, -1),
        jnp.swapaxes(dgi.reshape(heads, places, part, block), 0, 1).reshape(places, -1),
    ]
    packed = jnp.pad(jnp.concatenate(by_place, axis=1), ((0, 0), (0, padded - count)))
    packed = packed.reshape(n, scatter.ny, 2, -1, LANES)
    theirs = scatter.core_swap(pick(packed, 1 - scatter.core, 2).astype(BF16))
    packed = add(pick(packed, scatter.core, 2), theirs).astype(BF16)
    if scatter.ny == 2:
        small_sum = scatter.finish(pick(packed, scatter.y, 1), pick(packed, 1 - scatter.y, 1))
    else:
        small_sum = sum_rest(packed)
    small_sum = small_sum.reshape(-1)
    sums, at = [], 0
    for size in cuts:
        sums.append(small_sum[at : at + size])
        at += size

    return (
        outputs,
        grads,
        sums[0][None],
        sum_branch[None],
        sum_input[None],
        sums[2].reshape(1, CONV, rshare),
        sums[3][None],
        sums[7].reshape(gate_a.shape),
        sums[8].reshape(gate_a.shape),
        sums[4][None],
        sums[5][None],
        sums[6][None],
        sum_out[None],
        sums[1][None],
        sum_gate[None],
        sum_up[None],
        sum_down[None],
    )


def solution(mesh):
    tokens = P("section", None, "fsdp", "seq", None)
    vector = P("section", ("seq", "fsdp"))
    matrix = P("section", ("seq", "fsdp"), None)
    taps = P("section", None, ("seq", "fsdp"))
    gates = P("section", None, ("seq", "fsdp"), None)
    weights = (
        vector, matrix, matrix, taps, vector, gates, gates, vector, vector, vector, matrix, vector, matrix, matrix, matrix,
    )
    return jax.shard_map(
        body,
        mesh=mesh,
        in_specs=(tokens, P(None, "fsdp", None)) + weights,
        out_specs=(tokens, tokens) + weights,
        check_vma=False,
    )
```

```python
import functools

import jax
import jax.numpy as jnp
from jax import lax
from jax.experimental import pallas as pl
from jax.experimental.pallas import tpu as pltpu
from jax.sharding import PartitionSpec as P

CONV = 4
EPS = 1e-06
F32 = jnp.float32
BF16 = jnp.bfloat16
VMEM_BYTES = 56 << 20
LANES = 128
SUB = 8
COST = 4


def nn_dot(a, b):
    return lax.dot_general(a, b, (((1,), (0,)), ((), ())), preferred_element_type=F32)


def nt_dot(a, b):
    return lax.dot_general(a, b, (((1,), (1,)), ((), ())), preferred_element_type=F32)


def tn_dot(a, b):
    return lax.dot_general(a, b, (((0,), (0,)), ((), ())), preferred_element_type=F32)


def sigmoid(v):
    return 0.5 * jnp.tanh(0.5 * v) + 0.5


K0 = 0.7978845608028654
K1 = 0.044715


def gelu(v):
    return 0.5 * v * (1.0 + jnp.tanh(K0 * (v + K1 * v * v * v)))


def gelu_both(v):
    square = v * v
    t = jnp.tanh(K0 * v * (1.0 + K1 * square))
    half = 0.5 * (1.0 + t)
    slope = half + (0.5 * K0) * v * (1.0 - t * t) * (1.0 + (3.0 * K1) * square)
    return v * half, slope


def lanes(mask, width):
    return jnp.concatenate([mask] * (width // LANES), axis=1) if width > LANES else mask


def call(kernel, grid, in_specs, out_specs, out_shape, scratch, flops, bytes_accessed, args):
    return pl.pallas_call(
        kernel,
        grid=grid,
        in_specs=in_specs,
        out_specs=out_specs,
        out_shape=out_shape,
        scratch_shapes=scratch,
        compiler_params=pltpu.CompilerParams(
            dimension_semantics=("arbitrary",) * len(grid), vmem_limit_bytes=VMEM_BYTES
        ),
        cost_estimate=pl.CostEstimate(
            flops=int(flops) // COST, bytes_accessed=int(bytes_accessed) // COST, transcendentals=0
        ),
    )(*args)


def whole(shape):
    return pl.BlockSpec(shape, lambda c: (0,) * len(shape))


def columns(rows, width, offset=0):
    return pl.BlockSpec((rows, width), lambda c: (0, c + offset))


def struct(shape, dtype):
    return jax.ShapeDtypeStruct(shape, dtype)


def recur_in_kernel(
    groups, length,
    x_ref, halo_ref, gain_ref, wi_ref, ga_ref, gi_ref, vec_ref, mask_ref,
    normed_ref, ext_ref, rate_ref, igate_ref, keep_ref, local_ref, segp_ref, agg_ref,
    xn, conv, pre_a, pre_i,
):
    rows = groups * length
    steps = length // SUB
    width = wi_ref.shape[1]

    @pl.when(pl.program_id(0) == 0)
    def _():
        gain = gain_ref[...]
        for at, ref in ((0, x_ref), (rows, halo_ref)):
            v = ref[...].astype(F32)
            r = lax.rsqrt(jnp.mean(v * v, axis=-1, keepdims=True) + EPS)
            xn[at : at + ref.shape[0], :] = (v * r * gain).astype(BF16)
        normed_ref[...] = xn[0:rows, :]

    conv_in = nn_dot(xn[...], wi_ref[...]).astype(BF16).astype(F32)
    sub = lax.broadcasted_iota(jnp.int32, (SUB, width), 0)
    for g in range(groups):
        base = conv_in[g * length : (g + 1) * length]
        halo = conv_in[rows + g * SUB : rows + (g + 1) * SUB]
        for k in (3, 2, 1):
            block = pltpu.roll(base[(steps - k) * SUB : (steps - k + 1) * SUB], 1, 0)
            ext_ref[g, (3 - k) * SUB : (4 - k) * SUB, :] = jnp.where(sub == 0, halo[3 - k : 4 - k], block)
        ext_ref[g, 3 * SUB : 3 * SUB + length, :] = base
    taps = [vec_ref[k : k + 1, :] for k in range(CONV)]
    for g in range(groups):
        part = slice(g * length, (g + 1) * length)
        out = vec_ref[4:5, :] + taps[0] * ext_ref[g, 3 * SUB : 3 * SUB + length, :]
        for k in range(1, CONV):
            link = lanes(mask_ref[k, part, :], width)
            out = out + taps[k] * (link * ext_ref[g, (3 - k) * SUB : (3 - k) * SUB + length, :])
        conv[part, :] = out
    rounded = conv[...].astype(BF16)
    for h in range(width // LANES):
        col = slice(h * LANES, (h + 1) * LANES)
        pre_a[:, col] = nn_dot(rounded[:, col], ga_ref[h])
        pre_i[:, col] = nn_dot(rounded[:, col], gi_ref[h])
    bias_a, bias_i, scale = vec_ref[5:6, :], vec_ref[6:7, :], vec_ref[7:8, :]
    chunk = 4

    def step(i, carry):
        out = []
        for g in range(groups):
            h, p = carry[g]
            at = pl.multiple_of(g * length + i * (chunk * SUB), chunk * SUB)
            here = pl.ds(at, chunk * SUB)
            rate = sigmoid(pre_a[here, :] + bias_a)
            igate = sigmoid(pre_i[here, :] + bias_i)
            keep = jnp.exp(scale * rate) * lanes(mask_ref[0, here, :], width)
            driven = igate * conv[here, :] * jnp.sqrt(1.0 + 0.0001 - keep * keep)
            rate_ref[here, :] = rate
            igate_ref[here, :] = igate
            keep_ref[here, :] = keep
            states = []
            for q in range(chunk):
                kq = keep[q * SUB : (q + 1) * SUB]
                h = kq * h + driven[q * SUB : (q + 1) * SUB]
                p = kq * p
                states.append(h)
            local_ref[here, :] = jnp.concatenate(states, axis=0)
            out.append((h, p))
        return tuple(out)

    start = tuple((jnp.zeros((SUB, width), F32), jnp.ones((SUB, width), F32)) for _ in range(groups))
    done = lax.fori_loop(0, steps // chunk, step, start)
    for g in range(groups):
        h, p = done[g]
        segp_ref[g * SUB : (g + 1) * SUB, :] = p
        a, b = jnp.ones((1, width), F32), jnp.zeros((1, width), F32)
        for s in range(SUB):
            b = p[s : s + 1] * b + h[s : s + 1]
            a = p[s : s + 1] * a
        agg_ref[2 * g : 2 * g + 1, :] = a
        agg_ref[2 * g + 1 : 2 * g + 2, :] = b


def recur_in(x, halo, gain, w_in, first, gate_a, gate_i, vec, masks, groups, length):
    rows, dim = x.shape
    recur = vec.shape[1]
    width = 256
    blocks = recur // width
    block_f32 = columns(rows, width)
    heads = width // LANES
    ext_len = length + 3 * SUB
    return call(
        functools.partial(recur_in_kernel, groups, length),
        (blocks,),
        [
            whole(x.shape), whole(halo.shape), whole(gain.shape),
            columns(dim, width, (first + recur) // width),
            pl.BlockSpec((heads, LANES, LANES), lambda c: (c, 0, 0)),
            pl.BlockSpec((heads, LANES, LANES), lambda c: (c, 0, 0)),
            columns(8, width), whole(masks.shape),
        ],
        [
            whole((rows, dim)),
            pl.BlockSpec((groups, ext_len, width), lambda c: (0, 0, c)),
            block_f32, block_f32, block_f32, block_f32,
            columns(SUB * groups, width), columns(2 * groups, width),
        ],
        [
            struct((rows, dim), BF16), struct((groups, ext_len, recur), F32),
            struct((rows, recur), F32), struct((rows, recur), F32), struct((rows, recur), F32),
            struct((rows, recur), F32), struct((SUB * groups, recur), F32), struct((2 * groups, recur), F32),
        ],
        [
            pltpu.VMEM((rows + halo.shape[0], dim), BF16), pltpu.VMEM((rows, width), F32),
            pltpu.VMEM((rows, width), F32), pltpu.VMEM((rows, width), F32),
        ],
        2 * rows * dim * recur * 2.5,
        dim * recur * 2 + rows * recur * 4 * 5,
        (x, halo, gain, w_in, gate_a, gate_i, vec, masks),
    )


def branch_kernel(x_ref, w_ref, act_ref, slope_ref):
    act, slope = gelu_both(nn_dot(x_ref[...], w_ref[...]))
    act_ref[...] = act
    slope_ref[...] = slope


def branch_in(x, w_in, first, recur):
    rows, dim = x.shape
    width = 256
    block = columns(rows, width)
    return call(
        branch_kernel,
        (recur // width,),
        [whole(x.shape), columns(dim, width, first // width)],
        [block, block],
        [struct((rows, recur), F32)] * 2,
        [],
        2 * rows * dim * recur * 1.5,
        dim * recur * 2 + rows * recur * 8,
        (x, w_in),
    )


def recur_out_kernel(
    groups, length,
    x_ref, keep_ref, local_ref, act_ref, segp_ref, hin_ref, wo_ref, gain_ref,
    hidden_ref, mixed_ref, middle_ref, normed_ref,
    acc,
):
    steps = length // SUB
    width = keep_ref.shape[1]
    chunk = 4
    c = pl.program_id(0)
    start = []
    for g in range(groups):
        ends = local_ref[(g + 1) * length - SUB : (g + 1) * length, :]
        prods = segp_ref[g * SUB : (g + 1) * SUB, :]
        state = hin_ref[g : g + 1, :]
        entering = []
        for s in range(SUB):
            entering.append(state)
            state = prods[s : s + 1] * state + ends[s : s + 1]
        start.append(jnp.concatenate(entering, axis=0))

    def step(i, carry):
        out = []
        for g in range(groups):
            q = carry[g]
            at = pl.multiple_of(g * length + i * (chunk * SUB), chunk * SUB)
            here = pl.ds(at, chunk * SUB)
            keep = keep_ref[here, :]
            moved = []
            for r in range(chunk):
                q = keep[r * SUB : (r + 1) * SUB] * q
                moved.append(q)
            hidden = local_ref[here, :] + jnp.concatenate(moved, axis=0)
            hidden_ref[here, :] = hidden
            mixed_ref[here, :] = (hidden * act_ref[here, :]).astype(BF16)
            out.append(q)
        return tuple(out)

    lax.fori_loop(0, steps // chunk, step, tuple(start))
    part = nn_dot(mixed_ref[...], wo_ref[...])

    @pl.when(c == 0)
    def _():
        acc[...] = x_ref[...].astype(F32) + part

    @pl.when(c > 0)
    def _():
        acc[...] += part

    @pl.when(c == pl.num_programs(0) - 1)
    def _():
        m = acc[...]
        middle_ref[...] = m
        r = lax.rsqrt(jnp.mean(m * m, axis=-1, keepdims=True) + EPS)
        normed_ref[...] = (m * r * gain_ref[...]).astype(BF16)


def recur_out(x, keep, local, act, segp, hin, w_out, gain, groups, length):
    rows, dim = x.shape
    recur = keep.shape[1]
    width = 256
    block = columns(rows, width)
    return call(
        functools.partial(recur_out_kernel, groups, length),
        (recur // width,),
        [
            whole(x.shape), block, block, block, columns(SUB * groups, width), columns(groups, width),
            pl.BlockSpec((width, dim), lambda c: (c, 0)), whole(gain.shape),
        ],
        [block, block, whole((rows, dim)), whole((rows, dim))],
        [
            struct((rows, recur), F32), struct((rows, recur), BF16),
            struct((rows, dim), F32), struct((rows, dim), BF16),
        ],
        [pltpu.VMEM((rows, dim), F32)],
        2 * rows * dim * recur * 1.5,
        dim * recur * 2 + rows * recur * 18,
        (x, keep, local, act, segp, hin, w_out, gain),
    )


def ff_kernel(save, x_ref, mid_ref, wg_ref, wu_ref, wd_ref, *refs):
    c = pl.program_id(0)
    out_ref, acc = refs[-2:]
    x = x_ref[...]
    gate = nn_dot(x, wg_ref[...])
    up = nn_dot(x, wu_ref[...])
    if save:
        act_ref, slope_ref, product_ref = refs[:3]
        act, slope = gelu_both(gate)
        act_ref[...] = act.astype(BF16)
        slope_ref[...] = (up * slope).astype(BF16)
        product = (act * up).astype(BF16)
        product_ref[...] = product
    else:
        product = (gelu(gate) * up).astype(BF16)
    part = nn_dot(product, wd_ref[...])

    @pl.when(c == 0)
    def _():
        acc[...] = mid_ref[...] + part

    @pl.when(c > 0)
    def _():
        acc[...] += part

    @pl.when(c == pl.num_programs(0) - 1)
    def _():
        out_ref[...] = acc[...].astype(BF16)


def feed_forward(x, middle, w_gu, w_down, save):
    rows, dim = x.shape
    hidden = w_down.shape[0]
    width = 512
    blocks = hidden // width
    block = columns(rows, width)
    kept = 3 if save else 0
    return call(
        functools.partial(ff_kernel, save),
        (blocks,),
        [
            whole(x.shape), whole(middle.shape), columns(dim, width), columns(dim, width, blocks),
            pl.BlockSpec((width, dim), lambda c: (c, 0)),
        ],
        [block] * kept + [whole((rows, dim))],
        [struct((rows, hidden), BF16)] * kept + [struct((rows, dim), BF16)],
        [pltpu.VMEM((rows, dim), F32)],
        6 * rows * dim * hidden * 1.5,
        6 * dim * hidden,
        (x, middle, w_gu, w_gu, w_down),
    )


def norm_back(values, gain, grad):
    q = lax.rsqrt(jnp.mean(values * values, axis=-1, keepdims=True) + EPS)
    t = gain * grad
    back = q * t - values * (q * q * q * jnp.mean(values * t, axis=-1, keepdims=True))
    return back, jnp.sum(values * q * grad, axis=0, keepdims=True)


def ff_back_kernel(
    dout_ref, mid_ref, gain_ref, act_ref, slope_ref, wg_ref, wu_ref, wd_ref,
    dgu_ref, dmid_ref, low_ref, dgain_ref,
    acc,
):
    c = pl.program_id(0)
    dproduct = nt_dot(dout_ref[...], wd_ref[...])
    dgate = (dproduct * slope_ref[...].astype(F32)).astype(BF16)
    dup = (dproduct * act_ref[...].astype(F32)).astype(BF16)
    dgu_ref[0] = dgate
    dgu_ref[1] = dup
    part = nt_dot(dgate, wg_ref[...]) + nt_dot(dup, wu_ref[...])

    @pl.when(c == 0)
    def _():
        acc[...] = part

    @pl.when(c > 0)
    def _():
        acc[...] += part

    @pl.when(c == pl.num_programs(0) - 1)
    def _():
        back, dgain = norm_back(mid_ref[...], gain_ref[...], acc[...])
        dmid = dout_ref[...].astype(F32) + back
        dmid_ref[...] = dmid
        low_ref[...] = dmid.astype(BF16)
        dgain_ref[...] = dgain


def feed_forward_back(dout, middle, gain, act, slope, w_gu, w_down):
    rows, dim = dout.shape
    hidden = w_down.shape[0]
    width = 512
    blocks = hidden // width
    block = columns(rows, width)
    full = whole((rows, dim))
    return call(
        ff_back_kernel,
        (blocks,),
        [
            full, full, whole(gain.shape), block, block, columns(dim, width), columns(dim, width, blocks),
            pl.BlockSpec((width, dim), lambda c: (c, 0)),
        ],
        [pl.BlockSpec((2, rows, width), lambda c: (0, 0, c)), full, full, whole((1, dim))],
        [
            struct((2, rows, hidden), BF16), struct((rows, dim), F32),
            struct((rows, dim), BF16), struct((1, dim), F32),
        ],
        [pltpu.VMEM((rows, dim), F32)],
        6 * rows * dim * hidden * 1.2,
        6 * dim * hidden,
        (dout, middle, gain, act, slope, w_gu, w_gu, w_down),
    )


def mix_back_kernel(
    groups, length,
    low_ref, wo_ref, act_ref, slope_ref, hidden_ref, keep_ref,
    dbranch_ref, local_ref, sege_ref, segf_ref, agg_ref,
    dmixed,
):
    steps = length // SUB
    width = keep_ref.shape[1]
    chunk = 4
    dmixed[...] = nt_dot(low_ref[...], wo_ref[...])

    def step(i, carry):
        out = []
        for g in range(groups):
            s, p, after = carry[g]
            at = pl.multiple_of(g * length + (steps // chunk - 1 - i) * (chunk * SUB), chunk * SUB)
            here = pl.ds(at, chunk * SUB)
            d = dmixed[here, :]
            dbranch_ref[here, :] = (d * hidden_ref[here, :] * slope_ref[here, :]).astype(BF16)
            dhidden = d * act_ref[here, :]
            keep = keep_ref[here, :]
            states = [None] * chunk
            for r in reversed(range(chunk)):
                s = dhidden[r * SUB : (r + 1) * SUB] + after * s
                p = after * p
                after = keep[r * SUB : (r + 1) * SUB]
                states[r] = s
            local_ref[here, :] = jnp.concatenate(states, axis=0)
            out.append((s, p, after))
        return tuple(out)

    one = jnp.ones((SUB, width), F32)
    start = tuple((jnp.zeros((SUB, width), F32), one, one) for _ in range(groups))
    done = lax.fori_loop(0, steps // chunk, step, start)
    for g in range(groups):
        s, p, after = done[g]
        e, f = after * s, after * p
        sege_ref[g * SUB : (g + 1) * SUB, :] = e
        segf_ref[g * SUB : (g + 1) * SUB, :] = f
        a, b = jnp.ones((1, width), F32), jnp.zeros((1, width), F32)
        for r in reversed(range(SUB)):
            b = e[r : r + 1] + f[r : r + 1] * b
            a = f[r : r + 1] * a
        agg_ref[2 * g : 2 * g + 1, :] = a
        agg_ref[2 * g + 1 : 2 * g + 2, :] = b


def mix_back(low, w_out, act, slope, hidden, keep, groups, length):
    rows, dim = low.shape
    recur = keep.shape[1]
    width = 256
    block = columns(rows, width)
    return call(
        functools.partial(mix_back_kernel, groups, length),
        (recur // width,),
        [whole(low.shape), pl.BlockSpec((width, dim), lambda c: (c, 0)), block, block, block, block],
        [block, block, columns(SUB * groups, width), columns(SUB * groups, width), columns(2 * groups, width)],
        [
            struct((rows, recur), BF16), struct((rows, recur), F32), struct((SUB * groups, recur), F32),
            struct((SUB * groups, recur), F32), struct((2 * groups, recur), F32),
        ],
        [pltpu.VMEM((rows, width), F32)],
        2 * rows * dim * recur * 2,
        dim * recur * 2 + rows * recur * 18,
        (low, w_out, act, slope, hidden, keep),
    )


def gates_back_kernel(
    groups, length,
    local_ref, keep_ref, hidden_ref, ext_ref, rate_ref, igate_ref, sege_ref, segf_ref, gin_ref, hin_ref,
    ga_ref, gi_ref, vec_ref, mask_ref,
    din_ref, head_ref, dga_ref, dgi_ref, dvec_ref,
    dconv, low_a, low_i, rounded,
):
    steps = length // SUB
    width = keep_ref.shape[1]
    chunk = 4
    sub = lax.broadcasted_iota(jnp.int32, (SUB, width), 0)
    taps = [vec_ref[k : k + 1, :] for k in range(CONV)]
    conv_bias, scale = vec_ref[4:5, :], vec_ref[7:8, :]
    start = []
    for g in range(groups):
        e = sege_ref[g * SUB : (g + 1) * SUB, :]
        f = segf_ref[g * SUB : (g + 1) * SUB, :]
        y = gin_ref[g : g + 1, :]
        entering = [None] * SUB
        for s in reversed(range(SUB)):
            entering[s] = y
            y = e[s : s + 1] + f[s : s + 1] * y
        start.append((jnp.concatenate(entering, axis=0), jnp.ones((SUB, width), F32)))
    zero = jnp.zeros((SUB, width), F32)

    def fold(v):
        return functools.reduce(jnp.add, [v[q * SUB : (q + 1) * SUB] for q in range(v.shape[0] // SUB)])

    def step(i, carry):
        chains, sum_a, sum_i, sum_d = carry
        out = []
        j = steps // chunk - 1 - i
        for g in range(groups):
            r, after = chains[g]
            at = pl.multiple_of(g * length + j * (chunk * SUB), chunk * SUB)
            here = pl.ds(at, chunk * SUB)
            keep = keep_ref[here, :]
            parts = [None] * chunk
            for q in reversed(range(chunk)):
                r = after * r
                after = keep[q * SUB : (q + 1) * SUB]
                parts[q] = r
            state = local_ref[here, :] + jnp.concatenate(parts, axis=0)
            last = hidden_ref[(g + 1) * length - SUB : (g + 1) * length, :]
            wrapped = jnp.where(sub == 0, hin_ref[g : g + 1, :], pltpu.roll(last, 1, 0))
            before = pl.multiple_of(jnp.maximum(at - SUB, g * length), SUB)
            first = jnp.where(j == 0, wrapped, hidden_ref[pl.ds(before, SUB), :])
            rest = hidden_ref[pl.ds(at, (chunk - 1) * SUB), :]
            previous = jnp.concatenate([first, rest], axis=0)
            inner = pl.multiple_of(j * (chunk * SUB), chunk * SUB)
            conv = conv_bias + taps[0] * ext_ref[g, pl.ds(inner + 3 * SUB, chunk * SUB), :]
            for k in range(1, CONV):
                link = lanes(mask_ref[k, here, :], width)
                conv = conv + taps[k] * (link * ext_ref[g, pl.ds(inner + (3 - k) * SUB, chunk * SUB), :])
            rate, igate = rate_ref[here, :], igate_ref[here, :]
            space = 1.0 + 0.0001 - keep * keep
            inverse = lax.rsqrt(space)
            scaling = space * inverse
            both = state * igate
            dconv[here, :] = both * scaling
            with_conv = both * conv
            dlog = (state * previous - with_conv * (keep * inverse)) * keep
            dpre_a = (dlog * scale) * (rate * (1.0 - rate))
            dpre_i = (with_conv * scaling) * (1.0 - igate)
            low_a[here, :] = dpre_a.astype(BF16)
            low_i[here, :] = dpre_i.astype(BF16)
            rounded[here, :] = conv.astype(BF16)
            sum_a = sum_a + fold(dpre_a)
            sum_i = sum_i + fold(dpre_i)
            sum_d = sum_d + fold(dlog * rate)
            out.append((r, after))
        return tuple(out), sum_a, sum_i, sum_d

    _, sum_a, sum_i, sum_d = lax.fori_loop(0, steps // chunk, step, (tuple(start), zero, zero, zero))
    dvec_ref[5:6, :] = jnp.sum(sum_a, axis=0, keepdims=True)
    dvec_ref[6:7, :] = jnp.sum(sum_i, axis=0, keepdims=True)
    dvec_ref[7:8, :] = jnp.sum(sum_d, axis=0, keepdims=True)
    for h in range(width // LANES):
        col = slice(h * LANES, (h + 1) * LANES)
        dga_ref[h] = tn_dot(rounded[:, col], low_a[:, col])
        dgi_ref[h] = tn_dot(rounded[:, col], low_i[:, col])
        dconv[:, col] += nt_dot(low_a[:, col], ga_ref[h]) + nt_dot(low_i[:, col], gi_ref[h])

    sums = [zero] * (CONV + 1)
    for g in range(groups):

        def conv_step(i, carry, g=g):
            carry = list(carry)
            inner = pl.multiple_of(i * (chunk * SUB), chunk * SUB)
            here = pl.ds(pl.multiple_of(g * length + inner, chunk * SUB), chunk * SUB)
            d = dconv[here, :]
            carry[4] = carry[4] + fold(d)
            for k in range(CONV):
                masked = d if k == 0 else d * lanes(mask_ref[k, here, :], width)
                carry[k] = carry[k] + fold(masked * ext_ref[g, pl.ds(inner + (3 - k) * SUB, chunk * SUB), :])
            return tuple(carry)

        sums = list(lax.fori_loop(0, steps // chunk, conv_step, tuple(sums)))
        base = g * length
        tail = length - 3 * SUB
        total = taps[0] * dconv[base : base + tail, :]
        for k in range(1, CONV):
            there = slice(base + k * SUB, base + k * SUB + tail)
            total = total + taps[k] * (dconv[there, :] * lanes(mask_ref[k, there, :], width))
        din_ref[base : base + tail, :] = total

        def term(k, block):
            there = slice(base + block * SUB, base + (block + 1) * SUB)
            v = taps[k] * dconv[there, :]
            return v if k == 0 else v * lanes(mask_ref[k, there, :], width)

        heads = []
        for i in (3, 2, 1):
            j = steps - i
            value = term(0, j)
            head = None
            for k in range(1, CONV):
                if j + k < steps:
                    value = value + term(k, j + k)
                else:
                    t = term(k, j + k - steps)
                    value = value + jnp.where(sub == SUB - 1, 0.0, pltpu.roll(t, SUB - 1, 0))
                    head = t if head is None else head + t
            din_ref[base + j * SUB : base + (j + 1) * SUB, :] = value
            heads.append(head[0:1])
        head_ref[g * SUB : (g + 1) * SUB, :] = jnp.concatenate(heads + [jnp.zeros((SUB - 3, width), F32)], axis=0)
    for k in range(CONV + 1):
        dvec_ref[k : k + 1, :] = jnp.sum(sums[k], axis=0, keepdims=True)


def gates_back(local, keep, hidden, ext, rate, igate, sege, segf, gin, hin, gate_a, gate_i, vec, masks, groups, length):
    rows, recur = local.shape
    width = 256
    heads = width // LANES
    block = columns(rows, width)
    seg = columns(SUB * groups, width)
    gate = pl.BlockSpec((heads, LANES, LANES), lambda c: (c, 0, 0))
    return call(
        functools.partial(gates_back_kernel, groups, length),
        (recur // width,),
        [
            block, block, block, pl.BlockSpec((groups, length + 3 * SUB, width), lambda c: (0, 0, c)),
            block, block, seg, seg, columns(groups, width), columns(groups, width),
            gate, gate, columns(8, width), whole(masks.shape),
        ],
        [block, seg, gate, gate, columns(8, width)],
        [
            struct((rows, recur), F32), struct((SUB * groups, recur), F32), struct(gate_a.shape, F32),
            struct(gate_a.shape, F32), struct((8, recur), F32),
        ],
        [
            pltpu.VMEM((rows, width), F32), pltpu.VMEM((rows, width), BF16),
            pltpu.VMEM((rows, width), BF16), pltpu.VMEM((rows, width), BF16),
        ],
        rows * recur * 128 * 8 * 4,
        rows * recur * 28,
        (local, keep, hidden, ext, rate, igate, sege, segf, gin, hin, gate_a, gate_i, vec, masks),
    )


def branch_back_kernel(dbranch_ref, w_ref, out_ref):
    part = nt_dot(dbranch_ref[...], w_ref[...])

    @pl.when(pl.program_id(0) == 0)
    def _():
        out_ref[...] = part

    @pl.when(pl.program_id(0) > 0)
    def _():
        out_ref[...] += part


def branch_back(dbranch, w_in, first, dim):
    rows, recur = dbranch.shape
    width = 512
    return call(
        branch_back_kernel,
        (recur // width,),
        [columns(rows, width), columns(dim, width, first // width)],
        whole((rows, dim)),
        struct((rows, dim), F32),
        [],
        2 * rows * dim * recur,
        dim * recur * 2,
        (dbranch, w_in),
    )


def recur_in_back_kernel(
    groups, length,
    part_ref, din_ref, back_ref, wi_ref, x_ref, gain_ref, dmid_ref,
    low_ref, dx_ref, dgain_ref,
    acc,
):
    c = pl.program_id(0)
    width = din_ref.shape[1]
    rim = 4 * SUB
    sub = lax.broadcasted_iota(jnp.int32, (SUB, width), 0)
    for g in range(groups):
        base = g * length
        if length > rim:
            low_ref[base : base + length - rim, :] = din_ref[base : base + length - rim, :].astype(BF16)
        extra = [jnp.zeros((SUB, width), F32)]
        for i in range(3):
            extra.append(jnp.where(sub == SUB - 1, back_ref[g * SUB + i : g * SUB + i + 1, :], 0.0))
        tail = slice(base + length - rim, base + length)
        low_ref[tail, :] = (din_ref[tail, :] + jnp.concatenate(extra, axis=0)).astype(BF16)
    part = nt_dot(low_ref[...], wi_ref[...])

    @pl.when(c == 0)
    def _():
        acc[...] = part_ref[...] + part

    @pl.when(c > 0)
    def _():
        acc[...] += part

    @pl.when(c == pl.num_programs(0) - 1)
    def _():
        back, dgain = norm_back(x_ref[...].astype(F32), gain_ref[...], acc[...])
        dx_ref[...] = (dmid_ref[...] + back).astype(BF16)
        dgain_ref[...] = dgain


def recur_in_back(part, din, back, w_in, first, x, gain, dmid, groups, length):
    rows, dim = x.shape
    recur = din.shape[1]
    width = 512
    block = columns(rows, width)
    full = whole((rows, dim))
    return call(
        functools.partial(recur_in_back_kernel, groups, length),
        (recur // width,),
        [
            full, block, columns(SUB * groups, width), columns(dim, width, (first + recur) // width),
            full, whole(gain.shape), full,
        ],
        [block, full, whole((1, dim))],
        [struct((rows, recur), BF16), struct((rows, dim), BF16), struct((1, dim), F32)],
        [pltpu.VMEM((rows, dim), F32)],
        2 * rows * dim * recur * 1.5,
        2 * dim * recur + rows * recur * 8,
        (part, din, back, w_in, x, gain, dmid),
    )


def outer_kernel(places, pieces, place_ref, left_a, left_b, right_a, right_b, *refs):
    outs, (keep, send) = refs[:-2], refs[-2:]
    n, fs, share = places
    rows = left_a.shape[1]
    c = pl.program_id(0)
    per = pl.num_programs(0) // pieces

    @pl.when(c == 0)
    def _():
        core, y = place_ref[0], place_ref[1]
        for at in range(n):
            there = slice(at * share, (at + 1) * share)
            for scratch, side in ((keep, y), (send, 1 - y)):
                first = pl.multiple_of((at * fs + 2 * side + core) * share, share)
                scratch[there, 0:rows] = left_a[pl.ds(first, share), :]
                scratch[there, rows : 2 * rows] = left_b[pl.ds(first, share), :]

    right = jnp.concatenate([right_a[0], right_b[0]], axis=0)
    to_keep = nn_dot(keep[...], right).astype(BF16)
    to_send = nn_dot(send[...], right).astype(BF16)
    for p in range(pieces):

        @pl.when(c // per == p)
        def _(p=p):
            outs[2 * p][...] = to_keep
            outs[2 * p + 1][...] = to_send


def outer(lefts, at, k, rights, pieces, chosen, place, n, fs):
    rows = lefts[0].shape[1]
    count, _, total = rights[0].shape
    share = k // (n * fs)
    piece = count * total // pieces
    width = next(w for w in (768, 512, 384, 256, 128, piece) if piece % w == 0)
    across, per = total // width, piece // width
    skipped, pieces = chosen[0] * per, chosen[1]

    def out_block(p):
        return pl.BlockSpec((n * share, width), lambda c, place: (0, jnp.clip(c - p * per, 0, per - 1)))

    left = pl.BlockSpec((k, rows), lambda c, place: (at // k, 0))
    right = pl.BlockSpec((1, rows, width), lambda c, place: ((c + skipped) // across, 0, (c + skipped) % across))
    outs = pl.pallas_call(
        functools.partial(outer_kernel, (n, fs, share), pieces),
        grid_spec=pltpu.PrefetchScalarGridSpec(
            num_scalar_prefetch=1,
            grid=(pieces * per,),
            in_specs=[left, left, right, right],
            out_specs=[out_block(p) for p in range(pieces) for _ in range(2)],
            scratch_shapes=[pltpu.VMEM((n * share, 2 * rows), BF16)] * 2,
        ),
        out_shape=[struct((n * share, piece), BF16)] * (2 * pieces),
        compiler_params=pltpu.CompilerParams(dimension_semantics=("arbitrary",), vmem_limit_bytes=VMEM_BYTES),
        cost_estimate=pl.CostEstimate(
            flops=8 * n * share * rows * pieces * piece // COST, bytes_accessed=1, transcendentals=0
        ),
    )(place, *lefts, *rights)
    return [(outs[2 * p], outs[2 * p + 1]) for p in range(pieces)]


def unfold_kernel(folded_ref, out_ref):
    height, width = folded_ref.shape[0], out_ref.shape[1]
    for q in range(out_ref.shape[0] // height):
        out_ref[q * height : (q + 1) * height, :] = folded_ref[:, q * width : (q + 1) * width]


def unfold_first(packed, places, height, rows, width):
    return call(
        unfold_kernel,
        (places,),
        [pl.BlockSpec((height, rows // height * width), lambda c: (c, 0))],
        pl.BlockSpec((rows, width), lambda c: (c, 0)),
        struct((places * rows, width), packed.dtype),
        [],
        0,
        places * rows * width * 4,
        (packed,),
    )


def shifted(value, axis, by):
    length = lax.axis_size(axis)
    pairs = [(i, i + by) for i in range(length) if 0 <= i + by < length]
    return lax.ppermute(value, axis, pairs)


def entering(agg, groups, reverse):
    n = lax.axis_size("seq")
    sign = -1 if reverse else 1
    got = {k: shifted(agg, "seq", sign * k) for k in range(1, n)}
    state = jnp.zeros((groups, agg.shape[1]), F32)
    for k in range(n - 1, 0, -1):
        part = got[k].reshape(groups, 2, -1)
        state = part[:, 0] * state + part[:, 1]
    return state


def add(*parts):
    return functools.reduce(jnp.add, [p.astype(F32) for p in parts])


def line_sum(slots, mine, n, send):
    def at(offset):
        return slots((mine + offset) % n)

    up, down = at(n - 1), at(1)
    for s in range(1, n):
        got_up = send(up, [(i, i + 1) for i in range(s)])
        got_down = send(down, [(i, i - 1) for i in range(n - s, n)])
        if s < n - 1:
            up = add(at(n - 1 - s), got_up).astype(BF16)
            down = add(at(s + 1), got_down).astype(BF16)
    return add(at(0), got_up, got_down)


class Scatter:
    def __init__(self):
        self.n, self.fs = lax.axis_size("seq"), lax.axis_size("fsdp")
        self.ny = self.fs // 2
        self.z, f = lax.axis_index("seq"), lax.axis_index("fsdp")
        self.y, self.core = f // 2, f % 2
        self.got = None

    def core_swap(self, value):
        return lax.ppermute(value, "fsdp", [(i, i ^ 1) for i in range(self.fs)])

    def y_send(self, value, pairs):
        return lax.ppermute(value, "fsdp", [(2 * a + c, 2 * b + c) for a, b in pairs for c in range(2)])

    def over_y(self, keep, send, beside=()):
        if self.got is not None:
            send = after(send, self.got)
        self.got = self.y_send(send, [(0, 1), (1, 0)])
        return add(after(keep, beside), self.got).astype(BF16)

    def over_z(self, shares):
        return lax.psum_scatter(shares, "seq", scatter_dimension=0, tiled=True)[0].astype(F32)


def pick(value, index, axis):
    return lax.dynamic_index_in_dim(value, index, axis, keepdims=False)


def reorder(v):
    length, d = v.shape[-2:]
    return jnp.swapaxes(v.reshape(-1, SUB, length // SUB, d), 1, 2).reshape(-1, d)


def restore(v, shape):
    length, d = shape[-2:]
    return jnp.swapaxes(v.reshape(-1, length // SUB, SUB, d), 1, 2).reshape(shape)


def tail_rows(v, groups, length):
    d = v.shape[1]
    last = v.reshape(groups, length // SUB, SUB, d)[:, length // SUB - 3 :, SUB - 1]
    last = jnp.pad(last, ((0, 0), (0, SUB - 3), (0, 0))).reshape(groups * SUB, d)
    return jnp.pad(last, ((0, -groups * SUB % 16), (0, 0)))


def fold_rows(v, height):
    count = -(-v.shape[0] // height)
    v = jnp.pad(v, ((0, count * height - v.shape[0]), (0, 0)))
    return jnp.concatenate([v[i * height : (i + 1) * height] for i in range(count)], axis=1)


def fold_places(v, height):
    places, rows, width = v.shape
    count = -(-rows // height)
    v = jnp.pad(v, ((0, 0), (0, count * height - rows), (0, 0))).reshape(places, count, height, width)
    return jnp.swapaxes(v, 1, 2).reshape(places, height, count * width)


def unfold_rows(v, rows, width):
    places, height, total = v.shape
    v = jnp.swapaxes(v.reshape(places, height, total // width, width), 1, 2)
    return v.reshape(places, -1, width)[:, :rows]


def after(value, *others):
    return lax.optimization_barrier((value, others))[0]


def gather(shard):
    return lax.all_gather(shard, ("seq", "fsdp"), axis=0, tiled=True)


def body(
    ends, segment_ids, norm_one, w_branch, w_input, conv_weight, conv_bias, gate_a, gate_i, bias_a, bias_i,
    decay, w_out, norm_two, w_gate, w_up, w_down,
):
    is_first = lax.axis_index("section") == 0
    z = lax.axis_index("seq")
    n, fs = lax.axis_size("seq"), lax.axis_size("fsdp")
    places = n * fs
    micro, seqs, length, dim = ends.shape[1:]
    parts_of = 1
    groups = micro * seqs // parts_of
    rows = groups * length
    recur = w_branch.shape[2]
    heads, part, block = gate_a.shape[1:]
    hidden_dim = w_gate.shape[2]

    dshare, rshare = dim // places, recur // places
    vectors = [norm_one, norm_two] + [conv_weight[:, k] for k in range(CONV)] + [conv_bias, bias_a, bias_i, decay]
    vectors = jnp.concatenate([jnp.pad(v, ((0, 0), (0, LANES - v.shape[1]))) for v in vectors], axis=0)
    vectors = jnp.pad(vectors, ((0, 2 * SUB - vectors.shape[0]), (0, 0)))
    small = jnp.concatenate([vectors, gate_a.reshape(-1, block), gate_i.reshape(-1, block)], axis=0)
    small_rows = small.shape[0]
    small = fold_rows(small, dshare)
    first = hidden_dim
    w_in = gather(
        jnp.concatenate(
            [fold_rows(w_down[0], dshare), w_branch[0], w_input[0], w_out[0].reshape(dshare, recur), small], axis=1
        )
    )
    w_gu = gather(jnp.concatenate([after(w_gate[0], small), w_up[0]], axis=1))
    w_out_all = w_in[:, first + 2 * recur : first + 3 * recur].reshape(recur, dim)
    small = unfold_rows(w_in[:, first + 3 * recur :].reshape(places, dshare, -1), small_rows, LANES)
    hshare = hidden_dim // places
    if dshare % 16 == 0:
        w_down_all = unfold_first(w_in, places, dshare, hshare, dim)
    else:
        w_down_all = unfold_rows(w_in[:, :first].reshape(places, dshare, -1), hshare, dim).reshape(hidden_dim, dim)

    def vector(row, share):
        return small[:, row, :share].reshape(1, places * share).astype(F32)

    gain_one, gain_two = vector(0, dshare), vector(1, dshare)
    decays = vector(9, rshare)
    vec = jnp.concatenate([vector(r, rshare) for r in range(2, 9)] + [-8.0 * jax.nn.softplus(decays)], axis=0)
    gates_a, gates_i = [
        jnp.swapaxes(small[:, r : r + heads * part].reshape(places, heads, part, block), 0, 1).reshape(heads, block, block)
        for r in (2 * SUB, 2 * SUB + heads * part)
    ]

    padded_ids = jnp.pad(segment_ids, ((0, 0), (0, 0), (CONV - 1, 0)), constant_values=-1)
    window = lax.dynamic_slice_in_dim(padded_ids, z * length, length + CONV - 1, axis=2)
    current = window[:, :, CONV - 1 :]
    masks = jnp.stack(
        [window[:, :, CONV - 1 - k : CONV - 1 - k + length] == current for k in (1, 1, 2, 3)]
    ).astype(F32)
    masks = jnp.swapaxes(masks.reshape(4, parts_of, groups, SUB, length // SUB), 3, 4).reshape(4, parts_of, rows, 1)
    masks = jnp.broadcast_to(masks, (4, parts_of, rows, LANES))
    masks = [masks[:, m] for m in range(parts_of)]
    micros = range(parts_of)

    def forward(xs, halos, save):
        got = []
        for m in micros:
            got.append(recur_in(xs[m], halos[m], gain_one, w_in, first, gates_a, gates_i, vec, masks[m], groups, length))
        hin = entering(jnp.concatenate([g[7] for g in got], axis=0), parts_of * groups, False)
        acts = [branch_in(after(g[0], got[-1][7]), w_in, first, recur) for g in got]
        outs, saved = [], []
        for m in micros:
            normed, ext, rate, igate, keep, local, segp, _ = got[m]
            act, slope = acts[m]
            mine = hin[m * groups : (m + 1) * groups]
            if m:
                keep = after(keep, outs[-1])
            hidden, mixed, middle, normed_two = recur_out(
                xs[m], keep, local, act, segp, mine, w_out_all, gain_two, groups, length
            )
            results = feed_forward(normed_two, middle, w_gu, w_down_all, save)
            outs.append(results[-1])
            saved.append(
                (normed, ext, rate, igate, keep, mine, hidden, mixed, middle, normed_two, act, slope) + tuple(results[:-1])
            )
        return outs, saved

    def back_ff(m, dout, saved):
        return feed_forward_back(dout, saved[m][8], gain_two, saved[m][12], saved[m][13], w_gu, w_down_all)

    def back_mix(m, low, saved):
        return mix_back(low, w_out_all, saved[m][10], saved[m][11], saved[m][6], saved[m][4], groups, length)

    def back_gates(m, mixed_back, gin, saved):
        normed, ext, rate, igate, keep, hin, hidden = saved[m][:7]
        _, local, sege, segf, _ = mixed_back
        din, head, dga, dgi, dvec = gates_back(
            local, keep, hidden, ext, rate, igate, sege, segf, gin[m * groups : (m + 1) * groups], hin,
            gates_a, gates_i, vec, masks[m], groups, length,
        )
        return din, shifted(head, "seq", -1), dga, dgi, dvec

    def back_in(m, part, gates, dmid, xs):
        return recur_in_back(part, gates[0], gates[1], w_in, first, xs[m], gain_one, dmid, groups, length)

    own = [reorder(v) for v in ends[0].reshape((parts_of, -1) + ends.shape[3:])]
    tails = [shifted(tail_rows(v, groups, length), "seq", 1) for v in own]
    outs, _ = forward(own, tails, False)
    xs, halos = [], []
    for m in micros:
        received = shifted(outs[m], "section", 1)
        received_halo = lax.ppermute(
            tail_rows(outs[m], groups, length), ("section", "seq"), [(i, n + i + 1) for i in range(n - 1)]
        )
        xs.append(jnp.where(is_first, own[m], received))
        halos.append(jnp.where(is_first, tails[m], received_halo))
    outs, saved = forward(xs, halos, True)

    ff = [back_ff(m, own[m], saved) for m in micros]
    mix = [back_mix(m, ff[m][2], saved) for m in micros]
    gin = entering(jnp.concatenate([v[4] for v in mix], axis=0), parts_of * groups, True)
    parts = [branch_back(after(v[0], mix[-1][4]), w_in, first, dim) for v in mix]
    gates = [back_gates(m, mix[m], gin, saved) for m in micros]
    sent = []
    for m in micros:
        dx = back_in(m, after(parts[m], gates[-1][0], *sent[-1:]), gates[m], ff[m][1], xs)[1]
        sent.append(dx)

    scatter = Scatter()
    swap = scatter.core_swap
    place = jnp.stack([scatter.core, scatter.y]).astype(jnp.int32)
    dx = sent[-1]
    kinds = {"product": 14, "two": 9, "one": 0, "mixed": 7}
    starts_at, stacked, total_rows = {}, [], 0
    for name, index in kinds.items():
        v = after(saved[0][index], dx)
        gap = -total_rows % v.shape[1]
        if gap:
            stacked.append(jnp.zeros((rows, gap), BF16))
        starts_at[name] = (total_rows + gap, v.shape[1])
        total_rows += gap + v.shape[1]
        stacked.append(v)
    lefts = jnp.concatenate([v.T for v in stacked], axis=0)
    lefts = (lefts, swap(lefts))
    dout = jnp.where(is_first, after(shifted(dx, "section", -1), lefts[0]), own[0])
    dout, lefts = lax.optimization_barrier((dout, lefts))

    def pair(value):
        value = value if value.ndim == 3 else value[None]
        return value, swap(value)

    def products(name, rights, pieces=1, chosen=None):
        at, k = starts_at[name]
        chosen = chosen or (0, pieces)
        if scatter.ny == 2:
            return outer(lefts, at, k, rights, pieces, chosen, place, n, fs)
        left = jnp.concatenate([v[at : at + k] for v in lefts], axis=1)
        right = jnp.concatenate([jnp.concatenate(list(v), axis=1) for v in rights], axis=0)
        grad = nn_dot(left, right).astype(BF16)
        grad = pick(grad.reshape(n, scatter.ny, 2, -1, grad.shape[1]), scatter.core, 2)
        return [(p,) for p in jnp.split(grad, pieces, axis=3)[chosen[0] : sum(chosen)]]

    def over_y(grads, *beside):
        if scatter.ny == 2:
            return scatter.over_y(*[g.reshape(n, -1, g.shape[1]) for g in grads], beside)
        (grad,) = grads
        return line_sum(lambda d: pick(grad, d, 1), scatter.y, scatter.ny, scatter.y_send).astype(BF16)

    down = products("product", pair(dout), 2)
    dgu, dmid, out_low, dgain_two = back_ff(0, after(dout, down), saved)
    down_sums = [over_y(down[0], out_low)]
    dgu, out_low = after((dgu, out_low), down_sums[0])
    gu_pair = pair(dgu)
    mix = back_mix(0, out_low, saved)
    down_sums.append(over_y(down[1], mix[0]))
    first_gate = products("two", after(gu_pair, down_sums[1]), 4, (0, 1))
    gin = entering(after(mix[4], first_gate), groups, True)
    gate_up = first_gate + products("two", after(gu_pair, first_gate), 4, (1, 3))
    gate_up_sums = [over_y(gate_up[0], gate_up[1], gin)]
    gates = back_gates(0, after(mix, gate_up_sums[0]), gin, saved)
    gate_up_sums.append(over_y(gate_up[1], gates[0]))
    out_low, dbranch, gates = after((out_low, mix[0], gates), gate_up_sums[1])
    out_pair, branch_pair = pair(out_low), pair(dbranch)
    base = branch_back(dbranch, w_in, first, dim)
    results = back_in(0, base, gates, dmid, xs)
    gate_up_sums.append(over_y(gate_up[2], results[1], out_pair[1], branch_pair[1]))
    input_pair = pair(after(results[0], gate_up_sums[2]))
    out = products("mixed", after(out_pair, gate_up_sums[2]))
    branch = products("one", after(branch_pair, out))
    gate_up_sums.append(over_y(gate_up[3], branch))
    into = products("one", after(input_pair, gate_up_sums[3]))
    out_sum = over_y(out[0], into)
    branch_sum = over_y(branch[0])

    outputs = restore(outs[0], ends.shape)
    input_grads = restore(results[1], ends.shape)
    dgain_one = results[2]
    dga, dgi, dvec = gates[2:5]
    ddecay = -8.0 * jax.nn.sigmoid(decays) * dvec[7:8]
    shares = [dgain_one, dgain_two] + [dvec[k : k + 1] for k in range(7)] + [ddecay]
    shares = [v.reshape(places, 1, -1) for v in shares]
    shares = [jnp.pad(v, ((0, 0), (0, 0), (0, LANES - v.shape[2]))) for v in shares]
    shares = jnp.pad(jnp.concatenate(shares, axis=1), ((0, 0), (0, 2 * SUB - len(shares)), (0, 0)))
    packed = jnp.concatenate(
        [shares]
        + [jnp.swapaxes(v.reshape(heads, places, part, block), 0, 1).reshape(places, -1, block) for v in (dga, dgi)],
        axis=1,
    )
    extra = fold_places(packed, dshare).reshape(n, scatter.ny, 2, dshare, -1)
    theirs = swap(pick(extra, 1 - scatter.core, 2).astype(BF16))
    extra = add(pick(extra, scatter.core, 2), theirs).astype(BF16)
    if scatter.ny == 2:
        sides = (pick(extra, scatter.y, 1), pick(extra, 1 - scatter.y, 1))
        into = [
            jnp.concatenate([g.reshape(n, dshare, -1), v], axis=2).reshape(n * dshare, -1) for g, v in zip(into[0], sides)
        ]
    else:
        into = (jnp.concatenate([into[0][0], extra], axis=3),)
    input_sum = over_y(into)

    sum_down = jnp.concatenate([scatter.over_z(v) for v in down_sums], axis=1)
    sum_gate, sum_up = [
        jnp.concatenate([scatter.over_z(v) for v in gate_up_sums[i : i + 2]], axis=1) for i in (0, 2)
    ]
    sum_out, sum_branch, sum_input = [scatter.over_z(v) for v in (out_sum, branch_sum, input_sum)]
    sum_input, sums = sum_input[:, :recur], sum_input[:, recur:]
    sums = unfold_rows(sums[None], small_rows, LANES)[0]
    gate_sums = [sums[r : r + heads * part].reshape(gate_a.shape) for r in (2 * SUB, 2 * SUB + heads * part)]

    return (
        outputs,
        input_grads,
        sums[0:1, :dshare],
        sum_branch[None],
        sum_input[None],
        sums[2 : 2 + CONV, :rshare][None],
        sums[6:7, :rshare],
        gate_sums[0],
        gate_sums[1],
        sums[7:8, :rshare],
        sums[8:9, :rshare],
        sums[9:10, :rshare],
        sum_out[None],
        sums[1:2, :dshare],
        sum_gate[None],
        sum_up[None],
        sum_down[None],
    )


def solution(mesh):
    tokens = P("section", None, "fsdp", "seq", None)
    vector = P("section", ("seq", "fsdp"))
    matrix = P("section", ("seq", "fsdp"), None)
    taps = P("section", None, ("seq", "fsdp"))
    gates = P("section", None, ("seq", "fsdp"), None)
    weights = (
        vector, matrix, matrix, taps, vector, gates, gates, vector, vector, vector, matrix, vector, matrix, matrix, matrix,
    )
    return jax.shard_map(
        body,
        mesh=mesh,
        in_specs=(tokens, P(None, "fsdp", None)) + weights,
        out_specs=(tokens, tokens) + weights,
        check_vma=False,
    )
```

```python
import functools

import jax
import jax.numpy as jnp
from jax import lax
from jax.experimental import pallas as pl
from jax.experimental.pallas import tpu as pltpu
from jax.sharding import PartitionSpec as P

CONV = 4
EPS = 1e-06
F32 = jnp.float32
BF16 = jnp.bfloat16
VMEM_BYTES = 56 << 20
LANES = 128
SUB = 8
COST = 4


def nn_dot(a, b):
    return lax.dot_general(a, b, (((1,), (0,)), ((), ())), preferred_element_type=F32)


def nt_dot(a, b):
    return lax.dot_general(a, b, (((1,), (1,)), ((), ())), preferred_element_type=F32)


def tn_dot(a, b):
    return lax.dot_general(a, b, (((0,), (0,)), ((), ())), preferred_element_type=F32)


def sigmoid(v):
    return 0.5 * jnp.tanh(0.5 * v) + 0.5


K0 = 0.7978845608028654
K1 = 0.044715


def gelu(v):
    return 0.5 * v * (1.0 + jnp.tanh(K0 * (v + K1 * v * v * v)))


def gelu_both(v):
    square = v * v
    t = jnp.tanh(K0 * v * (1.0 + K1 * square))
    half = 0.5 * (1.0 + t)
    slope = half + (0.5 * K0) * v * (1.0 - t * t) * (1.0 + (3.0 * K1) * square)
    return v * half, slope


def lanes(mask, width):
    return jnp.concatenate([mask] * (width // LANES), axis=1) if width > LANES else mask


def call(kernel, grid, in_specs, out_specs, out_shape, scratch, flops, bytes_accessed, args):
    return pl.pallas_call(
        kernel,
        grid=grid,
        in_specs=in_specs,
        out_specs=out_specs,
        out_shape=out_shape,
        scratch_shapes=scratch,
        compiler_params=pltpu.CompilerParams(
            dimension_semantics=("arbitrary",) * len(grid), vmem_limit_bytes=VMEM_BYTES
        ),
        cost_estimate=pl.CostEstimate(
            flops=int(flops) // COST, bytes_accessed=int(bytes_accessed) // COST, transcendentals=0
        ),
    )(*args)


def whole(shape):
    return pl.BlockSpec(shape, lambda c: (0,) * len(shape))


def columns(rows, width, offset=0):
    return pl.BlockSpec((rows, width), lambda c: (0, c + offset))


def struct(shape, dtype):
    return jax.ShapeDtypeStruct(shape, dtype)


def recur_in_kernel(
    groups, length,
    x_ref, halo_ref, gain_ref, wi_ref, ga_ref, gi_ref, vec_ref, mask_ref,
    normed_ref, ext_ref, rate_ref, igate_ref, keep_ref, local_ref, segp_ref, agg_ref,
    xn, conv, pre_a, pre_i,
):
    rows = groups * length
    steps = length // SUB
    width = wi_ref.shape[1]

    @pl.when(pl.program_id(0) == 0)
    def _():
        gain = gain_ref[...]
        for at, ref in ((0, x_ref), (rows, halo_ref)):
            v = ref[...].astype(F32)
            r = lax.rsqrt(jnp.mean(v * v, axis=-1, keepdims=True) + EPS)
            xn[at : at + ref.shape[0], :] = (v * r * gain).astype(BF16)
        normed_ref[...] = xn[0:rows, :]

    conv_in = nn_dot(xn[...], wi_ref[...]).astype(BF16).astype(F32)
    sub = lax.broadcasted_iota(jnp.int32, (SUB, width), 0)
    for g in range(groups):
        base = conv_in[g * length : (g + 1) * length]
        halo = conv_in[rows + g * SUB : rows + (g + 1) * SUB]
        for k in (3, 2, 1):
            block = pltpu.roll(base[(steps - k) * SUB : (steps - k + 1) * SUB], 1, 0)
            ext_ref[g, (3 - k) * SUB : (4 - k) * SUB, :] = jnp.where(sub == 0, halo[3 - k : 4 - k], block)
        ext_ref[g, 3 * SUB : 3 * SUB + length, :] = base
    taps = [vec_ref[k : k + 1, :] for k in range(CONV)]
    for g in range(groups):
        part = slice(g * length, (g + 1) * length)
        out = vec_ref[4:5, :] + taps[0] * ext_ref[g, 3 * SUB : 3 * SUB + length, :]
        for k in range(1, CONV):
            link = lanes(mask_ref[k, part, :], width)
            out = out + taps[k] * (link * ext_ref[g, (3 - k) * SUB : (3 - k) * SUB + length, :])
        conv[part, :] = out
    rounded = conv[...].astype(BF16)
    for h in range(width // LANES):
        col = slice(h * LANES, (h + 1) * LANES)
        pre_a[:, col] = nn_dot(rounded[:, col], ga_ref[h])
        pre_i[:, col] = nn_dot(rounded[:, col], gi_ref[h])
    bias_a, bias_i, scale = vec_ref[5:6, :], vec_ref[6:7, :], vec_ref[7:8, :]
    chunk = 4

    def step(i, carry):
        out = []
        for g in range(groups):
            h, p = carry[g]
            at = pl.multiple_of(g * length + i * (chunk * SUB), chunk * SUB)
            here = pl.ds(at, chunk * SUB)
            rate = sigmoid(pre_a[here, :] + bias_a)
            igate = sigmoid(pre_i[here, :] + bias_i)
            keep = jnp.exp(scale * rate) * lanes(mask_ref[0, here, :], width)
            driven = igate * conv[here, :] * jnp.sqrt(1.0 + 0.0001 - keep * keep)
            rate_ref[here, :] = rate
            igate_ref[here, :] = igate
            keep_ref[here, :] = keep
            states = []
            for q in range(chunk):
                kq = keep[q * SUB : (q + 1) * SUB]
                h = kq * h + driven[q * SUB : (q + 1) * SUB]
                p = kq * p
                states.append(h)
            local_ref[here, :] = jnp.concatenate(states, axis=0)
            out.append((h, p))
        return tuple(out)

    start = tuple((jnp.zeros((SUB, width), F32), jnp.ones((SUB, width), F32)) for _ in range(groups))
    done = lax.fori_loop(0, steps // chunk, step, start)
    for g in range(groups):
        h, p = done[g]
        segp_ref[g * SUB : (g + 1) * SUB, :] = p
        a, b = jnp.ones((1, width), F32), jnp.zeros((1, width), F32)
        for s in range(SUB):
            b = p[s : s + 1] * b + h[s : s + 1]
            a = p[s : s + 1] * a
        agg_ref[2 * g : 2 * g + 1, :] = a
        agg_ref[2 * g + 1 : 2 * g + 2, :] = b


def recur_in(x, halo, gain, w_in, first, gate_a, gate_i, vec, masks, groups, length):
    rows, dim = x.shape
    recur = vec.shape[1]
    width = 512
    blocks = recur // width
    block_f32 = columns(rows, width)
    heads = width // LANES
    ext_len = length + 3 * SUB
    return call(
        functools.partial(recur_in_kernel, groups, length),
        (blocks,),
        [
            whole(x.shape), whole(halo.shape), whole(gain.shape),
            columns(dim, width, (first + recur) // width),
            pl.BlockSpec((heads, LANES, LANES), lambda c: (c, 0, 0)),
            pl.BlockSpec((heads, LANES, LANES), lambda c: (c, 0, 0)),
            columns(8, width), whole(masks.shape),
        ],
        [
            whole((rows, dim)),
            pl.BlockSpec((groups, ext_len, width), lambda c: (0, 0, c)),
            block_f32, block_f32, block_f32, block_f32,
            columns(SUB * groups, width), columns(2 * groups, width),
        ],
        [
            struct((rows, dim), BF16), struct((groups, ext_len, recur), F32),
            struct((rows, recur), F32), struct((rows, recur), F32), struct((rows, recur), F32),
            struct((rows, recur), F32), struct((SUB * groups, recur), F32), struct((2 * groups, recur), F32),
        ],
        [
            pltpu.VMEM((rows + halo.shape[0], dim), BF16), pltpu.VMEM((rows, width), F32),
            pltpu.VMEM((rows, width), F32), pltpu.VMEM((rows, width), F32),
        ],
        2 * rows * dim * recur * 2.5,
        dim * recur * 2 + rows * recur * 4 * 5,
        (x, halo, gain, w_in, gate_a, gate_i, vec, masks),
    )


def branch_kernel(x_ref, w_ref, act_ref, slope_ref):
    act, slope = gelu_both(nn_dot(x_ref[...], w_ref[...]))
    act_ref[...] = act
    slope_ref[...] = slope


def branch_in(x, w_in, first, recur):
    rows, dim = x.shape
    width = 512
    block = columns(rows, width)
    return call(
        branch_kernel,
        (recur // width,),
        [whole(x.shape), columns(dim, width, first // width)],
        [block, block],
        [struct((rows, recur), F32)] * 2,
        [],
        2 * rows * dim * recur * 1.5,
        dim * recur * 2 + rows * recur * 8,
        (x, w_in),
    )


def recur_out_kernel(
    groups, length,
    x_ref, keep_ref, local_ref, act_ref, segp_ref, hin_ref, wo_ref, gain_ref,
    hidden_ref, mixed_ref, middle_ref, normed_ref,
    acc,
):
    steps = length // SUB
    width = keep_ref.shape[1]
    chunk = 4
    c = pl.program_id(0)
    start = []
    for g in range(groups):
        ends = local_ref[(g + 1) * length - SUB : (g + 1) * length, :]
        prods = segp_ref[g * SUB : (g + 1) * SUB, :]
        state = hin_ref[g : g + 1, :]
        entering = []
        for s in range(SUB):
            entering.append(state)
            state = prods[s : s + 1] * state + ends[s : s + 1]
        start.append(jnp.concatenate(entering, axis=0))

    def step(i, carry):
        out = []
        for g in range(groups):
            q = carry[g]
            at = pl.multiple_of(g * length + i * (chunk * SUB), chunk * SUB)
            here = pl.ds(at, chunk * SUB)
            keep = keep_ref[here, :]
            moved = []
            for r in range(chunk):
                q = keep[r * SUB : (r + 1) * SUB] * q
                moved.append(q)
            hidden = local_ref[here, :] + jnp.concatenate(moved, axis=0)
            hidden_ref[here, :] = hidden
            mixed_ref[here, :] = (hidden * act_ref[here, :]).astype(BF16)
            out.append(q)
        return tuple(out)

    lax.fori_loop(0, steps // chunk, step, tuple(start))
    part = nn_dot(mixed_ref[...], wo_ref[...])

    @pl.when(c == 0)
    def _():
        acc[...] = x_ref[...].astype(F32) + part

    @pl.when(c > 0)
    def _():
        acc[...] += part

    @pl.when(c == pl.num_programs(0) - 1)
    def _():
        m = acc[...]
        middle_ref[...] = m
        r = lax.rsqrt(jnp.mean(m * m, axis=-1, keepdims=True) + EPS)
        normed_ref[...] = (m * r * gain_ref[...]).astype(BF16)


def recur_out(x, keep, local, act, segp, hin, w_out, gain, groups, length):
    rows, dim = x.shape
    recur = keep.shape[1]
    width = 512
    block = columns(rows, width)
    return call(
        functools.partial(recur_out_kernel, groups, length),
        (recur // width,),
        [
            whole(x.shape), block, block, block, columns(SUB * groups, width), columns(groups, width),
            pl.BlockSpec((width, dim), lambda c: (c, 0)), whole(gain.shape),
        ],
        [block, block, whole((rows, dim)), whole((rows, dim))],
        [
            struct((rows, recur), F32), struct((rows, recur), BF16),
            struct((rows, dim), F32), struct((rows, dim), BF16),
        ],
        [pltpu.VMEM((rows, dim), F32)],
        2 * rows * dim * recur * 1.5,
        dim * recur * 2 + rows * recur * 18,
        (x, keep, local, act, segp, hin, w_out, gain),
    )


def ff_kernel(save, x_ref, mid_ref, wg_ref, wu_ref, wd_ref, *refs):
    c = pl.program_id(0)
    out_ref, acc = refs[-2:]
    x = x_ref[...]
    gate = nn_dot(x, wg_ref[...])
    up = nn_dot(x, wu_ref[...])
    if save:
        act_ref, slope_ref, product_ref = refs[:3]
        act, slope = gelu_both(gate)
        act_ref[...] = act.astype(BF16)
        slope_ref[...] = (up * slope).astype(BF16)
        product = (act * up).astype(BF16)
        product_ref[...] = product
    else:
        product = (gelu(gate) * up).astype(BF16)
    part = nn_dot(product, wd_ref[...])

    @pl.when(c == 0)
    def _():
        acc[...] = mid_ref[...] + part

    @pl.when(c > 0)
    def _():
        acc[...] += part

    @pl.when(c == pl.num_programs(0) - 1)
    def _():
        out_ref[...] = acc[...].astype(BF16)


def feed_forward(x, middle, w_gu, w_down, save):
    rows, dim = x.shape
    hidden = w_down.shape[0]
    width = 512
    blocks = hidden // width
    block = columns(rows, width)
    kept = 3 if save else 0
    return call(
        functools.partial(ff_kernel, save),
        (blocks,),
        [
            whole(x.shape), whole(middle.shape), columns(dim, width), columns(dim, width, blocks),
            pl.BlockSpec((width, dim), lambda c: (c, 0)),
        ],
        [block] * kept + [whole((rows, dim))],
        [struct((rows, hidden), BF16)] * kept + [struct((rows, dim), BF16)],
        [pltpu.VMEM((rows, dim), F32)],
        6 * rows * dim * hidden * 1.5,
        6 * dim * hidden,
        (x, middle, w_gu, w_gu, w_down),
    )


def norm_back(values, gain, grad):
    q = lax.rsqrt(jnp.mean(values * values, axis=-1, keepdims=True) + EPS)
    t = gain * grad
    back = q * t - values * (q * q * q * jnp.mean(values * t, axis=-1, keepdims=True))
    return back, jnp.sum(values * q * grad, axis=0, keepdims=True)


def ff_back_kernel(
    dout_ref, mid_ref, gain_ref, act_ref, slope_ref, wg_ref, wu_ref, wd_ref,
    dgu_ref, dmid_ref, low_ref, dgain_ref,
    acc,
):
    c = pl.program_id(0)
    dproduct = nt_dot(dout_ref[...], wd_ref[...])
    dgate = (dproduct * slope_ref[...].astype(F32)).astype(BF16)
    dup = (dproduct * act_ref[...].astype(F32)).astype(BF16)
    dgu_ref[0] = dgate
    dgu_ref[1] = dup
    part = nt_dot(dgate, wg_ref[...]) + nt_dot(dup, wu_ref[...])

    @pl.when(c == 0)
    def _():
        acc[...] = part

    @pl.when(c > 0)
    def _():
        acc[...] += part

    @pl.when(c == pl.num_programs(0) - 1)
    def _():
        back, dgain = norm_back(mid_ref[...], gain_ref[...], acc[...])
        dmid = dout_ref[...].astype(F32) + back
        dmid_ref[...] = dmid
        low_ref[...] = dmid.astype(BF16)
        dgain_ref[...] = dgain


def feed_forward_back(dout, middle, gain, act, slope, w_gu, w_down):
    rows, dim = dout.shape
    hidden = w_down.shape[0]
    width = 512
    blocks = hidden // width
    block = columns(rows, width)
    full = whole((rows, dim))
    return call(
        ff_back_kernel,
        (blocks,),
        [
            full, full, whole(gain.shape), block, block, columns(dim, width), columns(dim, width, blocks),
            pl.BlockSpec((width, dim), lambda c: (c, 0)),
        ],
        [pl.BlockSpec((2, rows, width), lambda c: (0, 0, c)), full, full, whole((1, dim))],
        [
            struct((2, rows, hidden), BF16), struct((rows, dim), F32),
            struct((rows, dim), BF16), struct((1, dim), F32),
        ],
        [pltpu.VMEM((rows, dim), F32)],
        6 * rows * dim * hidden * 1.2,
        6 * dim * hidden,
        (dout, middle, gain, act, slope, w_gu, w_gu, w_down),
    )


def mix_back_kernel(
    groups, length,
    low_ref, wo_ref, act_ref, slope_ref, hidden_ref, keep_ref,
    dbranch_ref, local_ref, sege_ref, segf_ref, agg_ref,
    dmixed,
):
    steps = length // SUB
    width = keep_ref.shape[1]
    chunk = 4
    dmixed[...] = nt_dot(low_ref[...], wo_ref[...])

    def step(i, carry):
        out = []
        for g in range(groups):
            s, p, after = carry[g]
            at = pl.multiple_of(g * length + (steps // chunk - 1 - i) * (chunk * SUB), chunk * SUB)
            here = pl.ds(at, chunk * SUB)
            d = dmixed[here, :]
            dbranch_ref[here, :] = (d * hidden_ref[here, :] * slope_ref[here, :]).astype(BF16)
            dhidden = d * act_ref[here, :]
            keep = keep_ref[here, :]
            states = [None] * chunk
            for r in reversed(range(chunk)):
                s = dhidden[r * SUB : (r + 1) * SUB] + after * s
                p = after * p
                after = keep[r * SUB : (r + 1) * SUB]
                states[r] = s
            local_ref[here, :] = jnp.concatenate(states, axis=0)
            out.append((s, p, after))
        return tuple(out)

    one = jnp.ones((SUB, width), F32)
    start = tuple((jnp.zeros((SUB, width), F32), one, one) for _ in range(groups))
    done = lax.fori_loop(0, steps // chunk, step, start)
    for g in range(groups):
        s, p, after = done[g]
        e, f = after * s, after * p
        sege_ref[g * SUB : (g + 1) * SUB, :] = e
        segf_ref[g * SUB : (g + 1) * SUB, :] = f
        a, b = jnp.ones((1, width), F32), jnp.zeros((1, width), F32)
        for r in reversed(range(SUB)):
            b = e[r : r + 1] + f[r : r + 1] * b
            a = f[r : r + 1] * a
        agg_ref[2 * g : 2 * g + 1, :] = a
        agg_ref[2 * g + 1 : 2 * g + 2, :] = b


def mix_back(low, w_out, act, slope, hidden, keep, groups, length):
    rows, dim = low.shape
    recur = keep.shape[1]
    width = 512
    block = columns(rows, width)
    return call(
        functools.partial(mix_back_kernel, groups, length),
        (recur // width,),
        [whole(low.shape), pl.BlockSpec((width, dim), lambda c: (c, 0)), block, block, block, block],
        [block, block, columns(SUB * groups, width), columns(SUB * groups, width), columns(2 * groups, width)],
        [
            struct((rows, recur), BF16), struct((rows, recur), F32), struct((SUB * groups, recur), F32),
            struct((SUB * groups, recur), F32), struct((2 * groups, recur), F32),
        ],
        [pltpu.VMEM((rows, width), F32)],
        2 * rows * dim * recur * 2,
        dim * recur * 2 + rows * recur * 18,
        (low, w_out, act, slope, hidden, keep),
    )


def gates_back_kernel(
    groups, length,
    local_ref, keep_ref, hidden_ref, ext_ref, rate_ref, igate_ref, sege_ref, segf_ref, gin_ref, hin_ref,
    ga_ref, gi_ref, vec_ref, mask_ref,
    din_ref, head_ref, dga_ref, dgi_ref, dvec_ref,
    dconv, low_a, low_i, rounded,
):
    steps = length // SUB
    width = keep_ref.shape[1]
    chunk = 4
    sub = lax.broadcasted_iota(jnp.int32, (SUB, width), 0)
    taps = [vec_ref[k : k + 1, :] for k in range(CONV)]
    conv_bias, scale = vec_ref[4:5, :], vec_ref[7:8, :]
    start = []
    for g in range(groups):
        e = sege_ref[g * SUB : (g + 1) * SUB, :]
        f = segf_ref[g * SUB : (g + 1) * SUB, :]
        y = gin_ref[g : g + 1, :]
        entering = [None] * SUB
        for s in reversed(range(SUB)):
            entering[s] = y
            y = e[s : s + 1] + f[s : s + 1] * y
        start.append((jnp.concatenate(entering, axis=0), jnp.ones((SUB, width), F32)))
    zero = jnp.zeros((SUB, width), F32)

    def fold(v):
        return functools.reduce(jnp.add, [v[q * SUB : (q + 1) * SUB] for q in range(v.shape[0] // SUB)])

    def step(i, carry):
        chains, sum_a, sum_i, sum_d = carry
        out = []
        j = steps // chunk - 1 - i
        for g in range(groups):
            r, after = chains[g]
            at = pl.multiple_of(g * length + j * (chunk * SUB), chunk * SUB)
            here = pl.ds(at, chunk * SUB)
            keep = keep_ref[here, :]
            parts = [None] * chunk
            for q in reversed(range(chunk)):
                r = after * r
                after = keep[q * SUB : (q + 1) * SUB]
                parts[q] = r
            state = local_ref[here, :] + jnp.concatenate(parts, axis=0)
            last = hidden_ref[(g + 1) * length - SUB : (g + 1) * length, :]
            wrapped = jnp.where(sub == 0, hin_ref[g : g + 1, :], pltpu.roll(last, 1, 0))
            before = pl.multiple_of(jnp.maximum(at - SUB, g * length), SUB)
            first = jnp.where(j == 0, wrapped, hidden_ref[pl.ds(before, SUB), :])
            rest = hidden_ref[pl.ds(at, (chunk - 1) * SUB), :]
            previous = jnp.concatenate([first, rest], axis=0)
            inner = pl.multiple_of(j * (chunk * SUB), chunk * SUB)
            conv = conv_bias + taps[0] * ext_ref[g, pl.ds(inner + 3 * SUB, chunk * SUB), :]
            for k in range(1, CONV):
                link = lanes(mask_ref[k, here, :], width)
                conv = conv + taps[k] * (link * ext_ref[g, pl.ds(inner + (3 - k) * SUB, chunk * SUB), :])
            rate, igate = rate_ref[here, :], igate_ref[here, :]
            space = 1.0 + 0.0001 - keep * keep
            inverse = lax.rsqrt(space)
            scaling = space * inverse
            both = state * igate
            dconv[here, :] = both * scaling
            with_conv = both * conv
            dlog = (state * previous - with_conv * (keep * inverse)) * keep
            dpre_a = (dlog * scale) * (rate * (1.0 - rate))
            dpre_i = (with_conv * scaling) * (1.0 - igate)
            low_a[here, :] = dpre_a.astype(BF16)
            low_i[here, :] = dpre_i.astype(BF16)
            rounded[here, :] = conv.astype(BF16)
            sum_a = sum_a + fold(dpre_a)
            sum_i = sum_i + fold(dpre_i)
            sum_d = sum_d + fold(dlog * rate)
            out.append((r, after))
        return tuple(out), sum_a, sum_i, sum_d

    _, sum_a, sum_i, sum_d = lax.fori_loop(0, steps // chunk, step, (tuple(start), zero, zero, zero))
    dvec_ref[5:6, :] = jnp.sum(sum_a, axis=0, keepdims=True)
    dvec_ref[6:7, :] = jnp.sum(sum_i, axis=0, keepdims=True)
    dvec_ref[7:8, :] = jnp.sum(sum_d, axis=0, keepdims=True)
    for h in range(width // LANES):
        col = slice(h * LANES, (h + 1) * LANES)
        dga_ref[h] = tn_dot(rounded[:, col], low_a[:, col])
        dgi_ref[h] = tn_dot(rounded[:, col], low_i[:, col])
        dconv[:, col] += nt_dot(low_a[:, col], ga_ref[h]) + nt_dot(low_i[:, col], gi_ref[h])

    sums = [zero] * (CONV + 1)
    for g in range(groups):

        def conv_step(i, carry, g=g):
            carry = list(carry)
            inner = pl.multiple_of(i * (chunk * SUB), chunk * SUB)
            here = pl.ds(pl.multiple_of(g * length + inner, chunk * SUB), chunk * SUB)
            d = dconv[here, :]
            carry[4] = carry[4] + fold(d)
            for k in range(CONV):
                masked = d if k == 0 else d * lanes(mask_ref[k, here, :], width)
                carry[k] = carry[k] + fold(masked * ext_ref[g, pl.ds(inner + (3 - k) * SUB, chunk * SUB), :])
            return tuple(carry)

        sums = list(lax.fori_loop(0, steps // chunk, conv_step, tuple(sums)))
        base = g * length
        tail = length - 3 * SUB
        total = taps[0] * dconv[base : base + tail, :]
        for k in range(1, CONV):
            there = slice(base + k * SUB, base + k * SUB + tail)
            total = total + taps[k] * (dconv[there, :] * lanes(mask_ref[k, there, :], width))
        din_ref[base : base + tail, :] = total

        def term(k, block):
            there = slice(base + block * SUB, base + (block + 1) * SUB)
            v = taps[k] * dconv[there, :]
            return v if k == 0 else v * lanes(mask_ref[k, there, :], width)

        heads = []
        for i in (3, 2, 1):
            j = steps - i
            value = term(0, j)
            head = None
            for k in range(1, CONV):
                if j + k < steps:
                    value = value + term(k, j + k)
                else:
                    t = term(k, j + k - steps)
                    value = value + jnp.where(sub == SUB - 1, 0.0, pltpu.roll(t, SUB - 1, 0))
                    head = t if head is None else head + t
            din_ref[base + j * SUB : base + (j + 1) * SUB, :] = value
            heads.append(head[0:1])
        head_ref[g * SUB : (g + 1) * SUB, :] = jnp.concatenate(heads + [jnp.zeros((SUB - 3, width), F32)], axis=0)
    for k in range(CONV + 1):
        dvec_ref[k : k + 1, :] = jnp.sum(sums[k], axis=0, keepdims=True)


def gates_back(local, keep, hidden, ext, rate, igate, sege, segf, gin, hin, gate_a, gate_i, vec, masks, groups, length):
    rows, recur = local.shape
    width = 512
    heads = width // LANES
    block = columns(rows, width)
    seg = columns(SUB * groups, width)
    gate = pl.BlockSpec((heads, LANES, LANES), lambda c: (c, 0, 0))
    return call(
        functools.partial(gates_back_kernel, groups, length),
        (recur // width,),
        [
            block, block, block, pl.BlockSpec((groups, length + 3 * SUB, width), lambda c: (0, 0, c)),
            block, block, seg, seg, columns(groups, width), columns(groups, width),
            gate, gate, columns(8, width), whole(masks.shape),
        ],
        [block, seg, gate, gate, columns(8, width)],
        [
            struct((rows, recur), F32), struct((SUB * groups, recur), F32), struct(gate_a.shape, F32),
            struct(gate_a.shape, F32), struct((8, recur), F32),
        ],
        [
            pltpu.VMEM((rows, width), F32), pltpu.VMEM((rows, width), BF16),
            pltpu.VMEM((rows, width), BF16), pltpu.VMEM((rows, width), BF16),
        ],
        rows * recur * 128 * 8 * 4,
        rows * recur * 28,
        (local, keep, hidden, ext, rate, igate, sege, segf, gin, hin, gate_a, gate_i, vec, masks),
    )


def branch_back_kernel(dbranch_ref, w_ref, out_ref):
    part = nt_dot(dbranch_ref[...], w_ref[...])

    @pl.when(pl.program_id(0) == 0)
    def _():
        out_ref[...] = part

    @pl.when(pl.program_id(0) > 0)
    def _():
        out_ref[...] += part


def branch_back(dbranch, w_in, first, dim):
    rows, recur = dbranch.shape
    width = 512
    return call(
        branch_back_kernel,
        (recur // width,),
        [columns(rows, width), columns(dim, width, first // width)],
        whole((rows, dim)),
        struct((rows, dim), F32),
        [],
        2 * rows * dim * recur,
        dim * recur * 2,
        (dbranch, w_in),
    )


def recur_in_back_kernel(
    groups, length,
    part_ref, din_ref, back_ref, wi_ref, x_ref, gain_ref, dmid_ref,
    low_ref, dx_ref, dgain_ref,
    acc,
):
    c = pl.program_id(0)
    width = din_ref.shape[1]
    rim = 4 * SUB
    sub = lax.broadcasted_iota(jnp.int32, (SUB, width), 0)
    for g in range(groups):
        base = g * length
        if length > rim:
            low_ref[base : base + length - rim, :] = din_ref[base : base + length - rim, :].astype(BF16)
        extra = [jnp.zeros((SUB, width), F32)]
        for i in range(3):
            extra.append(jnp.where(sub == SUB - 1, back_ref[g * SUB + i : g * SUB + i + 1, :], 0.0))
        tail = slice(base + length - rim, base + length)
        low_ref[tail, :] = (din_ref[tail, :] + jnp.concatenate(extra, axis=0)).astype(BF16)
    part = nt_dot(low_ref[...], wi_ref[...])

    @pl.when(c == 0)
    def _():
        acc[...] = part_ref[...] + part

    @pl.when(c > 0)
    def _():
        acc[...] += part

    @pl.when(c == pl.num_programs(0) - 1)
    def _():
        back, dgain = norm_back(x_ref[...].astype(F32), gain_ref[...], acc[...])
        dx_ref[...] = (dmid_ref[...] + back).astype(BF16)
        dgain_ref[...] = dgain


def recur_in_back(part, din, back, w_in, first, x, gain, dmid, groups, length):
    rows, dim = x.shape
    recur = din.shape[1]
    width = 512
    block = columns(rows, width)
    full = whole((rows, dim))
    return call(
        functools.partial(recur_in_back_kernel, groups, length),
        (recur // width,),
        [
            full, block, columns(SUB * groups, width), columns(dim, width, (first + recur) // width),
            full, whole(gain.shape), full,
        ],
        [block, full, whole((1, dim))],
        [struct((rows, recur), BF16), struct((rows, dim), BF16), struct((1, dim), F32)],
        [pltpu.VMEM((rows, dim), F32)],
        2 * rows * dim * recur * 1.5,
        2 * dim * recur + rows * recur * 8,
        (part, din, back, w_in, x, gain, dmid),
    )


def outer_kernel(places, pieces, place_ref, left_a, left_b, right_a, right_b, *refs):
    outs, (keep, send) = refs[:-2], refs[-2:]
    n, fs, share = places
    rows = left_a.shape[1]
    c = pl.program_id(0)
    per = pl.num_programs(0) // pieces

    @pl.when(c == 0)
    def _():
        core, y = place_ref[0], place_ref[1]
        for at in range(n):
            there = slice(at * share, (at + 1) * share)
            for scratch, side in ((keep, y), (send, 1 - y)):
                first = pl.multiple_of((at * fs + 2 * side + core) * share, share)
                scratch[there, 0:rows] = left_a[pl.ds(first, share), :]
                scratch[there, rows : 2 * rows] = left_b[pl.ds(first, share), :]

    right = jnp.concatenate([right_a[0], right_b[0]], axis=0)
    to_keep = nn_dot(keep[...], right).astype(BF16)
    to_send = nn_dot(send[...], right).astype(BF16)
    for p in range(pieces):

        @pl.when(c // per == p)
        def _(p=p):
            outs[2 * p][...] = to_keep
            outs[2 * p + 1][...] = to_send


def outer(lefts, at, k, rights, pieces, chosen, place, n, fs):
    rows = lefts[0].shape[1]
    count, _, total = rights[0].shape
    share = k // (n * fs)
    piece = count * total // pieces
    width = next(w for w in (768, 512, 384, 256, 128, piece) if piece % w == 0)
    across, per = total // width, piece // width
    skipped, pieces = chosen[0] * per, chosen[1]

    def out_block(p):
        return pl.BlockSpec((n * share, width), lambda c, place: (0, jnp.clip(c - p * per, 0, per - 1)))

    left = pl.BlockSpec((k, rows), lambda c, place: (at // k, 0))
    right = pl.BlockSpec((1, rows, width), lambda c, place: ((c + skipped) // across, 0, (c + skipped) % across))
    outs = pl.pallas_call(
        functools.partial(outer_kernel, (n, fs, share), pieces),
        grid_spec=pltpu.PrefetchScalarGridSpec(
            num_scalar_prefetch=1,
            grid=(pieces * per,),
            in_specs=[left, left, right, right],
            out_specs=[out_block(p) for p in range(pieces) for _ in range(2)],
            scratch_shapes=[pltpu.VMEM((n * share, 2 * rows), BF16)] * 2,
        ),
        out_shape=[struct((n * share, piece), BF16)] * (2 * pieces),
        compiler_params=pltpu.CompilerParams(dimension_semantics=("arbitrary",), vmem_limit_bytes=VMEM_BYTES),
        cost_estimate=pl.CostEstimate(
            flops=8 * n * share * rows * pieces * piece // COST, bytes_accessed=1, transcendentals=0
        ),
    )(place, *lefts, *rights)
    return [(outs[2 * p], outs[2 * p + 1]) for p in range(pieces)]


def unfold_kernel(folded_ref, out_ref):
    height, width = folded_ref.shape[0], out_ref.shape[1]
    for q in range(out_ref.shape[0] // height):
        out_ref[q * height : (q + 1) * height, :] = folded_ref[:, q * width : (q + 1) * width]


def unfold_first(packed, places, height, rows, width):
    return call(
        unfold_kernel,
        (places,),
        [pl.BlockSpec((height, rows // height * width), lambda c: (c, 0))],
        pl.BlockSpec((rows, width), lambda c: (c, 0)),
        struct((places * rows, width), packed.dtype),
        [],
        0,
        places * rows * width * 4,
        (packed,),
    )


def shifted(value, axis, by):
    length = lax.axis_size(axis)
    pairs = [(i, i + by) for i in range(length) if 0 <= i + by < length]
    return lax.ppermute(value, axis, pairs)


def entering(agg, groups, reverse):
    n = lax.axis_size("seq")
    sign = -1 if reverse else 1
    got = {k: shifted(agg, "seq", sign * k) for k in range(1, n)}
    state = jnp.zeros((groups, agg.shape[1]), F32)
    for k in range(n - 1, 0, -1):
        part = got[k].reshape(groups, 2, -1)
        state = part[:, 0] * state + part[:, 1]
    return state


def add(*parts):
    return functools.reduce(jnp.add, [p.astype(F32) for p in parts])


def line_sum(slots, mine, n, send):
    def at(offset):
        return slots((mine + offset) % n)

    up, down = at(n - 1), at(1)
    for s in range(1, n):
        got_up = send(up, [(i, i + 1) for i in range(s)])
        got_down = send(down, [(i, i - 1) for i in range(n - s, n)])
        if s < n - 1:
            up = add(at(n - 1 - s), got_up).astype(BF16)
            down = add(at(s + 1), got_down).astype(BF16)
    return add(at(0), got_up, got_down)


class Scatter:
    def __init__(self):
        self.n, self.fs = lax.axis_size("seq"), lax.axis_size("fsdp")
        self.ny = self.fs // 2
        self.z, f = lax.axis_index("seq"), lax.axis_index("fsdp")
        self.y, self.core = f // 2, f % 2

    def core_swap(self, value):
        return lax.ppermute(value, "fsdp", [(i, i ^ 1) for i in range(self.fs)])

    def y_send(self, value, pairs):
        return lax.ppermute(value, "fsdp", [(2 * a + c, 2 * b + c) for a, b in pairs for c in range(2)])

    def over_y(self, keep, send, since, beside):
        return add(after(keep, beside), self.y_send(after(send, since), [(0, 1), (1, 0)])).astype(BF16)

    def over_z(self, shares):
        return lax.psum_scatter(shares, "seq", scatter_dimension=0, tiled=True)[0].astype(F32)


def pick(value, index, axis):
    return lax.dynamic_index_in_dim(value, index, axis, keepdims=False)


def reorder(v):
    length, d = v.shape[-2:]
    return jnp.swapaxes(v.reshape(-1, SUB, length // SUB, d), 1, 2).reshape(-1, d)


def restore(v, shape):
    length, d = shape[-2:]
    return jnp.swapaxes(v.reshape(-1, length // SUB, SUB, d), 1, 2).reshape(shape)


def tail_rows(v, groups, length):
    d = v.shape[1]
    last = v.reshape(groups, length // SUB, SUB, d)[:, length // SUB - 3 :, SUB - 1]
    last = jnp.pad(last, ((0, 0), (0, SUB - 3), (0, 0))).reshape(groups * SUB, d)
    return jnp.pad(last, ((0, -groups * SUB % 16), (0, 0)))


def fold_rows(v, height):
    count = -(-v.shape[0] // height)
    v = jnp.pad(v, ((0, count * height - v.shape[0]), (0, 0)))
    return jnp.concatenate([v[i * height : (i + 1) * height] for i in range(count)], axis=1)


def fold_places(v, height):
    places, rows, width = v.shape
    count = -(-rows // height)
    v = jnp.pad(v, ((0, 0), (0, count * height - rows), (0, 0))).reshape(places, count, height, width)
    return jnp.swapaxes(v, 1, 2).reshape(places, height, count * width)


def unfold_rows(v, rows, width):
    places, height, total = v.shape
    v = jnp.swapaxes(v.reshape(places, height, total // width, width), 1, 2)
    return v.reshape(places, -1, width)[:, :rows]


def after(value, *others):
    return lax.optimization_barrier((value, others))[0]


def gather(shard):
    return lax.all_gather(shard, ("seq", "fsdp"), axis=0, tiled=True)


def body(
    ends, segment_ids, norm_one, w_branch, w_input, conv_weight, conv_bias, gate_a, gate_i, bias_a, bias_i,
    decay, w_out, norm_two, w_gate, w_up, w_down,
):
    is_first = lax.axis_index("section") == 0
    z = lax.axis_index("seq")
    n, fs = lax.axis_size("seq"), lax.axis_size("fsdp")
    places = n * fs
    micro, seqs, length, dim = ends.shape[1:]
    parts_of = 1
    groups = micro * seqs // parts_of
    rows = groups * length
    recur = w_branch.shape[2]
    heads, part, block = gate_a.shape[1:]
    hidden_dim = w_gate.shape[2]

    dshare, rshare = dim // places, recur // places
    vectors = [norm_one, norm_two] + [conv_weight[:, k] for k in range(CONV)] + [conv_bias, bias_a, bias_i, decay]
    vectors = jnp.concatenate([jnp.pad(v, ((0, 0), (0, LANES - v.shape[1]))) for v in vectors], axis=0)
    vectors = jnp.pad(vectors, ((0, 2 * SUB - vectors.shape[0]), (0, 0)))
    small = jnp.concatenate([vectors, gate_a.reshape(-1, block), gate_i.reshape(-1, block)], axis=0)
    small_rows = small.shape[0]
    small = fold_rows(small, dshare)
    first = hidden_dim
    w_in = gather(
        jnp.concatenate(
            [fold_rows(w_down[0], dshare), w_branch[0], w_input[0], w_out[0].reshape(dshare, recur), small], axis=1
        )
    )
    w_gu = gather(jnp.concatenate([after(w_gate[0], small), w_up[0]], axis=1))
    w_out_all = w_in[:, first + 2 * recur : first + 3 * recur].reshape(recur, dim)
    small = unfold_rows(w_in[:, first + 3 * recur :].reshape(places, dshare, -1), small_rows, LANES)
    hshare = hidden_dim // places
    if dshare % 16 == 0:
        w_down_all = unfold_first(w_in, places, dshare, hshare, dim)
    else:
        w_down_all = unfold_rows(w_in[:, :first].reshape(places, dshare, -1), hshare, dim).reshape(hidden_dim, dim)

    def vector(row, share):
        return small[:, row, :share].reshape(1, places * share).astype(F32)

    gain_one, gain_two = vector(0, dshare), vector(1, dshare)
    decays = vector(9, rshare)
    vec = jnp.concatenate([vector(r, rshare) for r in range(2, 9)] + [-8.0 * jax.nn.softplus(decays)], axis=0)
    gates_a, gates_i = [
        jnp.swapaxes(small[:, r : r + heads * part].reshape(places, heads, part, block), 0, 1).reshape(heads, block, block)
        for r in (2 * SUB, 2 * SUB + heads * part)
    ]

    padded_ids = jnp.pad(segment_ids, ((0, 0), (0, 0), (CONV - 1, 0)), constant_values=-1)
    window = lax.dynamic_slice_in_dim(padded_ids, z * length, length + CONV - 1, axis=2)
    current = window[:, :, CONV - 1 :]
    masks = jnp.stack(
        [window[:, :, CONV - 1 - k : CONV - 1 - k + length] == current for k in (1, 1, 2, 3)]
    ).astype(F32)
    masks = jnp.swapaxes(masks.reshape(4, parts_of, groups, SUB, length // SUB), 3, 4).reshape(4, parts_of, rows, 1)
    masks = jnp.broadcast_to(masks, (4, parts_of, rows, LANES))
    masks = [masks[:, m] for m in range(parts_of)]
    micros = range(parts_of)

    def forward(xs, halos, save):
        got = []
        for m in micros:
            got.append(recur_in(xs[m], halos[m], gain_one, w_in, first, gates_a, gates_i, vec, masks[m], groups, length))
        hin = entering(jnp.concatenate([g[7] for g in got], axis=0), parts_of * groups, False)
        acts = [branch_in(after(g[0], got[-1][7]), w_in, first, recur) for g in got]
        outs, saved = [], []
        for m in micros:
            normed, ext, rate, igate, keep, local, segp, _ = got[m]
            act, slope = acts[m]
            mine = hin[m * groups : (m + 1) * groups]
            if m:
                keep = after(keep, outs[-1])
            hidden, mixed, middle, normed_two = recur_out(
                xs[m], keep, local, act, segp, mine, w_out_all, gain_two, groups, length
            )
            results = feed_forward(normed_two, middle, w_gu, w_down_all, save)
            outs.append(results[-1])
            saved.append(
                (normed, ext, rate, igate, keep, mine, hidden, mixed, middle, normed_two, act, slope) + tuple(results[:-1])
            )
        return outs, saved

    def back_ff(m, dout, saved):
        return feed_forward_back(dout, saved[m][8], gain_two, saved[m][12], saved[m][13], w_gu, w_down_all)

    def back_mix(m, low, saved):
        return mix_back(low, w_out_all, saved[m][10], saved[m][11], saved[m][6], saved[m][4], groups, length)

    def back_gates(m, mixed_back, gin, saved):
        normed, ext, rate, igate, keep, hin, hidden = saved[m][:7]
        _, local, sege, segf, _ = mixed_back
        din, head, dga, dgi, dvec = gates_back(
            local, keep, hidden, ext, rate, igate, sege, segf, gin[m * groups : (m + 1) * groups], hin,
            gates_a, gates_i, vec, masks[m], groups, length,
        )
        return din, shifted(head, "seq", -1), dga, dgi, dvec

    def back_in(m, part, gates, dmid, xs):
        return recur_in_back(part, gates[0], gates[1], w_in, first, xs[m], gain_one, dmid, groups, length)

    own = [reorder(v) for v in ends[0].reshape((parts_of, -1) + ends.shape[3:])]
    tails = [shifted(tail_rows(v, groups, length), "seq", 1) for v in own]
    outs, _ = forward(own, tails, False)
    xs, halos = [], []
    for m in micros:
        received = shifted(outs[m], "section", 1)
        received_halo = lax.ppermute(
            tail_rows(outs[m], groups, length), ("section", "seq"), [(i, n + i + 1) for i in range(n - 1)]
        )
        xs.append(jnp.where(is_first, own[m], received))
        halos.append(jnp.where(is_first, tails[m], received_halo))
    outs, saved = forward(xs, halos, True)

    scatter = Scatter()
    swap = scatter.core_swap
    place = jnp.stack([scatter.core, scatter.y]).astype(jnp.int32)

    ff = back_ff(0, own[0], saved)
    mix = back_mix(0, ff[2], saved)
    gin = entering(mix[4], groups, True)
    product_t = after(saved[0][14], mix[4]).T
    product_pair = (product_t, swap(product_t))
    gates = back_gates(0, after(mix, product_t), gin, saved)
    base = branch_back(after(mix[0], gates[0]), w_in, first, dim)
    dx = back_in(0, base, gates, ff[1], xs)[1]
    others = [after(saved[0][i], dx) for i in (9, 0, 7)]
    starts_at, total_rows = [], 0
    for i, v in enumerate(others):
        gap = -total_rows % v.shape[1]
        if gap:
            others[i] = jnp.concatenate([jnp.zeros((rows, gap), BF16), v], axis=1)
        starts_at.append((total_rows + gap, v.shape[1]))
        total_rows += gap + v.shape[1]
    others = jnp.concatenate([v.T for v in others], axis=0)
    received = after(shifted(dx, "section", -1), others, product_pair)
    others = after(others, received)
    others = (others, swap(others))
    lefts = {"product": (product_pair, 0, hidden_dim)}
    for name, (at, k) in zip(("two", "one", "mixed"), starts_at):
        lefts[name] = (others, at, k)
    dout = jnp.where(is_first, received, own[0])

    def pair(value):
        value = value if value.ndim == 3 else value[None]
        return value, swap(value)

    def products(name, rights, pieces=1, chosen=None):
        both, at, k = lefts[name]
        chosen = chosen or (0, pieces)
        if scatter.ny == 2:
            return outer(both, at, k, rights, pieces, chosen, place, n, fs)
        left = jnp.concatenate([v[at : at + k] for v in both], axis=1)
        right = jnp.concatenate([jnp.concatenate(list(v), axis=1) for v in rights], axis=0)
        grad = nn_dot(left, right).astype(BF16)
        grad = pick(grad.reshape(n, scatter.ny, 2, -1, grad.shape[1]), scatter.core, 2)
        return [(p,) for p in jnp.split(grad, pieces, axis=3)[chosen[0] : sum(chosen)]]

    def over_y(grads, since, *beside):
        if scatter.ny == 2:
            return scatter.over_y(*[g.reshape(n, -1, g.shape[1]) for g in grads], since, beside)
        (grad,) = grads
        return line_sum(lambda d: pick(grad, d, 1), scatter.y, scatter.ny, scatter.y_send).astype(BF16)

    down = products("product", pair(dout), 2)
    dgu, dmid, out_low, dgain_two = back_ff(0, after(dout, down), saved)
    down_sums = [over_y(down[0], (), out_low)]
    down_sums.append(None)
    gu_pair = pair(after(dgu, down_sums[0]))
    mix = back_mix(0, after(out_low, down_sums[0]), saved)
    gate_up = products("two", after(gu_pair, mix[0]), 4, (0, 1))
    down_sums[1] = over_y(down[1], out_low, gate_up[0])
    gin = entering(after(mix[4], down_sums[1]), groups, True)
    gate_up += products("two", after(gu_pair, down_sums[1]), 4, (1, 3))
    gate_up_sums = [over_y(gate_up[0], (), gate_up[1], gin)]
    gates = back_gates(0, after(mix, gate_up_sums[0]), gin, saved)
    gate_up_sums.append(over_y(gate_up[1], gin, gates[0]))
    out_low, dbranch, gates = after((out_low, mix[0], gates), gate_up_sums[1])
    out_pair, branch_pair = pair(out_low), pair(dbranch)
    base = branch_back(dbranch, w_in, first, dim)
    results = back_in(0, base, gates, dmid, xs)
    gate_up_sums.append(over_y(gate_up[2], gates[0], results[1], out_pair[1], branch_pair[1]))
    input_pair = pair(after(results[0], gate_up_sums[2]))
    out = products("mixed", after(out_pair, gate_up_sums[2]))
    branch = products("one", after(branch_pair, out))
    dgain_one = results[2]
    dga, dgi, dvec = gates[2:5]
    ddecay = -8.0 * jax.nn.sigmoid(decays) * dvec[7:8]
    shares = [dgain_one, dgain_two] + [dvec[k : k + 1] for k in range(7)] + [ddecay]
    shares = [v.reshape(places, 1, -1) for v in shares]
    shares = [jnp.pad(v, ((0, 0), (0, 0), (0, LANES - v.shape[2]))) for v in shares]
    shares = jnp.pad(jnp.concatenate(shares, axis=1), ((0, 0), (0, 2 * SUB - len(shares)), (0, 0)))
    packed = jnp.concatenate(
        [shares]
        + [jnp.swapaxes(v.reshape(heads, places, part, block), 0, 1).reshape(places, -1, block) for v in (dga, dgi)],
        axis=1,
    )
    extra = fold_places(packed, dshare).reshape(n, scatter.ny, 2, dshare, -1)
    theirs = swap(pick(extra, 1 - scatter.core, 2).astype(BF16))
    extra = add(pick(extra, scatter.core, 2), theirs).astype(BF16)
    gate_up_sums.append(over_y(gate_up[3], results[1], branch, extra))
    into = products("one", after(input_pair, gate_up_sums[3]))
    out_sum = over_y(out[0], branch, into)
    if scatter.ny == 2:
        sides = (pick(extra, scatter.y, 1), pick(extra, 1 - scatter.y, 1))
        last = [
            jnp.concatenate([g.reshape(n, dshare, -1), v], axis=2).reshape(n * dshare, -1) for g, v in zip(into[0], sides)
        ]
    else:
        last = (jnp.concatenate([into[0][0], extra], axis=3),)
    branch_sum = over_y(branch[0], last)
    input_sum = over_y(last, out_sum)

    outputs = restore(outs[0], ends.shape)
    input_grads = restore(results[1], ends.shape)
    shares = down_sums + gate_up_sums + [out_sum, branch_sum, input_sum]
    for i in range(1, len(shares)):
        shares[i] = after(shares[i], shares[i - 1])
    totals = [scatter.over_z(v) for v in shares]
    sum_down, sum_gate, sum_up = [jnp.concatenate(totals[i : i + 2], axis=1) for i in (0, 2, 4)]
    sum_out, sum_branch, sum_input = totals[6:]
    sum_input, sums = sum_input[:, :recur], sum_input[:, recur:]
    sums = unfold_rows(sums[None], small_rows, LANES)[0]
    gate_sums = [sums[r : r + heads * part].reshape(gate_a.shape) for r in (2 * SUB, 2 * SUB + heads * part)]

    return (
        outputs,
        input_grads,
        sums[0:1, :dshare],
        sum_branch[None],
        sum_input[None],
        sums[2 : 2 + CONV, :rshare][None],
        sums[6:7, :rshare],
        gate_sums[0],
        gate_sums[1],
        sums[7:8, :rshare],
        sums[8:9, :rshare],
        sums[9:10, :rshare],
        sum_out[None],
        sums[1:2, :dshare],
        sum_gate[None],
        sum_up[None],
        sum_down[None],
    )


def solution(mesh):
    tokens = P("section", None, "fsdp", "seq", None)
    vector = P("section", ("seq", "fsdp"))
    matrix = P("section", ("seq", "fsdp"), None)
    taps = P("section", None, ("seq", "fsdp"))
    gates = P("section", None, ("seq", "fsdp"), None)
    weights = (
        vector, matrix, matrix, taps, vector, gates, gates, vector, vector, vector, matrix, vector, matrix, matrix, matrix,
    )
    return jax.shard_map(
        body,
        mesh=mesh,
        in_specs=(tokens, P(None, "fsdp", None)) + weights,
        out_specs=(tokens, tokens) + weights,
        check_vma=False,
    )
```

```python
import functools

import jax
import jax.numpy as jnp
from jax import lax
from jax.experimental import pallas as pl
from jax.experimental.pallas import tpu as pltpu
from jax.sharding import PartitionSpec as P

CONV = 4
EPS = 1e-06
F32 = jnp.float32
BF16 = jnp.bfloat16
VMEM_BYTES = 56 << 20
LANES = 128
SUB = 8
COST = 4


def nn_dot(a, b):
    return lax.dot_general(a, b, (((1,), (0,)), ((), ())), preferred_element_type=F32)


def nt_dot(a, b):
    return lax.dot_general(a, b, (((1,), (1,)), ((), ())), preferred_element_type=F32)


def tn_dot(a, b):
    return lax.dot_general(a, b, (((0,), (0,)), ((), ())), preferred_element_type=F32)


def sigmoid(v):
    return 0.5 * jnp.tanh(0.5 * v) + 0.5


K0 = 0.7978845608028654
K1 = 0.044715


def gelu(v):
    return 0.5 * v * (1.0 + jnp.tanh(K0 * (v + K1 * v * v * v)))


def gelu_both(v):
    square = v * v
    t = jnp.tanh(K0 * v * (1.0 + K1 * square))
    half = 0.5 * (1.0 + t)
    slope = half + (0.5 * K0) * v * (1.0 - t * t) * (1.0 + (3.0 * K1) * square)
    return v * half, slope


def lanes(mask, width):
    return jnp.concatenate([mask] * (width // LANES), axis=1) if width > LANES else mask


def call(kernel, grid, in_specs, out_specs, out_shape, scratch, flops, bytes_accessed, args):
    return pl.pallas_call(
        kernel,
        grid=grid,
        in_specs=in_specs,
        out_specs=out_specs,
        out_shape=out_shape,
        scratch_shapes=scratch,
        compiler_params=pltpu.CompilerParams(
            dimension_semantics=("arbitrary",) * len(grid), vmem_limit_bytes=VMEM_BYTES
        ),
        cost_estimate=pl.CostEstimate(
            flops=int(flops) // COST, bytes_accessed=int(bytes_accessed) // COST, transcendentals=0
        ),
    )(*args)


def whole(shape):
    return pl.BlockSpec(shape, lambda c: (0,) * len(shape))


def columns(rows, width, offset=0):
    return pl.BlockSpec((rows, width), lambda c: (0, c + offset))


def struct(shape, dtype):
    return jax.ShapeDtypeStruct(shape, dtype)


def recur_in_kernel(
    groups, length,
    x_ref, halo_ref, gain_ref, wi_ref, ga_ref, gi_ref, vec_ref, mask_ref,
    normed_ref, ext_ref, rate_ref, igate_ref, keep_ref, local_ref, segp_ref, agg_ref,
    xn, conv, pre_a, pre_i,
):
    rows = groups * length
    steps = length // SUB
    width = wi_ref.shape[1]

    @pl.when(pl.program_id(0) == 0)
    def _():
        gain = gain_ref[...]
        for at, ref in ((0, x_ref), (rows, halo_ref)):
            v = ref[...].astype(F32)
            r = lax.rsqrt(jnp.mean(v * v, axis=-1, keepdims=True) + EPS)
            xn[at : at + ref.shape[0], :] = (v * r * gain).astype(BF16)
        normed_ref[...] = xn[0:rows, :]

    conv_in = nn_dot(xn[...], wi_ref[...]).astype(BF16).astype(F32)
    sub = lax.broadcasted_iota(jnp.int32, (SUB, width), 0)
    for g in range(groups):
        base = conv_in[g * length : (g + 1) * length]
        halo = conv_in[rows + g * SUB : rows + (g + 1) * SUB]
        for k in (3, 2, 1):
            block = pltpu.roll(base[(steps - k) * SUB : (steps - k + 1) * SUB], 1, 0)
            ext_ref[g, (3 - k) * SUB : (4 - k) * SUB, :] = jnp.where(sub == 0, halo[3 - k : 4 - k], block)
        ext_ref[g, 3 * SUB : 3 * SUB + length, :] = base
    taps = [vec_ref[k : k + 1, :] for k in range(CONV)]
    for g in range(groups):
        part = slice(g * length, (g + 1) * length)
        out = vec_ref[4:5, :] + taps[0] * ext_ref[g, 3 * SUB : 3 * SUB + length, :]
        for k in range(1, CONV):
            link = lanes(mask_ref[k, part, :], width)
            out = out + taps[k] * (link * ext_ref[g, (3 - k) * SUB : (3 - k) * SUB + length, :])
        conv[part, :] = out
    rounded = conv[...].astype(BF16)
    for h in range(width // LANES):
        col = slice(h * LANES, (h + 1) * LANES)
        pre_a[:, col] = nn_dot(rounded[:, col], ga_ref[h])
        pre_i[:, col] = nn_dot(rounded[:, col], gi_ref[h])
    bias_a, bias_i, scale = vec_ref[5:6, :], vec_ref[6:7, :], vec_ref[7:8, :]
    chunk = 4

    def step(i, carry):
        out = []
        for g in range(groups):
            h, p = carry[g]
            at = pl.multiple_of(g * length + i * (chunk * SUB), chunk * SUB)
            here = pl.ds(at, chunk * SUB)
            rate = sigmoid(pre_a[here, :] + bias_a)
            igate = sigmoid(pre_i[here, :] + bias_i)
            keep = jnp.exp(scale * rate) * lanes(mask_ref[0, here, :], width)
            driven = igate * conv[here, :] * jnp.sqrt(1.0 + 0.0001 - keep * keep)
            rate_ref[here, :] = rate
            igate_ref[here, :] = igate
            keep_ref[here, :] = keep
            states = []
            for q in range(chunk):
                kq = keep[q * SUB : (q + 1) * SUB]
                h = kq * h + driven[q * SUB : (q + 1) * SUB]
                p = kq * p
                states.append(h)
            local_ref[here, :] = jnp.concatenate(states, axis=0)
            out.append((h, p))
        return tuple(out)

    start = tuple((jnp.zeros((SUB, width), F32), jnp.ones((SUB, width), F32)) for _ in range(groups))
    done = lax.fori_loop(0, steps // chunk, step, start)
    for g in range(groups):
        h, p = done[g]
        segp_ref[g * SUB : (g + 1) * SUB, :] = p
        a, b = jnp.ones((1, width), F32), jnp.zeros((1, width), F32)
        for s in range(SUB):
            b = p[s : s + 1] * b + h[s : s + 1]
            a = p[s : s + 1] * a
        agg_ref[2 * g : 2 * g + 1, :] = a
        agg_ref[2 * g + 1 : 2 * g + 2, :] = b


def recur_in(x, halo, gain, w_in, first, gate_a, gate_i, vec, masks, groups, length):
    rows, dim = x.shape
    recur = vec.shape[1]
    width = 512
    blocks = recur // width
    block_f32 = columns(rows, width)
    heads = width // LANES
    ext_len = length + 3 * SUB
    return call(
        functools.partial(recur_in_kernel, groups, length),
        (blocks,),
        [
            whole(x.shape), whole(halo.shape), whole(gain.shape),
            columns(dim, width, (first + recur) // width),
            pl.BlockSpec((heads, LANES, LANES), lambda c: (c, 0, 0)),
            pl.BlockSpec((heads, LANES, LANES), lambda c: (c, 0, 0)),
            columns(8, width), whole(masks.shape),
        ],
        [
            whole((rows, dim)),
            pl.BlockSpec((groups, ext_len, width), lambda c: (0, 0, c)),
            block_f32, block_f32, block_f32, block_f32,
            columns(SUB * groups, width), columns(2 * groups, width),
        ],
        [
            struct((rows, dim), BF16), struct((groups, ext_len, recur), F32),
            struct((rows, recur), F32), struct((rows, recur), F32), struct((rows, recur), F32),
            struct((rows, recur), F32), struct((SUB * groups, recur), F32), struct((2 * groups, recur), F32),
        ],
        [
            pltpu.VMEM((rows + halo.shape[0], dim), BF16), pltpu.VMEM((rows, width), F32),
            pltpu.VMEM((rows, width), F32), pltpu.VMEM((rows, width), F32),
        ],
        2 * rows * dim * recur * 2.5,
        dim * recur * 2 + rows * recur * 4 * 5,
        (x, halo, gain, w_in, gate_a, gate_i, vec, masks),
    )


def branch_kernel(x_ref, w_ref, act_ref, slope_ref):
    act, slope = gelu_both(nn_dot(x_ref[...], w_ref[...]))
    act_ref[...] = act
    slope_ref[...] = slope


def branch_in(x, w_in, first, recur):
    rows, dim = x.shape
    width = 512
    block = columns(rows, width)
    return call(
        branch_kernel,
        (recur // width,),
        [whole(x.shape), columns(dim, width, first // width)],
        [block, block],
        [struct((rows, recur), F32)] * 2,
        [],
        2 * rows * dim * recur * 1.5,
        dim * recur * 2 + rows * recur * 8,
        (x, w_in),
    )


def recur_out_kernel(
    groups, length,
    x_ref, keep_ref, local_ref, act_ref, segp_ref, hin_ref, wo_ref, gain_ref,
    hidden_ref, mixed_ref, middle_ref, normed_ref,
    acc,
):
    steps = length // SUB
    width = keep_ref.shape[1]
    chunk = 4
    c = pl.program_id(0)
    start = []
    for g in range(groups):
        ends = local_ref[(g + 1) * length - SUB : (g + 1) * length, :]
        prods = segp_ref[g * SUB : (g + 1) * SUB, :]
        state = hin_ref[g : g + 1, :]
        entering = []
        for s in range(SUB):
            entering.append(state)
            state = prods[s : s + 1] * state + ends[s : s + 1]
        start.append(jnp.concatenate(entering, axis=0))

    def step(i, carry):
        out = []
        for g in range(groups):
            q = carry[g]
            at = pl.multiple_of(g * length + i * (chunk * SUB), chunk * SUB)
            here = pl.ds(at, chunk * SUB)
            keep = keep_ref[here, :]
            moved = []
            for r in range(chunk):
                q = keep[r * SUB : (r + 1) * SUB] * q
                moved.append(q)
            hidden = local_ref[here, :] + jnp.concatenate(moved, axis=0)
            hidden_ref[here, :] = hidden
            mixed_ref[here, :] = (hidden * act_ref[here, :]).astype(BF16)
            out.append(q)
        return tuple(out)

    lax.fori_loop(0, steps // chunk, step, tuple(start))
    part = nn_dot(mixed_ref[...], wo_ref[...])

    @pl.when(c == 0)
    def _():
        acc[...] = x_ref[...].astype(F32) + part

    @pl.when(c > 0)
    def _():
        acc[...] += part

    @pl.when(c == pl.num_programs(0) - 1)
    def _():
        m = acc[...]
        middle_ref[...] = m
        r = lax.rsqrt(jnp.mean(m * m, axis=-1, keepdims=True) + EPS)
        normed_ref[...] = (m * r * gain_ref[...]).astype(BF16)


def recur_out(x, keep, local, act, segp, hin, w_out, gain, groups, length):
    rows, dim = x.shape
    recur = keep.shape[1]
    width = 512
    block = columns(rows, width)
    return call(
        functools.partial(recur_out_kernel, groups, length),
        (recur // width,),
        [
            whole(x.shape), block, block, block, columns(SUB * groups, width), columns(groups, width),
            pl.BlockSpec((width, dim), lambda c: (c, 0)), whole(gain.shape),
        ],
        [block, block, whole((rows, dim)), whole((rows, dim))],
        [
            struct((rows, recur), F32), struct((rows, recur), BF16),
            struct((rows, dim), F32), struct((rows, dim), BF16),
        ],
        [pltpu.VMEM((rows, dim), F32)],
        2 * rows * dim * recur * 1.5,
        dim * recur * 2 + rows * recur * 18,
        (x, keep, local, act, segp, hin, w_out, gain),
    )


def ff_kernel(save, x_ref, mid_ref, wg_ref, wu_ref, wd_ref, *refs):
    c = pl.program_id(0)
    out_ref, acc = refs[-2:]
    x = x_ref[...]
    gate = nn_dot(x, wg_ref[...])
    up = nn_dot(x, wu_ref[...])
    if save:
        act_ref, slope_ref, product_ref = refs[:3]
        act, slope = gelu_both(gate)
        act_ref[...] = act.astype(BF16)
        slope_ref[...] = (up * slope).astype(BF16)
        product = (act * up).astype(BF16)
        product_ref[...] = product
    else:
        product = (gelu(gate) * up).astype(BF16)
    part = nn_dot(product, wd_ref[...])

    @pl.when(c == 0)
    def _():
        acc[...] = mid_ref[...] + part

    @pl.when(c > 0)
    def _():
        acc[...] += part

    @pl.when(c == pl.num_programs(0) - 1)
    def _():
        out_ref[...] = acc[...].astype(BF16)


def feed_forward(x, middle, w_gu, w_down, save):
    rows, dim = x.shape
    hidden = w_down.shape[0]
    width = 512
    blocks = hidden // width
    block = columns(rows, width)
    kept = 3 if save else 0
    return call(
        functools.partial(ff_kernel, save),
        (blocks,),
        [
            whole(x.shape), whole(middle.shape), columns(dim, width), columns(dim, width, blocks),
            pl.BlockSpec((width, dim), lambda c: (c, 0)),
        ],
        [block] * kept + [whole((rows, dim))],
        [struct((rows, hidden), BF16)] * kept + [struct((rows, dim), BF16)],
        [pltpu.VMEM((rows, dim), F32)],
        6 * rows * dim * hidden * 1.5,
        6 * dim * hidden,
        (x, middle, w_gu, w_gu, w_down),
    )


def norm_back(values, gain, grad):
    q = lax.rsqrt(jnp.mean(values * values, axis=-1, keepdims=True) + EPS)
    t = gain * grad
    back = q * t - values * (q * q * q * jnp.mean(values * t, axis=-1, keepdims=True))
    return back, jnp.sum(values * q * grad, axis=0, keepdims=True)


def down_back_kernel(dout_ref, wd_ref, dproduct_ref):
    dproduct_ref[...] = nt_dot(dout_ref[...], wd_ref[...]).astype(BF16)


def down_back(dout, w_down):
    rows, dim = dout.shape
    hidden = w_down.shape[0]
    width = 512
    return call(
        down_back_kernel,
        (hidden // width,),
        [whole((rows, dim)), pl.BlockSpec((width, dim), lambda c: (c, 0))],
        columns(rows, width),
        struct((rows, hidden), BF16),
        [],
        2 * rows * dim * hidden,
        2 * dim * hidden + 4 * rows * hidden,
        (dout, w_down),
    )


def ff_back_kernel(
    ready,
    dout_ref, mid_ref, gain_ref, act_ref, slope_ref, wg_ref, wu_ref, wd_ref,
    dgu_ref, dmid_ref, low_ref, dgain_ref,
    acc,
):
    c = pl.program_id(0)
    dproduct = wd_ref[...].astype(F32) if ready else nt_dot(dout_ref[...], wd_ref[...])
    dgate = (dproduct * slope_ref[...].astype(F32)).astype(BF16)
    dup = (dproduct * act_ref[...].astype(F32)).astype(BF16)
    dgu_ref[0] = dgate
    dgu_ref[1] = dup
    part = nt_dot(dgate, wg_ref[...]) + nt_dot(dup, wu_ref[...])

    @pl.when(c == 0)
    def _():
        acc[...] = part

    @pl.when(c > 0)
    def _():
        acc[...] += part

    @pl.when(c == pl.num_programs(0) - 1)
    def _():
        back, dgain = norm_back(mid_ref[...], gain_ref[...], acc[...])
        dmid = dout_ref[...].astype(F32) + back
        dmid_ref[...] = dmid
        low_ref[...] = dmid.astype(BF16)
        dgain_ref[...] = dgain


def feed_forward_back(dout, middle, gain, act, slope, w_gu, w_down, dproduct=None):
    rows, dim = dout.shape
    hidden = w_down.shape[0]
    width = 512
    blocks = hidden // width
    block = columns(rows, width)
    full = whole((rows, dim))
    return call(
        functools.partial(ff_back_kernel, dproduct is not None),
        (blocks,),
        [
            full, full, whole(gain.shape), block, block, columns(dim, width), columns(dim, width, blocks),
            pl.BlockSpec((width, dim), lambda c: (c, 0)) if dproduct is None else block,
        ],
        [pl.BlockSpec((2, rows, width), lambda c: (0, 0, c)), full, full, whole((1, dim))],
        [
            struct((2, rows, hidden), BF16), struct((rows, dim), F32),
            struct((rows, dim), BF16), struct((1, dim), F32),
        ],
        [pltpu.VMEM((rows, dim), F32)],
        6 * rows * dim * hidden * 1.2,
        6 * dim * hidden,
        (dout, middle, gain, act, slope, w_gu, w_gu, w_down if dproduct is None else dproduct),
    )


def mix_back_kernel(
    groups, length,
    low_ref, wo_ref, act_ref, slope_ref, hidden_ref, keep_ref,
    dbranch_ref, local_ref, sege_ref, segf_ref, agg_ref,
    dmixed,
):
    steps = length // SUB
    width = keep_ref.shape[1]
    chunk = 4
    dmixed[...] = nt_dot(low_ref[...], wo_ref[...])

    def step(i, carry):
        out = []
        for g in range(groups):
            s, p, after = carry[g]
            at = pl.multiple_of(g * length + (steps // chunk - 1 - i) * (chunk * SUB), chunk * SUB)
            here = pl.ds(at, chunk * SUB)
            d = dmixed[here, :]
            dbranch_ref[here, :] = (d * hidden_ref[here, :] * slope_ref[here, :]).astype(BF16)
            dhidden = d * act_ref[here, :]
            keep = keep_ref[here, :]
            states = [None] * chunk
            for r in reversed(range(chunk)):
                s = dhidden[r * SUB : (r + 1) * SUB] + after * s
                p = after * p
                after = keep[r * SUB : (r + 1) * SUB]
                states[r] = s
            local_ref[here, :] = jnp.concatenate(states, axis=0)
            out.append((s, p, after))
        return tuple(out)

    one = jnp.ones((SUB, width), F32)
    start = tuple((jnp.zeros((SUB, width), F32), one, one) for _ in range(groups))
    done = lax.fori_loop(0, steps // chunk, step, start)
    for g in range(groups):
        s, p, after = done[g]
        e, f = after * s, after * p
        sege_ref[g * SUB : (g + 1) * SUB, :] = e
        segf_ref[g * SUB : (g + 1) * SUB, :] = f
        a, b = jnp.ones((1, width), F32), jnp.zeros((1, width), F32)
        for r in reversed(range(SUB)):
            b = e[r : r + 1] + f[r : r + 1] * b
            a = f[r : r + 1] * a
        agg_ref[2 * g : 2 * g + 1, :] = a
        agg_ref[2 * g + 1 : 2 * g + 2, :] = b


def mix_back(low, w_out, act, slope, hidden, keep, groups, length):
    rows, dim = low.shape
    recur = keep.shape[1]
    width = 512
    block = columns(rows, width)
    return call(
        functools.partial(mix_back_kernel, groups, length),
        (recur // width,),
        [whole(low.shape), pl.BlockSpec((width, dim), lambda c: (c, 0)), block, block, block, block],
        [block, block, columns(SUB * groups, width), columns(SUB * groups, width), columns(2 * groups, width)],
        [
            struct((rows, recur), BF16), struct((rows, recur), F32), struct((SUB * groups, recur), F32),
            struct((SUB * groups, recur), F32), struct((2 * groups, recur), F32),
        ],
        [pltpu.VMEM((rows, width), F32)],
        2 * rows * dim * recur * 2,
        dim * recur * 2 + rows * recur * 18,
        (low, w_out, act, slope, hidden, keep),
    )


def gates_back_kernel(
    groups, length,
    local_ref, keep_ref, hidden_ref, ext_ref, rate_ref, igate_ref, sege_ref, segf_ref, gin_ref, hin_ref,
    ga_ref, gi_ref, vec_ref, mask_ref,
    din_ref, head_ref, dga_ref, dgi_ref, dvec_ref,
    dconv, low_a, low_i, rounded,
):
    steps = length // SUB
    width = keep_ref.shape[1]
    chunk = 4
    sub = lax.broadcasted_iota(jnp.int32, (SUB, width), 0)
    taps = [vec_ref[k : k + 1, :] for k in range(CONV)]
    conv_bias, scale = vec_ref[4:5, :], vec_ref[7:8, :]
    start = []
    for g in range(groups):
        e = sege_ref[g * SUB : (g + 1) * SUB, :]
        f = segf_ref[g * SUB : (g + 1) * SUB, :]
        y = gin_ref[g : g + 1, :]
        entering = [None] * SUB
        for s in reversed(range(SUB)):
            entering[s] = y
            y = e[s : s + 1] + f[s : s + 1] * y
        start.append((jnp.concatenate(entering, axis=0), jnp.ones((SUB, width), F32)))
    zero = jnp.zeros((SUB, width), F32)

    def fold(v):
        return functools.reduce(jnp.add, [v[q * SUB : (q + 1) * SUB] for q in range(v.shape[0] // SUB)])

    def step(i, carry):
        chains, sum_a, sum_i, sum_d = carry
        out = []
        j = steps // chunk - 1 - i
        for g in range(groups):
            r, after = chains[g]
            at = pl.multiple_of(g * length + j * (chunk * SUB), chunk * SUB)
            here = pl.ds(at, chunk * SUB)
            keep = keep_ref[here, :]
            parts = [None] * chunk
            for q in reversed(range(chunk)):
                r = after * r
                after = keep[q * SUB : (q + 1) * SUB]
                parts[q] = r
            state = local_ref[here, :] + jnp.concatenate(parts, axis=0)
            last = hidden_ref[(g + 1) * length - SUB : (g + 1) * length, :]
            wrapped = jnp.where(sub == 0, hin_ref[g : g + 1, :], pltpu.roll(last, 1, 0))
            before = pl.multiple_of(jnp.maximum(at - SUB, g * length), SUB)
            first = jnp.where(j == 0, wrapped, hidden_ref[pl.ds(before, SUB), :])
            rest = hidden_ref[pl.ds(at, (chunk - 1) * SUB), :]
            previous = jnp.concatenate([first, rest], axis=0)
            inner = pl.multiple_of(j * (chunk * SUB), chunk * SUB)
            conv = conv_bias + taps[0] * ext_ref[g, pl.ds(inner + 3 * SUB, chunk * SUB), :]
            for k in range(1, CONV):
                link = lanes(mask_ref[k, here, :], width)
                conv = conv + taps[k] * (link * ext_ref[g, pl.ds(inner + (3 - k) * SUB, chunk * SUB), :])
            rate, igate = rate_ref[here, :], igate_ref[here, :]
            space = 1.0 + 0.0001 - keep * keep
            inverse = lax.rsqrt(space)
            scaling = space * inverse
            both = state * igate
            dconv[here, :] = both * scaling
            with_conv = both * conv
            dlog = (state * previous - with_conv * (keep * inverse)) * keep
            dpre_a = (dlog * scale) * (rate * (1.0 - rate))
            dpre_i = (with_conv * scaling) * (1.0 - igate)
            low_a[here, :] = dpre_a.astype(BF16)
            low_i[here, :] = dpre_i.astype(BF16)
            rounded[here, :] = conv.astype(BF16)
            sum_a = sum_a + fold(dpre_a)
            sum_i = sum_i + fold(dpre_i)
            sum_d = sum_d + fold(dlog * rate)
            out.append((r, after))
        return tuple(out), sum_a, sum_i, sum_d

    _, sum_a, sum_i, sum_d = lax.fori_loop(0, steps // chunk, step, (tuple(start), zero, zero, zero))
    dvec_ref[5:6, :] = jnp.sum(sum_a, axis=0, keepdims=True)
    dvec_ref[6:7, :] = jnp.sum(sum_i, axis=0, keepdims=True)
    dvec_ref[7:8, :] = jnp.sum(sum_d, axis=0, keepdims=True)
    for h in range(width // LANES):
        col = slice(h * LANES, (h + 1) * LANES)
        dga_ref[h] = tn_dot(rounded[:, col], low_a[:, col])
        dgi_ref[h] = tn_dot(rounded[:, col], low_i[:, col])
        dconv[:, col] += nt_dot(low_a[:, col], ga_ref[h]) + nt_dot(low_i[:, col], gi_ref[h])

    sums = [zero] * (CONV + 1)
    for g in range(groups):

        def conv_step(i, carry, g=g):
            carry = list(carry)
            inner = pl.multiple_of(i * (chunk * SUB), chunk * SUB)
            here = pl.ds(pl.multiple_of(g * length + inner, chunk * SUB), chunk * SUB)
            d = dconv[here, :]
            carry[4] = carry[4] + fold(d)
            for k in range(CONV):
                masked = d if k == 0 else d * lanes(mask_ref[k, here, :], width)
                carry[k] = carry[k] + fold(masked * ext_ref[g, pl.ds(inner + (3 - k) * SUB, chunk * SUB), :])
            return tuple(carry)

        sums = list(lax.fori_loop(0, steps // chunk, conv_step, tuple(sums)))
        base = g * length
        tail = length - 3 * SUB
        total = taps[0] * dconv[base : base + tail, :]
        for k in range(1, CONV):
            there = slice(base + k * SUB, base + k * SUB + tail)
            total = total + taps[k] * (dconv[there, :] * lanes(mask_ref[k, there, :], width))
        din_ref[base : base + tail, :] = total

        def term(k, block):
            there = slice(base + block * SUB, base + (block + 1) * SUB)
            v = taps[k] * dconv[there, :]
            return v if k == 0 else v * lanes(mask_ref[k, there, :], width)

        heads = []
        for i in (3, 2, 1):
            j = steps - i
            value = term(0, j)
            head = None
            for k in range(1, CONV):
                if j + k < steps:
                    value = value + term(k, j + k)
                else:
                    t = term(k, j + k - steps)
                    value = value + jnp.where(sub == SUB - 1, 0.0, pltpu.roll(t, SUB - 1, 0))
                    head = t if head is None else head + t
            din_ref[base + j * SUB : base + (j + 1) * SUB, :] = value
            heads.append(head[0:1])
        head_ref[g * SUB : (g + 1) * SUB, :] = jnp.concatenate(heads + [jnp.zeros((SUB - 3, width), F32)], axis=0)
    for k in range(CONV + 1):
        dvec_ref[k : k + 1, :] = jnp.sum(sums[k], axis=0, keepdims=True)


def gates_back(local, keep, hidden, ext, rate, igate, sege, segf, gin, hin, gate_a, gate_i, vec, masks, groups, length):
    rows, recur = local.shape
    width = 512
    heads = width // LANES
    block = columns(rows, width)
    seg = columns(SUB * groups, width)
    gate = pl.BlockSpec((heads, LANES, LANES), lambda c: (c, 0, 0))
    return call(
        functools.partial(gates_back_kernel, groups, length),
        (recur // width,),
        [
            block, block, block, pl.BlockSpec((groups, length + 3 * SUB, width), lambda c: (0, 0, c)),
            block, block, seg, seg, columns(groups, width), columns(groups, width),
            gate, gate, columns(8, width), whole(masks.shape),
        ],
        [block, seg, gate, gate, columns(8, width)],
        [
            struct((rows, recur), F32), struct((SUB * groups, recur), F32), struct(gate_a.shape, F32),
            struct(gate_a.shape, F32), struct((8, recur), F32),
        ],
        [
            pltpu.VMEM((rows, width), F32), pltpu.VMEM((rows, width), BF16),
            pltpu.VMEM((rows, width), BF16), pltpu.VMEM((rows, width), BF16),
        ],
        rows * recur * 128 * 8 * 4,
        rows * recur * 28,
        (local, keep, hidden, ext, rate, igate, sege, segf, gin, hin, gate_a, gate_i, vec, masks),
    )


def branch_back_kernel(dbranch_ref, w_ref, out_ref):
    part = nt_dot(dbranch_ref[...], w_ref[...])

    @pl.when(pl.program_id(0) == 0)
    def _():
        out_ref[...] = part

    @pl.when(pl.program_id(0) > 0)
    def _():
        out_ref[...] += part


def branch_back(dbranch, w_in, first, dim):
    rows, recur = dbranch.shape
    width = 512
    return call(
        branch_back_kernel,
        (recur // width,),
        [columns(rows, width), columns(dim, width, first // width)],
        whole((rows, dim)),
        struct((rows, dim), F32),
        [],
        2 * rows * dim * recur,
        dim * recur * 2,
        (dbranch, w_in),
    )


def recur_in_back_kernel(
    groups, length,
    part_ref, din_ref, back_ref, wi_ref, x_ref, gain_ref, dmid_ref,
    low_ref, dx_ref, dgain_ref,
    acc,
):
    c = pl.program_id(0)
    width = din_ref.shape[1]
    rim = 4 * SUB
    sub = lax.broadcasted_iota(jnp.int32, (SUB, width), 0)
    for g in range(groups):
        base = g * length
        if length > rim:
            low_ref[base : base + length - rim, :] = din_ref[base : base + length - rim, :].astype(BF16)
        extra = [jnp.zeros((SUB, width), F32)]
        for i in range(3):
            extra.append(jnp.where(sub == SUB - 1, back_ref[g * SUB + i : g * SUB + i + 1, :], 0.0))
        tail = slice(base + length - rim, base + length)
        low_ref[tail, :] = (din_ref[tail, :] + jnp.concatenate(extra, axis=0)).astype(BF16)
    part = nt_dot(low_ref[...], wi_ref[...])

    @pl.when(c == 0)
    def _():
        acc[...] = part_ref[...] + part

    @pl.when(c > 0)
    def _():
        acc[...] += part

    @pl.when(c == pl.num_programs(0) - 1)
    def _():
        back, dgain = norm_back(x_ref[...].astype(F32), gain_ref[...], acc[...])
        dx_ref[...] = (dmid_ref[...] + back).astype(BF16)
        dgain_ref[...] = dgain


def recur_in_back(part, din, back, w_in, first, x, gain, dmid, groups, length):
    rows, dim = x.shape
    recur = din.shape[1]
    width = 512
    block = columns(rows, width)
    full = whole((rows, dim))
    return call(
        functools.partial(recur_in_back_kernel, groups, length),
        (recur // width,),
        [
            full, block, columns(SUB * groups, width), columns(dim, width, (first + recur) // width),
            full, whole(gain.shape), full,
        ],
        [block, full, whole((1, dim))],
        [struct((rows, recur), BF16), struct((rows, dim), BF16), struct((1, dim), F32)],
        [pltpu.VMEM((rows, dim), F32)],
        2 * rows * dim * recur * 1.5,
        2 * dim * recur + rows * recur * 8,
        (part, din, back, w_in, x, gain, dmid),
    )


def outer_kernel(places, pieces, place_ref, left_a, left_b, right_a, right_b, *refs):
    outs, (keep, send) = refs[:-2], refs[-2:]
    n, fs, share = places
    rows = left_a.shape[1]
    c = pl.program_id(0)
    per = pl.num_programs(0) // pieces

    @pl.when(c == 0)
    def _():
        core, y = place_ref[0], place_ref[1]
        for at in range(n):
            there = slice(at * share, (at + 1) * share)
            for scratch, side in ((keep, y), (send, 1 - y)):
                first = pl.multiple_of((at * fs + 2 * side + core) * share, share)
                scratch[there, 0:rows] = left_a[pl.ds(first, share), :]
                scratch[there, rows : 2 * rows] = left_b[pl.ds(first, share), :]

    right = jnp.concatenate([right_a[0], right_b[0]], axis=0)
    to_keep = nn_dot(keep[...], right).astype(BF16)
    to_send = nn_dot(send[...], right).astype(BF16)
    for p in range(pieces):

        @pl.when(c // per == p)
        def _(p=p):
            outs[2 * p][...] = to_keep
            outs[2 * p + 1][...] = to_send


def outer(lefts, at, k, rights, pieces, chosen, place, n, fs):
    rows = lefts[0].shape[1]
    count, _, total = rights[0].shape
    share = k // (n * fs)
    piece = count * total // pieces
    width = next(w for w in (768, 512, 384, 256, 128, piece) if piece % w == 0)
    across, per = total // width, piece // width
    skipped, pieces = chosen[0] * per, chosen[1]

    def out_block(p):
        return pl.BlockSpec((n * share, width), lambda c, place: (0, jnp.clip(c - p * per, 0, per - 1)))

    left = pl.BlockSpec((k, rows), lambda c, place: (at // k, 0))
    right = pl.BlockSpec((1, rows, width), lambda c, place: ((c + skipped) // across, 0, (c + skipped) % across))
    outs = pl.pallas_call(
        functools.partial(outer_kernel, (n, fs, share), pieces),
        grid_spec=pltpu.PrefetchScalarGridSpec(
            num_scalar_prefetch=1,
            grid=(pieces * per,),
            in_specs=[left, left, right, right],
            out_specs=[out_block(p) for p in range(pieces) for _ in range(2)],
            scratch_shapes=[pltpu.VMEM((n * share, 2 * rows), BF16)] * 2,
        ),
        out_shape=[struct((n * share, piece), BF16)] * (2 * pieces),
        compiler_params=pltpu.CompilerParams(dimension_semantics=("arbitrary",), vmem_limit_bytes=VMEM_BYTES),
        cost_estimate=pl.CostEstimate(
            flops=8 * n * share * rows * pieces * piece // COST, bytes_accessed=1, transcendentals=0
        ),
    )(place, *lefts, *rights)
    return [(outs[2 * p], outs[2 * p + 1]) for p in range(pieces)]


def unfold_kernel(folded_ref, out_ref):
    height, width = folded_ref.shape[0], out_ref.shape[1]
    for q in range(out_ref.shape[0] // height):
        out_ref[q * height : (q + 1) * height, :] = folded_ref[:, q * width : (q + 1) * width]


def unfold_first(packed, places, height, rows, width):
    return call(
        unfold_kernel,
        (places,),
        [pl.BlockSpec((height, rows // height * width), lambda c: (c, 0))],
        pl.BlockSpec((rows, width), lambda c: (c, 0)),
        struct((places * rows, width), packed.dtype),
        [],
        0,
        places * rows * width * 4,
        (packed,),
    )


def shifted(value, axis, by):
    length = lax.axis_size(axis)
    pairs = [(i, i + by) for i in range(length) if 0 <= i + by < length]
    return lax.ppermute(value, axis, pairs)


def entering(agg, groups, reverse):
    n = lax.axis_size("seq")
    sign = -1 if reverse else 1
    got = {k: shifted(agg, "seq", sign * k) for k in range(1, n)}
    state = jnp.zeros((groups, agg.shape[1]), F32)
    for k in range(n - 1, 0, -1):
        part = got[k].reshape(groups, 2, -1)
        state = part[:, 0] * state + part[:, 1]
    return state


def add(*parts):
    return functools.reduce(jnp.add, [p.astype(F32) for p in parts])


def line_sum(slots, mine, n, send):
    def at(offset):
        return slots((mine + offset) % n)

    up, down = at(n - 1), at(1)
    for s in range(1, n):
        got_up = send(up, [(i, i + 1) for i in range(s)])
        got_down = send(down, [(i, i - 1) for i in range(n - s, n)])
        if s < n - 1:
            up = add(at(n - 1 - s), got_up).astype(BF16)
            down = add(at(s + 1), got_down).astype(BF16)
    return add(at(0), got_up, got_down)


class Scatter:
    def __init__(self):
        self.n, self.fs = lax.axis_size("seq"), lax.axis_size("fsdp")
        self.ny = self.fs // 2
        self.z, f = lax.axis_index("seq"), lax.axis_index("fsdp")
        self.y, self.core = f // 2, f % 2

    def core_swap(self, value):
        return lax.ppermute(value, "fsdp", [(i, i ^ 1) for i in range(self.fs)])

    def y_send(self, value, pairs):
        return lax.ppermute(value, "fsdp", [(2 * a + c, 2 * b + c) for a, b in pairs for c in range(2)])

    def over_y(self, keep, send, since, beside):
        return add(after(keep, beside), self.y_send(after(send, since), [(0, 1), (1, 0)])).astype(BF16)

    def over_z(self, shares):
        return lax.psum_scatter(shares, "seq", scatter_dimension=0, tiled=True)[0].astype(F32)


def pick(value, index, axis):
    return lax.dynamic_index_in_dim(value, index, axis, keepdims=False)


def reorder(v):
    length, d = v.shape[-2:]
    return jnp.swapaxes(v.reshape(-1, SUB, length // SUB, d), 1, 2).reshape(-1, d)


def restore(v, shape):
    length, d = shape[-2:]
    return jnp.swapaxes(v.reshape(-1, length // SUB, SUB, d), 1, 2).reshape(shape)


def tail_rows(v, groups, length):
    d = v.shape[1]
    last = v.reshape(groups, length // SUB, SUB, d)[:, length // SUB - 3 :, SUB - 1]
    last = jnp.pad(last, ((0, 0), (0, SUB - 3), (0, 0))).reshape(groups * SUB, d)
    return jnp.pad(last, ((0, -groups * SUB % 16), (0, 0)))


def fold_rows(v, height):
    count = -(-v.shape[0] // height)
    v = jnp.pad(v, ((0, count * height - v.shape[0]), (0, 0)))
    return jnp.concatenate([v[i * height : (i + 1) * height] for i in range(count)], axis=1)


def fold_places(v, height):
    places, rows, width = v.shape
    count = -(-rows // height)
    v = jnp.pad(v, ((0, 0), (0, count * height - rows), (0, 0))).reshape(places, count, height, width)
    return jnp.swapaxes(v, 1, 2).reshape(places, height, count * width)


def unfold_rows(v, rows, width):
    places, height, total = v.shape
    v = jnp.swapaxes(v.reshape(places, height, total // width, width), 1, 2)
    return v.reshape(places, -1, width)[:, :rows]


def after(value, *others):
    return lax.optimization_barrier((value, others))[0]


def gather(shard):
    return lax.all_gather(shard, ("seq", "fsdp"), axis=0, tiled=True)


def body(
    ends, segment_ids, norm_one, w_branch, w_input, conv_weight, conv_bias, gate_a, gate_i, bias_a, bias_i,
    decay, w_out, norm_two, w_gate, w_up, w_down,
):
    is_first = lax.axis_index("section") == 0
    z = lax.axis_index("seq")
    n, fs = lax.axis_size("seq"), lax.axis_size("fsdp")
    places = n * fs
    micro, seqs, length, dim = ends.shape[1:]
    parts_of = 1
    groups = micro * seqs // parts_of
    rows = groups * length
    recur = w_branch.shape[2]
    heads, part, block = gate_a.shape[1:]
    hidden_dim = w_gate.shape[2]

    dshare, rshare = dim // places, recur // places
    vectors = [norm_one, norm_two] + [conv_weight[:, k] for k in range(CONV)] + [conv_bias, bias_a, bias_i, decay]
    vectors = jnp.concatenate([jnp.pad(v, ((0, 0), (0, LANES - v.shape[1]))) for v in vectors], axis=0)
    vectors = jnp.pad(vectors, ((0, 2 * SUB - vectors.shape[0]), (0, 0)))
    small = jnp.concatenate([vectors, gate_a.reshape(-1, block), gate_i.reshape(-1, block)], axis=0)
    small_rows = small.shape[0]
    small = fold_rows(small, dshare)
    first = hidden_dim
    w_in = gather(
        jnp.concatenate(
            [fold_rows(w_down[0], dshare), w_branch[0], w_input[0], w_out[0].reshape(dshare, recur), small], axis=1
        )
    )
    w_gu = gather(jnp.concatenate([after(w_gate[0], small), w_up[0]], axis=1))
    w_out_all = w_in[:, first + 2 * recur : first + 3 * recur].reshape(recur, dim)
    small = unfold_rows(w_in[:, first + 3 * recur :].reshape(places, dshare, -1), small_rows, LANES)
    hshare = hidden_dim // places
    if dshare % 16 == 0:
        w_down_all = unfold_first(w_in, places, dshare, hshare, dim)
    else:
        w_down_all = unfold_rows(w_in[:, :first].reshape(places, dshare, -1), hshare, dim).reshape(hidden_dim, dim)

    def vector(row, share):
        return small[:, row, :share].reshape(1, places * share).astype(F32)

    gain_one, gain_two = vector(0, dshare), vector(1, dshare)
    decays = vector(9, rshare)
    vec = jnp.concatenate([vector(r, rshare) for r in range(2, 9)] + [-8.0 * jax.nn.softplus(decays)], axis=0)
    gates_a, gates_i = [
        jnp.swapaxes(small[:, r : r + heads * part].reshape(places, heads, part, block), 0, 1).reshape(heads, block, block)
        for r in (2 * SUB, 2 * SUB + heads * part)
    ]

    padded_ids = jnp.pad(segment_ids, ((0, 0), (0, 0), (CONV - 1, 0)), constant_values=-1)
    window = lax.dynamic_slice_in_dim(padded_ids, z * length, length + CONV - 1, axis=2)
    current = window[:, :, CONV - 1 :]
    masks = jnp.stack(
        [window[:, :, CONV - 1 - k : CONV - 1 - k + length] == current for k in (1, 1, 2, 3)]
    ).astype(F32)
    masks = jnp.swapaxes(masks.reshape(4, parts_of, groups, SUB, length // SUB), 3, 4).reshape(4, parts_of, rows, 1)
    masks = jnp.broadcast_to(masks, (4, parts_of, rows, LANES))
    masks = [masks[:, m] for m in range(parts_of)]
    micros = range(parts_of)

    def forward(xs, halos, save):
        got = []
        for m in micros:
            got.append(recur_in(xs[m], halos[m], gain_one, w_in, first, gates_a, gates_i, vec, masks[m], groups, length))
        hin = entering(jnp.concatenate([g[7] for g in got], axis=0), parts_of * groups, False)
        acts = [branch_in(after(g[0], got[-1][7]), w_in, first, recur) for g in got]
        outs, saved = [], []
        for m in micros:
            normed, ext, rate, igate, keep, local, segp, _ = got[m]
            act, slope = acts[m]
            mine = hin[m * groups : (m + 1) * groups]
            if m:
                keep = after(keep, outs[-1])
            hidden, mixed, middle, normed_two = recur_out(
                xs[m], keep, local, act, segp, mine, w_out_all, gain_two, groups, length
            )
            results = feed_forward(normed_two, middle, w_gu, w_down_all, save)
            outs.append(results[-1])
            saved.append(
                (normed, ext, rate, igate, keep, mine, hidden, mixed, middle, normed_two, act, slope) + tuple(results[:-1])
            )
        return outs, saved

    def back_ff(m, dout, saved, dproduct=None):
        return feed_forward_back(dout, saved[m][8], gain_two, saved[m][12], saved[m][13], w_gu, w_down_all, dproduct)

    def back_mix(m, low, saved):
        return mix_back(low, w_out_all, saved[m][10], saved[m][11], saved[m][6], saved[m][4], groups, length)

    def back_gates(m, mixed_back, gin, saved):
        normed, ext, rate, igate, keep, hin, hidden = saved[m][:7]
        _, local, sege, segf, _ = mixed_back
        din, head, dga, dgi, dvec = gates_back(
            local, keep, hidden, ext, rate, igate, sege, segf, gin[m * groups : (m + 1) * groups], hin,
            gates_a, gates_i, vec, masks[m], groups, length,
        )
        return din, shifted(head, "seq", -1), dga, dgi, dvec

    def back_in(m, part, gates, dmid, xs):
        return recur_in_back(part, gates[0], gates[1], w_in, first, xs[m], gain_one, dmid, groups, length)

    own = [reorder(v) for v in ends[0].reshape((parts_of, -1) + ends.shape[3:])]
    tails = [shifted(tail_rows(v, groups, length), "seq", 1) for v in own]
    outs, _ = forward(own, tails, False)
    xs, halos = [], []
    for m in micros:
        dproduct = down_back(after(own[m], outs[m]), w_down_all)
        received = after(shifted(outs[m], "section", 1), dproduct)
        received_halo = lax.ppermute(
            tail_rows(outs[m], groups, length), ("section", "seq"), [(i, n + i + 1) for i in range(n - 1)]
        )
        xs.append(jnp.where(is_first, own[m], received))
        halos.append(jnp.where(is_first, tails[m], received_halo))
    outs, saved = forward(xs, halos, True)

    scatter = Scatter()
    swap = scatter.core_swap
    place = jnp.stack([scatter.core, scatter.y]).astype(jnp.int32)

    ff = back_ff(0, own[0], saved, dproduct)
    mix = back_mix(0, ff[2], saved)
    gin = entering(mix[4], groups, True)
    product_t = after(saved[0][14], mix[4]).T
    product_pair = (product_t, swap(product_t))
    gates = back_gates(0, after(mix, product_t), gin, saved)
    base = branch_back(after(mix[0], gates[0]), w_in, first, dim)
    dx = back_in(0, base, gates, ff[1], xs)[1]
    others = [after(saved[0][i], dx) for i in (9, 0, 7)]
    starts_at, total_rows = [], 0
    for i, v in enumerate(others):
        gap = -total_rows % v.shape[1]
        if gap:
            others[i] = jnp.concatenate([jnp.zeros((rows, gap), BF16), v], axis=1)
        starts_at.append((total_rows + gap, v.shape[1]))
        total_rows += gap + v.shape[1]
    others = jnp.concatenate([v.T for v in others], axis=0)
    received = after(shifted(dx, "section", -1), others, product_pair)
    others = after(others, received)
    others = (others, swap(others))
    lefts = {"product": (product_pair, 0, hidden_dim)}
    for name, (at, k) in zip(("two", "one", "mixed"), starts_at):
        lefts[name] = (others, at, k)
    dout = jnp.where(is_first, received, own[0])

    def pair(value):
        value = value if value.ndim == 3 else value[None]
        return value, swap(value)

    def products(name, rights, pieces=1, chosen=None):
        both, at, k = lefts[name]
        chosen = chosen or (0, pieces)
        if scatter.ny == 2:
            return outer(both, at, k, rights, pieces, chosen, place, n, fs)
        left = jnp.concatenate([v[at : at + k] for v in both], axis=1)
        right = jnp.concatenate([jnp.concatenate(list(v), axis=1) for v in rights], axis=0)
        grad = nn_dot(left, right).astype(BF16)
        grad = pick(grad.reshape(n, scatter.ny, 2, -1, grad.shape[1]), scatter.core, 2)
        return [(p,) for p in jnp.split(grad, pieces, axis=3)[chosen[0] : sum(chosen)]]

    def over_y(grads, since, *beside):
        if scatter.ny == 2:
            return scatter.over_y(*[g.reshape(n, -1, g.shape[1]) for g in grads], since, beside)
        (grad,) = grads
        return line_sum(lambda d: pick(grad, d, 1), scatter.y, scatter.ny, scatter.y_send).astype(BF16)

    down = products("product", pair(dout), 2)
    dgu, dmid, out_low, dgain_two = back_ff(0, after(dout, down), saved)
    down_sums = [over_y(down[0], (), out_low)]
    down_sums.append(None)
    gu_pair = pair(after(dgu, down_sums[0]))
    mix = back_mix(0, after(out_low, down_sums[0]), saved)
    gate_up = products("two", after(gu_pair, mix[0]), 4, (0, 1))
    down_sums[1] = over_y(down[1], out_low, gate_up[0])
    gin = entering(after(mix[4], down_sums[1]), groups, True)
    gate_up += products("two", after(gu_pair, down_sums[1]), 4, (1, 3))
    gate_up_sums = [over_y(gate_up[0], (), gate_up[1], gin)]
    gates = back_gates(0, after(mix, gate_up_sums[0]), gin, saved)
    gate_up_sums.append(over_y(gate_up[1], gin, gates[0]))
    out_low, dbranch = after((out_low, mix[0]), gate_up_sums[1])
    out_pair, branch_pair = pair(out_low), pair(dbranch)
    base = branch_back(dbranch, w_in, first, dim)
    results = back_in(0, base, gates, dmid, xs)
    gate_up_sums.append(over_y(gate_up[2], gates[0], results[1], out_pair[1], branch_pair[1]))
    input_pair = pair(after(results[0], gate_up_sums[2]))
    out = products("mixed", after(out_pair, gate_up_sums[2]))
    branch = products("one", after(branch_pair, out))
    dgain_one = results[2]
    dga, dgi, dvec = gates[2:5]
    ddecay = -8.0 * jax.nn.sigmoid(decays) * dvec[7:8]
    shares = [dgain_one, dgain_two] + [dvec[k : k + 1] for k in range(7)] + [ddecay]
    shares = [v.reshape(places, 1, -1) for v in shares]
    shares = [jnp.pad(v, ((0, 0), (0, 0), (0, LANES - v.shape[2]))) for v in shares]
    shares = jnp.pad(jnp.concatenate(shares, axis=1), ((0, 0), (0, 2 * SUB - len(shares)), (0, 0)))
    packed = jnp.concatenate(
        [shares]
        + [jnp.swapaxes(v.reshape(heads, places, part, block), 0, 1).reshape(places, -1, block) for v in (dga, dgi)],
        axis=1,
    )
    extra = fold_places(packed, dshare).reshape(n, scatter.ny, 2, dshare, -1)
    theirs = swap(pick(extra, 1 - scatter.core, 2).astype(BF16))
    extra = add(pick(extra, scatter.core, 2), theirs).astype(BF16)
    gate_up_sums.append(over_y(gate_up[3], results[1], branch, extra))
    into = products("one", after(input_pair, gate_up_sums[3]))
    out_sum = over_y(out[0], branch, into)
    if scatter.ny == 2:
        sides = (pick(extra, scatter.y, 1), pick(extra, 1 - scatter.y, 1))
        last = [
            jnp.concatenate([g.reshape(n, dshare, -1), v], axis=2).reshape(n * dshare, -1) for g, v in zip(into[0], sides)
        ]
    else:
        last = (jnp.concatenate([into[0][0], extra], axis=3),)
    branch_sum = over_y(branch[0], out_sum, last)
    input_sum = over_y(last, branch_sum)

    outputs = restore(outs[0], ends.shape)
    input_grads = restore(results[1], ends.shape)
    shares = down_sums + gate_up_sums + [out_sum, branch_sum, input_sum]
    for i in range(1, len(shares)):
        shares[i] = after(shares[i], shares[i - 1])
    totals = [scatter.over_z(v) for v in shares]
    sum_down, sum_gate, sum_up = [jnp.concatenate(totals[i : i + 2], axis=1) for i in (0, 2, 4)]
    sum_out, sum_branch, sum_input = totals[6:]
    sum_input, sums = sum_input[:, :recur], sum_input[:, recur:]
    sums = unfold_rows(sums[None], small_rows, LANES)[0]
    gate_sums = [sums[r : r + heads * part].reshape(gate_a.shape) for r in (2 * SUB, 2 * SUB + heads * part)]

    return (
        outputs,
        input_grads,
        sums[0:1, :dshare],
        sum_branch[None],
        sum_input[None],
        sums[2 : 2 + CONV, :rshare][None],
        sums[6:7, :rshare],
        gate_sums[0],
        gate_sums[1],
        sums[7:8, :rshare],
        sums[8:9, :rshare],
        sums[9:10, :rshare],
        sum_out[None],
        sums[1:2, :dshare],
        sum_gate[None],
        sum_up[None],
        sum_down[None],
    )


def solution(mesh):
    tokens = P("section", None, "fsdp", "seq", None)
    vector = P("section", ("seq", "fsdp"))
    matrix = P("section", ("seq", "fsdp"), None)
    taps = P("section", None, ("seq", "fsdp"))
    gates = P("section", None, ("seq", "fsdp"), None)
    weights = (
        vector, matrix, matrix, taps, vector, gates, gates, vector, vector, vector, matrix, vector, matrix, matrix, matrix,
    )
    return jax.shard_map(
        body,
        mesh=mesh,
        in_specs=(tokens, P(None, "fsdp", None)) + weights,
        out_specs=(tokens, tokens) + weights,
        check_vma=False,
    )
```

```python
import functools

import jax
import jax.numpy as jnp
from jax import lax
from jax.experimental import pallas as pl
from jax.experimental.pallas import tpu as pltpu
from jax.sharding import PartitionSpec as P

CONV = 4
EPS = 1e-06
F32 = jnp.float32
BF16 = jnp.bfloat16
VMEM_BYTES = 56 << 20
LANES = 128
SUB = 8
COST = 4


def nn_dot(a, b):
    return lax.dot_general(a, b, (((1,), (0,)), ((), ())), preferred_element_type=F32)


def nt_dot(a, b):
    return lax.dot_general(a, b, (((1,), (1,)), ((), ())), preferred_element_type=F32)


def tn_dot(a, b):
    return lax.dot_general(a, b, (((0,), (0,)), ((), ())), preferred_element_type=F32)


def sigmoid(v):
    return 0.5 * jnp.tanh(0.5 * v) + 0.5


K0 = 0.7978845608028654
K1 = 0.044715


def gelu(v):
    return 0.5 * v * (1.0 + jnp.tanh(K0 * (v + K1 * v * v * v)))


def gelu_both(v):
    square = v * v
    t = jnp.tanh(K0 * v * (1.0 + K1 * square))
    half = 0.5 * (1.0 + t)
    slope = half + (0.5 * K0) * v * (1.0 - t * t) * (1.0 + (3.0 * K1) * square)
    return v * half, slope


def lanes(mask, width):
    return jnp.concatenate([mask] * (width // LANES), axis=1) if width > LANES else mask


def call(kernel, grid, in_specs, out_specs, out_shape, scratch, flops, bytes_accessed, args):
    return pl.pallas_call(
        kernel,
        grid=grid,
        in_specs=in_specs,
        out_specs=out_specs,
        out_shape=out_shape,
        scratch_shapes=scratch,
        compiler_params=pltpu.CompilerParams(
            dimension_semantics=("arbitrary",) * len(grid), vmem_limit_bytes=VMEM_BYTES
        ),
        cost_estimate=pl.CostEstimate(
            flops=int(flops) // COST, bytes_accessed=int(bytes_accessed) // COST, transcendentals=0
        ),
    )(*args)


def whole(shape):
    return pl.BlockSpec(shape, lambda c: (0,) * len(shape))


def columns(rows, width, offset=0):
    return pl.BlockSpec((rows, width), lambda c: (0, c + offset))


def struct(shape, dtype):
    return jax.ShapeDtypeStruct(shape, dtype)


def recur_in_kernel(
    groups, length,
    x_ref, halo_ref, gain_ref, wi_ref, ga_ref, gi_ref, vec_ref, mask_ref,
    normed_ref, ext_ref, rate_ref, igate_ref, keep_ref, local_ref, segp_ref, agg_ref,
    xn, conv, pre_a, pre_i,
):
    rows = groups * length
    steps = length // SUB
    width = wi_ref.shape[1]

    @pl.when(pl.program_id(0) == 0)
    def _():
        gain = gain_ref[...]
        for at, ref in ((0, x_ref), (rows, halo_ref)):
            v = ref[...].astype(F32)
            r = lax.rsqrt(jnp.mean(v * v, axis=-1, keepdims=True) + EPS)
            xn[at : at + ref.shape[0], :] = (v * r * gain).astype(BF16)
        normed_ref[...] = xn[0:rows, :]

    conv_in = nn_dot(xn[...], wi_ref[...]).astype(BF16).astype(F32)
    sub = lax.broadcasted_iota(jnp.int32, (SUB, width), 0)
    for g in range(groups):
        base = conv_in[g * length : (g + 1) * length]
        halo = conv_in[rows + g * SUB : rows + (g + 1) * SUB]
        for k in (3, 2, 1):
            block = pltpu.roll(base[(steps - k) * SUB : (steps - k + 1) * SUB], 1, 0)
            ext_ref[g, (3 - k) * SUB : (4 - k) * SUB, :] = jnp.where(sub == 0, halo[3 - k : 4 - k], block)
        ext_ref[g, 3 * SUB : 3 * SUB + length, :] = base
    taps = [vec_ref[k : k + 1, :] for k in range(CONV)]
    for g in range(groups):
        part = slice(g * length, (g + 1) * length)
        out = vec_ref[4:5, :] + taps[0] * ext_ref[g, 3 * SUB : 3 * SUB + length, :]
        for k in range(1, CONV):
            link = lanes(mask_ref[k, part, :], width)
            out = out + taps[k] * (link * ext_ref[g, (3 - k) * SUB : (3 - k) * SUB + length, :])
        conv[part, :] = out
    rounded = conv[...].astype(BF16)
    for h in range(width // LANES):
        col = slice(h * LANES, (h + 1) * LANES)
        pre_a[:, col] = nn_dot(rounded[:, col], ga_ref[h])
        pre_i[:, col] = nn_dot(rounded[:, col], gi_ref[h])
    bias_a, bias_i, scale = vec_ref[5:6, :], vec_ref[6:7, :], vec_ref[7:8, :]
    chunk = 4

    def step(i, carry):
        out = []
        for g in range(groups):
            h, p = carry[g]
            at = pl.multiple_of(g * length + i * (chunk * SUB), chunk * SUB)
            here = pl.ds(at, chunk * SUB)
            rate = sigmoid(pre_a[here, :] + bias_a)
            igate = sigmoid(pre_i[here, :] + bias_i)
            keep = jnp.exp(scale * rate) * lanes(mask_ref[0, here, :], width)
            driven = igate * conv[here, :] * jnp.sqrt(1.0 + 0.0001 - keep * keep)
            rate_ref[here, :] = rate
            igate_ref[here, :] = igate
            keep_ref[here, :] = keep
            states = []
            for q in range(chunk):
                kq = keep[q * SUB : (q + 1) * SUB]
                h = kq * h + driven[q * SUB : (q + 1) * SUB]
                p = kq * p
                states.append(h)
            local_ref[here, :] = jnp.concatenate(states, axis=0)
            out.append((h, p))
        return tuple(out)

    start = tuple((jnp.zeros((SUB, width), F32), jnp.ones((SUB, width), F32)) for _ in range(groups))
    done = lax.fori_loop(0, steps // chunk, step, start)
    for g in range(groups):
        h, p = done[g]
        segp_ref[g * SUB : (g + 1) * SUB, :] = p
        a, b = jnp.ones((1, width), F32), jnp.zeros((1, width), F32)
        for s in range(SUB):
            b = p[s : s + 1] * b + h[s : s + 1]
            a = p[s : s + 1] * a
        agg_ref[2 * g : 2 * g + 1, :] = a
        agg_ref[2 * g + 1 : 2 * g + 2, :] = b


def recur_in(x, halo, gain, w_in, first, gate_a, gate_i, vec, masks, groups, length):
    rows, dim = x.shape
    recur = vec.shape[1]
    width = 512
    blocks = recur // width
    block_f32 = columns(rows, width)
    heads = width // LANES
    ext_len = length + 3 * SUB
    return call(
        functools.partial(recur_in_kernel, groups, length),
        (blocks,),
        [
            whole(x.shape), whole(halo.shape), whole(gain.shape),
            columns(dim, width, (first + recur) // width),
            pl.BlockSpec((heads, LANES, LANES), lambda c: (c, 0, 0)),
            pl.BlockSpec((heads, LANES, LANES), lambda c: (c, 0, 0)),
            columns(8, width), whole(masks.shape),
        ],
        [
            whole((rows, dim)),
            pl.BlockSpec((groups, ext_len, width), lambda c: (0, 0, c)),
            block_f32, block_f32, block_f32, block_f32,
            columns(SUB * groups, width), columns(2 * groups, width),
        ],
        [
            struct((rows, dim), BF16), struct((groups, ext_len, recur), F32),
            struct((rows, recur), F32), struct((rows, recur), F32), struct((rows, recur), F32),
            struct((rows, recur), F32), struct((SUB * groups, recur), F32), struct((2 * groups, recur), F32),
        ],
        [
            pltpu.VMEM((rows + halo.shape[0], dim), BF16), pltpu.VMEM((rows, width), F32),
            pltpu.VMEM((rows, width), F32), pltpu.VMEM((rows, width), F32),
        ],
        2 * rows * dim * recur * 2.5,
        dim * recur * 2 + rows * recur * 4 * 5,
        (x, halo, gain, w_in, gate_a, gate_i, vec, masks),
    )


def branch_kernel(x_ref, w_ref, act_ref, slope_ref):
    act, slope = gelu_both(nn_dot(x_ref[...], w_ref[...]))
    act_ref[...] = act
    slope_ref[...] = slope


def branch_in(x, w_in, first, recur):
    rows, dim = x.shape
    width = 512
    block = columns(rows, width)
    return call(
        branch_kernel,
        (recur // width,),
        [whole(x.shape), columns(dim, width, first // width)],
        [block, block],
        [struct((rows, recur), F32)] * 2,
        [],
        2 * rows * dim * recur * 1.5,
        dim * recur * 2 + rows * recur * 8,
        (x, w_in),
    )


def recur_out_kernel(
    groups, length,
    x_ref, keep_ref, local_ref, act_ref, segp_ref, hin_ref, wo_ref, gain_ref,
    hidden_ref, mixed_ref, middle_ref, normed_ref,
    acc,
):
    steps = length // SUB
    width = keep_ref.shape[1]
    chunk = 4
    c = pl.program_id(0)
    start = []
    for g in range(groups):
        ends = local_ref[(g + 1) * length - SUB : (g + 1) * length, :]
        prods = segp_ref[g * SUB : (g + 1) * SUB, :]
        state = hin_ref[g : g + 1, :]
        entering = []
        for s in range(SUB):
            entering.append(state)
            state = prods[s : s + 1] * state + ends[s : s + 1]
        start.append(jnp.concatenate(entering, axis=0))

    def step(i, carry):
        out = []
        for g in range(groups):
            q = carry[g]
            at = pl.multiple_of(g * length + i * (chunk * SUB), chunk * SUB)
            here = pl.ds(at, chunk * SUB)
            keep = keep_ref[here, :]
            moved = []
            for r in range(chunk):
                q = keep[r * SUB : (r + 1) * SUB] * q
                moved.append(q)
            hidden = local_ref[here, :] + jnp.concatenate(moved, axis=0)
            hidden_ref[here, :] = hidden
            mixed_ref[here, :] = (hidden * act_ref[here, :]).astype(BF16)
            out.append(q)
        return tuple(out)

    lax.fori_loop(0, steps // chunk, step, tuple(start))
    part = nn_dot(mixed_ref[...], wo_ref[...])

    @pl.when(c == 0)
    def _():
        acc[...] = x_ref[...].astype(F32) + part

    @pl.when(c > 0)
    def _():
        acc[...] += part

    @pl.when(c == pl.num_programs(0) - 1)
    def _():
        m = acc[...]
        middle_ref[...] = m
        r = lax.rsqrt(jnp.mean(m * m, axis=-1, keepdims=True) + EPS)
        normed_ref[...] = (m * r * gain_ref[...]).astype(BF16)


def recur_out(x, keep, local, act, segp, hin, w_out, gain, groups, length):
    rows, dim = x.shape
    recur = keep.shape[1]
    width = 512
    block = columns(rows, width)
    return call(
        functools.partial(recur_out_kernel, groups, length),
        (recur // width,),
        [
            whole(x.shape), block, block, block, columns(SUB * groups, width), columns(groups, width),
            pl.BlockSpec((width, dim), lambda c: (c, 0)), whole(gain.shape),
        ],
        [block, block, whole((rows, dim)), whole((rows, dim))],
        [
            struct((rows, recur), F32), struct((rows, recur), BF16),
            struct((rows, dim), F32), struct((rows, dim), BF16),
        ],
        [pltpu.VMEM((rows, dim), F32)],
        2 * rows * dim * recur * 1.5,
        dim * recur * 2 + rows * recur * 18,
        (x, keep, local, act, segp, hin, w_out, gain),
    )


def ff_kernel(save, x_ref, mid_ref, wg_ref, wu_ref, wd_ref, *refs):
    c = pl.program_id(0)
    out_ref, acc = refs[-2:]
    x = x_ref[...]
    gate = nn_dot(x, wg_ref[...])
    up = nn_dot(x, wu_ref[...])
    if save:
        act_ref, slope_ref, product_ref = refs[:3]
        act, slope = gelu_both(gate)
        act_ref[...] = act.astype(BF16)
        slope_ref[...] = (up * slope).astype(BF16)
        product = (act * up).astype(BF16)
        product_ref[...] = product.T
    else:
        product = (gelu(gate) * up).astype(BF16)
    part = nn_dot(product, wd_ref[...])

    @pl.when(c == 0)
    def _():
        acc[...] = mid_ref[...] + part

    @pl.when(c > 0)
    def _():
        acc[...] += part

    @pl.when(c == pl.num_programs(0) - 1)
    def _():
        out_ref[...] = acc[...].astype(BF16)


def feed_forward(x, middle, w_gu, w_down, save):
    rows, dim = x.shape
    hidden = w_down.shape[0]
    width = 512
    blocks = hidden // width
    block = columns(rows, width)
    return call(
        functools.partial(ff_kernel, save),
        (blocks,),
        [
            whole(x.shape), whole(middle.shape), columns(dim, width), columns(dim, width, blocks),
            pl.BlockSpec((width, dim), lambda c: (c, 0)),
        ],
        ([block] * 2 + [pl.BlockSpec((width, rows), lambda c: (c, 0))] if save else []) + [whole((rows, dim))],
        ([struct((rows, hidden), BF16)] * 2 + [struct((hidden, rows), BF16)] if save else [])
        + [struct((rows, dim), BF16)],
        [pltpu.VMEM((rows, dim), F32)],
        6 * rows * dim * hidden * 1.5,
        6 * dim * hidden,
        (x, middle, w_gu, w_gu, w_down),
    )


def norm_back(values, gain, grad):
    q = lax.rsqrt(jnp.mean(values * values, axis=-1, keepdims=True) + EPS)
    t = gain * grad
    back = q * t - values * (q * q * q * jnp.mean(values * t, axis=-1, keepdims=True))
    return back, jnp.sum(values * q * grad, axis=0, keepdims=True)


def down_back_kernel(dout_ref, wd_ref, dproduct_ref):
    dproduct_ref[...] = nt_dot(dout_ref[...], wd_ref[...]).astype(BF16)


def down_back(dout, w_down):
    rows, dim = dout.shape
    hidden = w_down.shape[0]
    width = 512
    return call(
        down_back_kernel,
        (hidden // width,),
        [whole((rows, dim)), pl.BlockSpec((width, dim), lambda c: (c, 0))],
        columns(rows, width),
        struct((rows, hidden), BF16),
        [],
        2 * rows * dim * hidden,
        2 * dim * hidden + 4 * rows * hidden,
        (dout, w_down),
    )


def ff_back_kernel(
    ready,
    dout_ref, mid_ref, gain_ref, act_ref, slope_ref, wg_ref, wu_ref, wd_ref,
    dgu_ref, dmid_ref, low_ref, dgain_ref,
    acc,
):
    c = pl.program_id(0)
    dproduct = wd_ref[...].astype(F32) if ready else nt_dot(dout_ref[...], wd_ref[...])
    dgate = (dproduct * slope_ref[...].astype(F32)).astype(BF16)
    dup = (dproduct * act_ref[...].astype(F32)).astype(BF16)
    dgu_ref[0] = dgate
    dgu_ref[1] = dup
    part = nt_dot(dgate, wg_ref[...]) + nt_dot(dup, wu_ref[...])

    @pl.when(c == 0)
    def _():
        acc[...] = part

    @pl.when(c > 0)
    def _():
        acc[...] += part

    @pl.when(c == pl.num_programs(0) - 1)
    def _():
        back, dgain = norm_back(mid_ref[...], gain_ref[...], acc[...])
        dmid = dout_ref[...].astype(F32) + back
        dmid_ref[...] = dmid
        low_ref[...] = dmid.astype(BF16)
        dgain_ref[...] = dgain


def feed_forward_back(dout, middle, gain, act, slope, w_gu, w_down, dproduct=None):
    rows, dim = dout.shape
    hidden = w_down.shape[0]
    width = 512
    blocks = hidden // width
    block = columns(rows, width)
    full = whole((rows, dim))
    return call(
        functools.partial(ff_back_kernel, dproduct is not None),
        (blocks,),
        [
            full, full, whole(gain.shape), block, block, columns(dim, width), columns(dim, width, blocks),
            pl.BlockSpec((width, dim), lambda c: (c, 0)) if dproduct is None else block,
        ],
        [pl.BlockSpec((2, rows, width), lambda c: (0, 0, c)), full, full, whole((1, dim))],
        [
            struct((2, rows, hidden), BF16), struct((rows, dim), F32),
            struct((rows, dim), BF16), struct((1, dim), F32),
        ],
        [pltpu.VMEM((rows, dim), F32)],
        6 * rows * dim * hidden * 1.2,
        6 * dim * hidden,
        (dout, middle, gain, act, slope, w_gu, w_gu, w_down if dproduct is None else dproduct),
    )


def mix_back_kernel(
    groups, length,
    low_ref, wo_ref, act_ref, slope_ref, hidden_ref, keep_ref,
    dbranch_ref, local_ref, sege_ref, segf_ref, agg_ref,
    dmixed,
):
    steps = length // SUB
    width = keep_ref.shape[1]
    chunk = 4
    dmixed[...] = nt_dot(low_ref[...], wo_ref[...])

    def step(i, carry):
        out = []
        for g in range(groups):
            s, p, after = carry[g]
            at = pl.multiple_of(g * length + (steps // chunk - 1 - i) * (chunk * SUB), chunk * SUB)
            here = pl.ds(at, chunk * SUB)
            d = dmixed[here, :]
            dbranch_ref[here, :] = (d * hidden_ref[here, :] * slope_ref[here, :]).astype(BF16)
            dhidden = d * act_ref[here, :]
            keep = keep_ref[here, :]
            states = [None] * chunk
            for r in reversed(range(chunk)):
                s = dhidden[r * SUB : (r + 1) * SUB] + after * s
                p = after * p
                after = keep[r * SUB : (r + 1) * SUB]
                states[r] = s
            local_ref[here, :] = jnp.concatenate(states, axis=0)
            out.append((s, p, after))
        return tuple(out)

    one = jnp.ones((SUB, width), F32)
    start = tuple((jnp.zeros((SUB, width), F32), one, one) for _ in range(groups))
    done = lax.fori_loop(0, steps // chunk, step, start)
    for g in range(groups):
        s, p, after = done[g]
        e, f = after * s, after * p
        sege_ref[g * SUB : (g + 1) * SUB, :] = e
        segf_ref[g * SUB : (g + 1) * SUB, :] = f
        a, b = jnp.ones((1, width), F32), jnp.zeros((1, width), F32)
        for r in reversed(range(SUB)):
            b = e[r : r + 1] + f[r : r + 1] * b
            a = f[r : r + 1] * a
        agg_ref[2 * g : 2 * g + 1, :] = a
        agg_ref[2 * g + 1 : 2 * g + 2, :] = b


def mix_back(low, w_out, act, slope, hidden, keep, groups, length):
    rows, dim = low.shape
    recur = keep.shape[1]
    width = 512
    block = columns(rows, width)
    return call(
        functools.partial(mix_back_kernel, groups, length),
        (recur // width,),
        [whole(low.shape), pl.BlockSpec((width, dim), lambda c: (c, 0)), block, block, block, block],
        [block, block, columns(SUB * groups, width), columns(SUB * groups, width), columns(2 * groups, width)],
        [
            struct((rows, recur), BF16), struct((rows, recur), F32), struct((SUB * groups, recur), F32),
            struct((SUB * groups, recur), F32), struct((2 * groups, recur), F32),
        ],
        [pltpu.VMEM((rows, width), F32)],
        2 * rows * dim * recur * 2,
        dim * recur * 2 + rows * recur * 18,
        (low, w_out, act, slope, hidden, keep),
    )


def gates_back_kernel(
    groups, length,
    local_ref, keep_ref, hidden_ref, ext_ref, rate_ref, igate_ref, sege_ref, segf_ref, gin_ref, hin_ref,
    ga_ref, gi_ref, vec_ref, mask_ref,
    din_ref, head_ref, dga_ref, dgi_ref, dvec_ref,
    dconv, low_a, low_i, rounded,
):
    steps = length // SUB
    width = keep_ref.shape[1]
    chunk = 4
    sub = lax.broadcasted_iota(jnp.int32, (SUB, width), 0)
    taps = [vec_ref[k : k + 1, :] for k in range(CONV)]
    conv_bias, scale = vec_ref[4:5, :], vec_ref[7:8, :]
    start = []
    for g in range(groups):
        e = sege_ref[g * SUB : (g + 1) * SUB, :]
        f = segf_ref[g * SUB : (g + 1) * SUB, :]
        y = gin_ref[g : g + 1, :]
        entering = [None] * SUB
        for s in reversed(range(SUB)):
            entering[s] = y
            y = e[s : s + 1] + f[s : s + 1] * y
        start.append((jnp.concatenate(entering, axis=0), jnp.ones((SUB, width), F32)))
    zero = jnp.zeros((SUB, width), F32)

    def fold(v):
        return functools.reduce(jnp.add, [v[q * SUB : (q + 1) * SUB] for q in range(v.shape[0] // SUB)])

    def step(i, carry):
        chains, sum_a, sum_i, sum_d = carry
        out = []
        j = steps // chunk - 1 - i
        for g in range(groups):
            r, after = chains[g]
            at = pl.multiple_of(g * length + j * (chunk * SUB), chunk * SUB)
            here = pl.ds(at, chunk * SUB)
            keep = keep_ref[here, :]
            parts = [None] * chunk
            for q in reversed(range(chunk)):
                r = after * r
                after = keep[q * SUB : (q + 1) * SUB]
                parts[q] = r
            state = local_ref[here, :] + jnp.concatenate(parts, axis=0)
            last = hidden_ref[(g + 1) * length - SUB : (g + 1) * length, :]
            wrapped = jnp.where(sub == 0, hin_ref[g : g + 1, :], pltpu.roll(last, 1, 0))
            before = pl.multiple_of(jnp.maximum(at - SUB, g * length), SUB)
            first = jnp.where(j == 0, wrapped, hidden_ref[pl.ds(before, SUB), :])
            rest = hidden_ref[pl.ds(at, (chunk - 1) * SUB), :]
            previous = jnp.concatenate([first, rest], axis=0)
            inner = pl.multiple_of(j * (chunk * SUB), chunk * SUB)
            conv = conv_bias + taps[0] * ext_ref[g, pl.ds(inner + 3 * SUB, chunk * SUB), :]
            for k in range(1, CONV):
                link = lanes(mask_ref[k, here, :], width)
                conv = conv + taps[k] * (link * ext_ref[g, pl.ds(inner + (3 - k) * SUB, chunk * SUB), :])
            rate, igate = rate_ref[here, :], igate_ref[here, :]
            space = 1.0 + 0.0001 - keep * keep
            inverse = lax.rsqrt(space)
            scaling = space * inverse
            both = state * igate
            dconv[here, :] = both * scaling
            with_conv = both * conv
            dlog = (state * previous - with_conv * (keep * inverse)) * keep
            dpre_a = (dlog * scale) * (rate * (1.0 - rate))
            dpre_i = (with_conv * scaling) * (1.0 - igate)
            low_a[here, :] = dpre_a.astype(BF16)
            low_i[here, :] = dpre_i.astype(BF16)
            rounded[here, :] = conv.astype(BF16)
            sum_a = sum_a + fold(dpre_a)
            sum_i = sum_i + fold(dpre_i)
            sum_d = sum_d + fold(dlog * rate)
            out.append((r, after))
        return tuple(out), sum_a, sum_i, sum_d

    _, sum_a, sum_i, sum_d = lax.fori_loop(0, steps // chunk, step, (tuple(start), zero, zero, zero))
    dvec_ref[5:6, :] = jnp.sum(sum_a, axis=0, keepdims=True)
    dvec_ref[6:7, :] = jnp.sum(sum_i, axis=0, keepdims=True)
    dvec_ref[7:8, :] = jnp.sum(sum_d, axis=0, keepdims=True)
    for h in range(width // LANES):
        col = slice(h * LANES, (h + 1) * LANES)
        dga_ref[h] = tn_dot(rounded[:, col], low_a[:, col])
        dgi_ref[h] = tn_dot(rounded[:, col], low_i[:, col])
        dconv[:, col] += nt_dot(low_a[:, col], ga_ref[h]) + nt_dot(low_i[:, col], gi_ref[h])

    sums = [zero] * (CONV + 1)
    for g in range(groups):

        def conv_step(i, carry, g=g):
            carry = list(carry)
            inner = pl.multiple_of(i * (chunk * SUB), chunk * SUB)
            here = pl.ds(pl.multiple_of(g * length + inner, chunk * SUB), chunk * SUB)
            d = dconv[here, :]
            carry[4] = carry[4] + fold(d)
            for k in range(CONV):
                masked = d if k == 0 else d * lanes(mask_ref[k, here, :], width)
                carry[k] = carry[k] + fold(masked * ext_ref[g, pl.ds(inner + (3 - k) * SUB, chunk * SUB), :])
            return tuple(carry)

        sums = list(lax.fori_loop(0, steps // chunk, conv_step, tuple(sums)))
        base = g * length
        tail = length - 3 * SUB
        total = taps[0] * dconv[base : base + tail, :]
        for k in range(1, CONV):
            there = slice(base + k * SUB, base + k * SUB + tail)
            total = total + taps[k] * (dconv[there, :] * lanes(mask_ref[k, there, :], width))
        din_ref[base : base + tail, :] = total

        def term(k, block):
            there = slice(base + block * SUB, base + (block + 1) * SUB)
            v = taps[k] * dconv[there, :]
            return v if k == 0 else v * lanes(mask_ref[k, there, :], width)

        heads = []
        for i in (3, 2, 1):
            j = steps - i
            value = term(0, j)
            head = None
            for k in range(1, CONV):
                if j + k < steps:
                    value = value + term(k, j + k)
                else:
                    t = term(k, j + k - steps)
                    value = value + jnp.where(sub == SUB - 1, 0.0, pltpu.roll(t, SUB - 1, 0))
                    head = t if head is None else head + t
            din_ref[base + j * SUB : base + (j + 1) * SUB, :] = value
            heads.append(head[0:1])
        head_ref[g * SUB : (g + 1) * SUB, :] = jnp.concatenate(heads + [jnp.zeros((SUB - 3, width), F32)], axis=0)
    for k in range(CONV + 1):
        dvec_ref[k : k + 1, :] = jnp.sum(sums[k], axis=0, keepdims=True)


def gates_back(local, keep, hidden, ext, rate, igate, sege, segf, gin, hin, gate_a, gate_i, vec, masks, groups, length):
    rows, recur = local.shape
    width = 512
    heads = width // LANES
    block = columns(rows, width)
    seg = columns(SUB * groups, width)
    gate = pl.BlockSpec((heads, LANES, LANES), lambda c: (c, 0, 0))
    return call(
        functools.partial(gates_back_kernel, groups, length),
        (recur // width,),
        [
            block, block, block, pl.BlockSpec((groups, length + 3 * SUB, width), lambda c: (0, 0, c)),
            block, block, seg, seg, columns(groups, width), columns(groups, width),
            gate, gate, columns(8, width), whole(masks.shape),
        ],
        [block, seg, gate, gate, columns(8, width)],
        [
            struct((rows, recur), F32), struct((SUB * groups, recur), F32), struct(gate_a.shape, F32),
            struct(gate_a.shape, F32), struct((8, recur), F32),
        ],
        [
            pltpu.VMEM((rows, width), F32), pltpu.VMEM((rows, width), BF16),
            pltpu.VMEM((rows, width), BF16), pltpu.VMEM((rows, width), BF16),
        ],
        rows * recur * 128 * 8 * 4,
        rows * recur * 28,
        (local, keep, hidden, ext, rate, igate, sege, segf, gin, hin, gate_a, gate_i, vec, masks),
    )


def branch_back_kernel(dbranch_ref, w_ref, out_ref):
    part = nt_dot(dbranch_ref[...], w_ref[...])

    @pl.when(pl.program_id(0) == 0)
    def _():
        out_ref[...] = part

    @pl.when(pl.program_id(0) > 0)
    def _():
        out_ref[...] += part


def branch_back(dbranch, w_in, first, dim):
    rows, recur = dbranch.shape
    width = 512
    return call(
        branch_back_kernel,
        (recur // width,),
        [columns(rows, width), columns(dim, width, first // width)],
        whole((rows, dim)),
        struct((rows, dim), F32),
        [],
        2 * rows * dim * recur,
        dim * recur * 2,
        (dbranch, w_in),
    )


def recur_in_back_kernel(
    groups, length,
    part_ref, din_ref, back_ref, wi_ref, x_ref, gain_ref, dmid_ref,
    low_ref, dx_ref, dgain_ref,
    acc,
):
    c = pl.program_id(0)
    width = din_ref.shape[1]
    rim = 4 * SUB
    sub = lax.broadcasted_iota(jnp.int32, (SUB, width), 0)
    for g in range(groups):
        base = g * length
        if length > rim:
            low_ref[base : base + length - rim, :] = din_ref[base : base + length - rim, :].astype(BF16)
        extra = [jnp.zeros((SUB, width), F32)]
        for i in range(3):
            extra.append(jnp.where(sub == SUB - 1, back_ref[g * SUB + i : g * SUB + i + 1, :], 0.0))
        tail = slice(base + length - rim, base + length)
        low_ref[tail, :] = (din_ref[tail, :] + jnp.concatenate(extra, axis=0)).astype(BF16)
    part = nt_dot(low_ref[...], wi_ref[...])

    @pl.when(c == 0)
    def _():
        acc[...] = part_ref[...] + part

    @pl.when(c > 0)
    def _():
        acc[...] += part

    @pl.when(c == pl.num_programs(0) - 1)
    def _():
        back, dgain = norm_back(x_ref[...].astype(F32), gain_ref[...], acc[...])
        dx_ref[...] = (dmid_ref[...] + back).astype(BF16)
        dgain_ref[...] = dgain


def recur_in_back(part, din, back, w_in, first, x, gain, dmid, groups, length):
    rows, dim = x.shape
    recur = din.shape[1]
    width = 512
    block = columns(rows, width)
    full = whole((rows, dim))
    return call(
        functools.partial(recur_in_back_kernel, groups, length),
        (recur // width,),
        [
            full, block, columns(SUB * groups, width), columns(dim, width, (first + recur) // width),
            full, whole(gain.shape), full,
        ],
        [block, full, whole((1, dim))],
        [struct((rows, recur), BF16), struct((rows, dim), BF16), struct((1, dim), F32)],
        [pltpu.VMEM((rows, dim), F32)],
        2 * rows * dim * recur * 1.5,
        2 * dim * recur + rows * recur * 8,
        (part, din, back, w_in, x, gain, dmid),
    )


def outer_kernel(places, pieces, place_ref, left_a, left_b, right_a, right_b, *refs):
    outs, (keep, send) = refs[:-2], refs[-2:]
    n, fs, share = places
    rows = left_a.shape[1]
    c = pl.program_id(0)
    per = pl.num_programs(0) // pieces

    @pl.when(c == 0)
    def _():
        core, y = place_ref[0], place_ref[1]
        for at in range(n):
            there = slice(at * share, (at + 1) * share)
            for scratch, side in ((keep, y), (send, 1 - y)):
                first = pl.multiple_of((at * fs + 2 * side + core) * share, share)
                scratch[there, 0:rows] = left_a[pl.ds(first, share), :]
                scratch[there, rows : 2 * rows] = left_b[pl.ds(first, share), :]

    right = jnp.concatenate([right_a[0], right_b[0]], axis=0)
    to_keep = nn_dot(keep[...], right).astype(BF16)
    to_send = nn_dot(send[...], right).astype(BF16)
    for p in range(pieces):

        @pl.when(c // per == p)
        def _(p=p):
            outs[2 * p][...] = to_keep
            outs[2 * p + 1][...] = to_send


def outer(lefts, at, k, rights, pieces, chosen, place, n, fs):
    rows = lefts[0].shape[1]
    count, _, total = rights[0].shape
    share = k // (n * fs)
    piece = count * total // pieces
    width = next(w for w in (768, 512, 384, 256, 128, piece) if piece % w == 0)
    across, per = total // width, piece // width
    skipped, pieces = chosen[0] * per, chosen[1]

    def out_block(p):
        return pl.BlockSpec((n * share, width), lambda c, place: (0, jnp.clip(c - p * per, 0, per - 1)))

    left = pl.BlockSpec((k, rows), lambda c, place: (at // k, 0))
    right = pl.BlockSpec((1, rows, width), lambda c, place: ((c + skipped) // across, 0, (c + skipped) % across))
    outs = pl.pallas_call(
        functools.partial(outer_kernel, (n, fs, share), pieces),
        grid_spec=pltpu.PrefetchScalarGridSpec(
            num_scalar_prefetch=1,
            grid=(pieces * per,),
            in_specs=[left, left, right, right],
            out_specs=[out_block(p) for p in range(pieces) for _ in range(2)],
            scratch_shapes=[pltpu.VMEM((n * share, 2 * rows), BF16)] * 2,
        ),
        out_shape=[struct((n * share, piece), BF16)] * (2 * pieces),
        compiler_params=pltpu.CompilerParams(dimension_semantics=("arbitrary",), vmem_limit_bytes=VMEM_BYTES),
        cost_estimate=pl.CostEstimate(
            flops=8 * n * share * rows * pieces * piece // COST, bytes_accessed=1, transcendentals=0
        ),
    )(place, *lefts, *rights)
    return [(outs[2 * p], outs[2 * p + 1]) for p in range(pieces)]


def unfold_kernel(folded_ref, out_ref):
    height, width = folded_ref.shape[0], out_ref.shape[1]
    for q in range(out_ref.shape[0] // height):
        out_ref[q * height : (q + 1) * height, :] = folded_ref[:, q * width : (q + 1) * width]


def unfold_first(packed, places, height, rows, width):
    return call(
        unfold_kernel,
        (places,),
        [pl.BlockSpec((height, rows // height * width), lambda c: (c, 0))],
        pl.BlockSpec((rows, width), lambda c: (c, 0)),
        struct((places * rows, width), packed.dtype),
        [],
        0,
        places * rows * width * 4,
        (packed,),
    )


def shifted(value, axis, by):
    length = lax.axis_size(axis)
    pairs = [(i, i + by) for i in range(length) if 0 <= i + by < length]
    return lax.ppermute(value, axis, pairs)


def entering(agg, groups, reverse):
    n = lax.axis_size("seq")
    sign = -1 if reverse else 1
    got = {k: shifted(agg, "seq", sign * k) for k in range(1, n)}
    state = jnp.zeros((groups, agg.shape[1]), F32)
    for k in range(n - 1, 0, -1):
        part = got[k].reshape(groups, 2, -1)
        state = part[:, 0] * state + part[:, 1]
    return state


def add(*parts):
    return functools.reduce(jnp.add, [p.astype(F32) for p in parts])


def line_sum(slots, mine, n, send):
    def at(offset):
        return slots((mine + offset) % n)

    up, down = at(n - 1), at(1)
    for s in range(1, n):
        got_up = send(up, [(i, i + 1) for i in range(s)])
        got_down = send(down, [(i, i - 1) for i in range(n - s, n)])
        if s < n - 1:
            up = add(at(n - 1 - s), got_up).astype(BF16)
            down = add(at(s + 1), got_down).astype(BF16)
    return add(at(0), got_up, got_down)


class Scatter:
    def __init__(self):
        self.n, self.fs = lax.axis_size("seq"), lax.axis_size("fsdp")
        self.ny = self.fs // 2
        self.z, f = lax.axis_index("seq"), lax.axis_index("fsdp")
        self.y, self.core = f // 2, f % 2

    def core_swap(self, value):
        return lax.ppermute(value, "fsdp", [(i, i ^ 1) for i in range(self.fs)])

    def y_send(self, value, pairs):
        return lax.ppermute(value, "fsdp", [(2 * a + c, 2 * b + c) for a, b in pairs for c in range(2)])

    def over_y(self, keep, send, since, beside):
        return add(after(keep, beside), self.y_send(after(send, since), [(0, 1), (1, 0)])).astype(BF16)

    def over_z(self, shares):
        return lax.psum_scatter(shares, "seq", scatter_dimension=0, tiled=True)[0].astype(F32)


def pick(value, index, axis):
    return lax.dynamic_index_in_dim(value, index, axis, keepdims=False)


def reorder(v):
    length, d = v.shape[-2:]
    return jnp.swapaxes(v.reshape(-1, SUB, length // SUB, d), 1, 2).reshape(-1, d)


def restore(v, shape):
    length, d = shape[-2:]
    return jnp.swapaxes(v.reshape(-1, length // SUB, SUB, d), 1, 2).reshape(shape)


def tail_rows(v, groups, length):
    d = v.shape[1]
    last = v.reshape(groups, length // SUB, SUB, d)[:, length // SUB - 3 :, SUB - 1]
    last = jnp.pad(last, ((0, 0), (0, SUB - 3), (0, 0))).reshape(groups * SUB, d)
    return jnp.pad(last, ((0, -groups * SUB % 16), (0, 0)))


def fold_rows(v, height):
    count = -(-v.shape[0] // height)
    v = jnp.pad(v, ((0, count * height - v.shape[0]), (0, 0)))
    return jnp.concatenate([v[i * height : (i + 1) * height] for i in range(count)], axis=1)


def fold_places(v, height):
    places, rows, width = v.shape
    count = -(-rows // height)
    v = jnp.pad(v, ((0, 0), (0, count * height - rows), (0, 0))).reshape(places, count, height, width)
    return jnp.swapaxes(v, 1, 2).reshape(places, height, count * width)


def unfold_rows(v, rows, width):
    places, height, total = v.shape
    v = jnp.swapaxes(v.reshape(places, height, total // width, width), 1, 2)
    return v.reshape(places, -1, width)[:, :rows]


def after(value, *others):
    return lax.optimization_barrier((value, others))[0]


def gather(shard):
    return lax.all_gather(shard, ("seq", "fsdp"), axis=0, tiled=True)


def body(
    ends, segment_ids, norm_one, w_branch, w_input, conv_weight, conv_bias, gate_a, gate_i, bias_a, bias_i,
    decay, w_out, norm_two, w_gate, w_up, w_down,
):
    is_first = lax.axis_index("section") == 0
    z = lax.axis_index("seq")
    n, fs = lax.axis_size("seq"), lax.axis_size("fsdp")
    places = n * fs
    micro, seqs, length, dim = ends.shape[1:]
    parts_of = 1
    groups = micro * seqs // parts_of
    rows = groups * length
    recur = w_branch.shape[2]
    heads, part, block = gate_a.shape[1:]
    hidden_dim = w_gate.shape[2]

    dshare, rshare = dim // places, recur // places
    vectors = [norm_one, norm_two] + [conv_weight[:, k] for k in range(CONV)] + [conv_bias, bias_a, bias_i, decay]
    vectors = jnp.concatenate([jnp.pad(v, ((0, 0), (0, LANES - v.shape[1]))) for v in vectors], axis=0)
    vectors = jnp.pad(vectors, ((0, 2 * SUB - vectors.shape[0]), (0, 0)))
    small = jnp.concatenate([vectors, gate_a.reshape(-1, block), gate_i.reshape(-1, block)], axis=0)
    small_rows = small.shape[0]
    small = fold_rows(small, dshare)
    first = hidden_dim
    w_in = gather(
        jnp.concatenate(
            [fold_rows(w_down[0], dshare), w_branch[0], w_input[0], w_out[0].reshape(dshare, recur), small], axis=1
        )
    )
    w_gu = gather(jnp.concatenate([after(w_gate[0], small), w_up[0]], axis=1))
    w_out_all = w_in[:, first + 2 * recur : first + 3 * recur].reshape(recur, dim)
    small = unfold_rows(w_in[:, first + 3 * recur :].reshape(places, dshare, -1), small_rows, LANES)
    hshare = hidden_dim // places
    if dshare % 16 == 0:
        w_down_all = unfold_first(w_in, places, dshare, hshare, dim)
    else:
        w_down_all = unfold_rows(w_in[:, :first].reshape(places, dshare, -1), hshare, dim).reshape(hidden_dim, dim)

    def vector(row, share):
        return small[:, row, :share].reshape(1, places * share).astype(F32)

    gain_one, gain_two = vector(0, dshare), vector(1, dshare)
    decays = vector(9, rshare)
    vec = jnp.concatenate([vector(r, rshare) for r in range(2, 9)] + [-8.0 * jax.nn.softplus(decays)], axis=0)
    gates_a, gates_i = [
        jnp.swapaxes(small[:, r : r + heads * part].reshape(places, heads, part, block), 0, 1).reshape(heads, block, block)
        for r in (2 * SUB, 2 * SUB + heads * part)
    ]

    padded_ids = jnp.pad(segment_ids, ((0, 0), (0, 0), (CONV - 1, 0)), constant_values=-1)
    window = lax.dynamic_slice_in_dim(padded_ids, z * length, length + CONV - 1, axis=2)
    current = window[:, :, CONV - 1 :]
    masks = jnp.stack(
        [window[:, :, CONV - 1 - k : CONV - 1 - k + length] == current for k in (1, 1, 2, 3)]
    ).astype(F32)
    masks = jnp.swapaxes(masks.reshape(4, parts_of, groups, SUB, length // SUB), 3, 4).reshape(4, parts_of, rows, 1)
    masks = jnp.broadcast_to(masks, (4, parts_of, rows, LANES))
    masks = [masks[:, m] for m in range(parts_of)]
    micros = range(parts_of)

    def forward(xs, halos, save):
        got = []
        for m in micros:
            got.append(recur_in(xs[m], halos[m], gain_one, w_in, first, gates_a, gates_i, vec, masks[m], groups, length))
        hin = entering(jnp.concatenate([g[7] for g in got], axis=0), parts_of * groups, False)
        acts = [branch_in(after(g[0], got[-1][7]), w_in, first, recur) for g in got]
        outs, saved = [], []
        for m in micros:
            normed, ext, rate, igate, keep, local, segp, _ = got[m]
            act, slope = acts[m]
            mine = hin[m * groups : (m + 1) * groups]
            if m:
                keep = after(keep, outs[-1])
            hidden, mixed, middle, normed_two = recur_out(
                xs[m], keep, local, act, segp, mine, w_out_all, gain_two, groups, length
            )
            results = feed_forward(normed_two, middle, w_gu, w_down_all, save)
            outs.append(results[-1])
            saved.append(
                (normed, ext, rate, igate, keep, mine, hidden, mixed, middle, normed_two, act, slope) + tuple(results[:-1])
            )
        return outs, saved

    def back_ff(m, dout, saved, dproduct=None):
        return feed_forward_back(dout, saved[m][8], gain_two, saved[m][12], saved[m][13], w_gu, w_down_all, dproduct)

    def back_mix(m, low, saved):
        return mix_back(low, w_out_all, saved[m][10], saved[m][11], saved[m][6], saved[m][4], groups, length)

    def back_gates(m, mixed_back, gin, saved):
        normed, ext, rate, igate, keep, hin, hidden = saved[m][:7]
        _, local, sege, segf, _ = mixed_back
        din, head, dga, dgi, dvec = gates_back(
            local, keep, hidden, ext, rate, igate, sege, segf, gin[m * groups : (m + 1) * groups], hin,
            gates_a, gates_i, vec, masks[m], groups, length,
        )
        return din, shifted(head, "seq", -1), dga, dgi, dvec

    def back_in(m, part, gates, dmid, xs):
        return recur_in_back(part, gates[0], gates[1], w_in, first, xs[m], gain_one, dmid, groups, length)

    own = [reorder(v) for v in ends[0].reshape((parts_of, -1) + ends.shape[3:])]
    tails = [shifted(tail_rows(v, groups, length), "seq", 1) for v in own]
    outs, _ = forward(own, tails, False)
    xs, halos = [], []
    for m in micros:
        dproduct = down_back(after(own[m], outs[m]), w_down_all)
        received = after(shifted(outs[m], "section", 1), dproduct)
        received_halo = lax.ppermute(
            tail_rows(outs[m], groups, length), ("section", "seq"), [(i, n + i + 1) for i in range(n - 1)]
        )
        xs.append(jnp.where(is_first, own[m], received))
        halos.append(jnp.where(is_first, tails[m], received_halo))
    outs, saved = forward(xs, halos, True)

    scatter = Scatter()
    swap = scatter.core_swap
    place = jnp.stack([scatter.core, scatter.y]).astype(jnp.int32)

    ff = back_ff(0, own[0], saved, dproduct)
    mix = back_mix(0, ff[2], saved)
    gin = entering(mix[4], groups, True)
    product_t = saved[0][14]
    product_pair = (product_t, swap(after(product_t, mix[4])))
    gates = back_gates(0, mix, gin, saved)
    base = branch_back(after(mix[0], gates[0]), w_in, first, dim)
    dx = back_in(0, base, gates, ff[1], xs)[1]
    others = [after(saved[0][i], dx) for i in (9, 0, 7)]
    starts_at, total_rows = [], 0
    for i, v in enumerate(others):
        gap = -total_rows % v.shape[1]
        if gap:
            others[i] = jnp.concatenate([jnp.zeros((rows, gap), BF16), v], axis=1)
        starts_at.append((total_rows + gap, v.shape[1]))
        total_rows += gap + v.shape[1]
    others = jnp.concatenate([v.T for v in others], axis=0)
    received = after(shifted(dx, "section", -1), others, product_pair)
    others = after(others, received)
    others = (others, swap(others))
    lefts = {"product": (product_pair, 0, hidden_dim)}
    for name, (at, k) in zip(("two", "one", "mixed"), starts_at):
        lefts[name] = (others, at, k)
    dout = jnp.where(is_first, received, own[0])

    def pair(value):
        value = value if value.ndim == 3 else value[None]
        return value, swap(value)

    def products(name, rights, pieces=1, chosen=None):
        both, at, k = lefts[name]
        chosen = chosen or (0, pieces)
        if scatter.ny == 2:
            return outer(both, at, k, rights, pieces, chosen, place, n, fs)
        left = jnp.concatenate([v[at : at + k] for v in both], axis=1)
        right = jnp.concatenate([jnp.concatenate(list(v), axis=1) for v in rights], axis=0)
        grad = nn_dot(left, right).astype(BF16)
        grad = pick(grad.reshape(n, scatter.ny, 2, -1, grad.shape[1]), scatter.core, 2)
        return [(p,) for p in jnp.split(grad, pieces, axis=3)[chosen[0] : sum(chosen)]]

    def over_y(grads, since, *beside):
        if scatter.ny == 2:
            return scatter.over_y(*[g.reshape(n, -1, g.shape[1]) for g in grads], since, beside)
        (grad,) = grads
        return line_sum(lambda d: pick(grad, d, 1), scatter.y, scatter.ny, scatter.y_send).astype(BF16)

    down = products("product", pair(dout), 2)
    dgu, dmid, out_low, dgain_two = back_ff(0, after(dout, down), saved)
    down_sums = [over_y(down[0], (), out_low)]
    down_sums.append(None)
    gu_pair = pair(after(dgu, down_sums[0]))
    mix = back_mix(0, after(out_low, down_sums[0]), saved)
    gate_up = products("two", after(gu_pair, mix[0]), 4, (0, 1))
    down_sums[1] = over_y(down[1], out_low, gate_up[0])
    gin = entering(after(mix[4], down_sums[1]), groups, True)
    gate_up += products("two", after(gu_pair, down_sums[1]), 4, (1, 3))
    gate_up_sums = [over_y(gate_up[0], (), gate_up[1], gin)]
    gates = back_gates(0, after(mix, gate_up_sums[0]), gin, saved)
    gate_up_sums.append(over_y(gate_up[1], gin, gates[0]))
    out_low, dbranch = after((out_low, mix[0]), gate_up_sums[1])
    out_pair, branch_pair = pair(out_low), pair(dbranch)
    base = branch_back(dbranch, w_in, first, dim)
    results = back_in(0, base, gates, dmid, xs)
    gate_up_sums.append(over_y(gate_up[2], gates[0], results[1], out_pair[1], branch_pair[1]))
    input_pair = pair(after(results[0], gate_up_sums[2]))
    out = products("mixed", after(out_pair, gate_up_sums[2]))
    branch = products("one", after(branch_pair, out))
    dgain_one = results[2]
    dga, dgi, dvec = gates[2:5]
    ddecay = -8.0 * jax.nn.sigmoid(decays) * dvec[7:8]
    shares = [dgain_one, dgain_two] + [dvec[k : k + 1] for k in range(7)] + [ddecay]
    shares = [v.reshape(places, 1, -1) for v in shares]
    shares = [jnp.pad(v, ((0, 0), (0, 0), (0, LANES - v.shape[2]))) for v in shares]
    shares = jnp.pad(jnp.concatenate(shares, axis=1), ((0, 0), (0, 2 * SUB - len(shares)), (0, 0)))
    packed = jnp.concatenate(
        [shares]
        + [jnp.swapaxes(v.reshape(heads, places, part, block), 0, 1).reshape(places, -1, block) for v in (dga, dgi)],
        axis=1,
    )
    extra = fold_places(packed, dshare).reshape(n, scatter.ny, 2, dshare, -1)
    theirs = swap(pick(extra, 1 - scatter.core, 2).astype(BF16))
    extra = add(pick(extra, scatter.core, 2), theirs).astype(BF16)
    gate_up_sums.append(over_y(gate_up[3], results[1], branch, extra))
    into = products("one", after(input_pair, gate_up_sums[3]))
    out_sum = over_y(out[0], branch, into)
    if scatter.ny == 2:
        sides = (pick(extra, scatter.y, 1), pick(extra, 1 - scatter.y, 1))
        last = [
            jnp.concatenate([g.reshape(n, dshare, -1), v], axis=2).reshape(n * dshare, -1) for g, v in zip(into[0], sides)
        ]
    else:
        last = (jnp.concatenate([into[0][0], extra], axis=3),)
    branch_sum = over_y(branch[0], out_sum, last)
    input_sum = over_y(last, branch_sum)

    outputs = restore(outs[0], ends.shape)
    input_grads = restore(results[1], ends.shape)
    shares = down_sums + gate_up_sums + [out_sum, branch_sum, input_sum]
    for i in range(1, len(shares)):
        shares[i] = after(shares[i], shares[i - 1])
    totals = [scatter.over_z(v) for v in shares]
    sum_down, sum_gate, sum_up = [jnp.concatenate(totals[i : i + 2], axis=1) for i in (0, 2, 4)]
    sum_out, sum_branch, sum_input = totals[6:]
    sum_input, sums = sum_input[:, :recur], sum_input[:, recur:]
    sums = unfold_rows(sums[None], small_rows, LANES)[0]
    gate_sums = [sums[r : r + heads * part].reshape(gate_a.shape) for r in (2 * SUB, 2 * SUB + heads * part)]

    return (
        outputs,
        input_grads,
        sums[0:1, :dshare],
        sum_branch[None],
        sum_input[None],
        sums[2 : 2 + CONV, :rshare][None],
        sums[6:7, :rshare],
        gate_sums[0],
        gate_sums[1],
        sums[7:8, :rshare],
        sums[8:9, :rshare],
        sums[9:10, :rshare],
        sum_out[None],
        sums[1:2, :dshare],
        sum_gate[None],
        sum_up[None],
        sum_down[None],
    )


def solution(mesh):
    tokens = P("section", None, "fsdp", "seq", None)
    vector = P("section", ("seq", "fsdp"))
    matrix = P("section", ("seq", "fsdp"), None)
    taps = P("section", None, ("seq", "fsdp"))
    gates = P("section", None, ("seq", "fsdp"), None)
    weights = (
        vector, matrix, matrix, taps, vector, gates, gates, vector, vector, vector, matrix, vector, matrix, matrix, matrix,
    )
    return jax.shard_map(
        body,
        mesh=mesh,
        in_specs=(tokens, P(None, "fsdp", None)) + weights,
        out_specs=(tokens, tokens) + weights,
        check_vma=False,
    )
```

```python
import functools

import jax
import jax.numpy as jnp
from jax import lax
from jax.experimental import pallas as pl
from jax.experimental.pallas import tpu as pltpu
from jax.sharding import PartitionSpec as P

CONV = 4
EPS = 1e-06
F32 = jnp.float32
BF16 = jnp.bfloat16
VMEM_BYTES = 56 << 20
LANES = 128
SUB = 8
COST = 4


def nn_dot(a, b):
    return lax.dot_general(a, b, (((1,), (0,)), ((), ())), preferred_element_type=F32)


def nt_dot(a, b):
    return lax.dot_general(a, b, (((1,), (1,)), ((), ())), preferred_element_type=F32)


def tn_dot(a, b):
    return lax.dot_general(a, b, (((0,), (0,)), ((), ())), preferred_element_type=F32)


def sigmoid(v):
    return 0.5 * jnp.tanh(0.5 * v) + 0.5


K0 = 0.7978845608028654
K1 = 0.044715


def gelu(v):
    return 0.5 * v * (1.0 + jnp.tanh(K0 * (v + K1 * v * v * v)))


def gelu_both(v):
    square = v * v
    t = jnp.tanh(K0 * v * (1.0 + K1 * square))
    half = 0.5 * (1.0 + t)
    slope = half + (0.5 * K0) * v * (1.0 - t * t) * (1.0 + (3.0 * K1) * square)
    return v * half, slope


def lanes(mask, width):
    return jnp.concatenate([mask] * (width // LANES), axis=1) if width > LANES else mask


def call(kernel, grid, in_specs, out_specs, out_shape, scratch, flops, bytes_accessed, args):
    return pl.pallas_call(
        kernel,
        grid=grid,
        in_specs=in_specs,
        out_specs=out_specs,
        out_shape=out_shape,
        scratch_shapes=scratch,
        compiler_params=pltpu.CompilerParams(
            dimension_semantics=("arbitrary",) * len(grid), vmem_limit_bytes=VMEM_BYTES
        ),
        cost_estimate=pl.CostEstimate(
            flops=int(flops) // COST, bytes_accessed=int(bytes_accessed) // COST, transcendentals=0
        ),
    )(*args)


def whole(shape):
    return pl.BlockSpec(shape, lambda c: (0,) * len(shape))


def columns(rows, width, offset=0):
    return pl.BlockSpec((rows, width), lambda c: (0, c + offset))


def struct(shape, dtype):
    return jax.ShapeDtypeStruct(shape, dtype)


def recur_in_kernel(
    groups, length,
    x_ref, halo_ref, gain_ref, wi_ref, ga_ref, gi_ref, vec_ref, mask_ref,
    normed_ref, ext_ref, rate_ref, igate_ref, keep_ref, local_ref, segp_ref, agg_ref,
    xn, conv, pre_a, pre_i,
):
    rows = groups * length
    steps = length // SUB
    width = wi_ref.shape[1]

    @pl.when(pl.program_id(0) == 0)
    def _():
        gain = gain_ref[...]
        for at, ref in ((0, x_ref), (rows, halo_ref)):
            v = ref[...].astype(F32)
            r = lax.rsqrt(jnp.mean(v * v, axis=-1, keepdims=True) + EPS)
            xn[at : at + ref.shape[0], :] = (v * r * gain).astype(BF16)
        normed_ref[...] = xn[0:rows, :]

    conv_in = nn_dot(xn[...], wi_ref[...]).astype(BF16).astype(F32)
    sub = lax.broadcasted_iota(jnp.int32, (SUB, width), 0)
    for g in range(groups):
        base = conv_in[g * length : (g + 1) * length]
        halo = conv_in[rows + g * SUB : rows + (g + 1) * SUB]
        for k in (3, 2, 1):
            block = pltpu.roll(base[(steps - k) * SUB : (steps - k + 1) * SUB], 1, 0)
            ext_ref[g, (3 - k) * SUB : (4 - k) * SUB, :] = jnp.where(sub == 0, halo[3 - k : 4 - k], block)
        ext_ref[g, 3 * SUB : 3 * SUB + length, :] = base
    taps = [vec_ref[k : k + 1, :] for k in range(CONV)]
    for g in range(groups):
        part = slice(g * length, (g + 1) * length)
        out = vec_ref[4:5, :] + taps[0] * ext_ref[g, 3 * SUB : 3 * SUB + length, :]
        for k in range(1, CONV):
            link = lanes(mask_ref[k, part, :], width)
            out = out + taps[k] * (link * ext_ref[g, (3 - k) * SUB : (3 - k) * SUB + length, :])
        conv[part, :] = out
    rounded = conv[...].astype(BF16)
    for h in range(width // LANES):
        col = slice(h * LANES, (h + 1) * LANES)
        pre_a[:, col] = nn_dot(rounded[:, col], ga_ref[h])
        pre_i[:, col] = nn_dot(rounded[:, col], gi_ref[h])
    bias_a, bias_i, scale = vec_ref[5:6, :], vec_ref[6:7, :], vec_ref[7:8, :]
    chunk = 4

    def step(i, carry):
        out = []
        for g in range(groups):
            h, p = carry[g]
            at = pl.multiple_of(g * length + i * (chunk * SUB), chunk * SUB)
            here = pl.ds(at, chunk * SUB)
            rate = sigmoid(pre_a[here, :] + bias_a)
            igate = sigmoid(pre_i[here, :] + bias_i)
            keep = jnp.exp(scale * rate) * lanes(mask_ref[0, here, :], width)
            driven = igate * conv[here, :] * jnp.sqrt(1.0 + 0.0001 - keep * keep)
            rate_ref[here, :] = rate
            igate_ref[here, :] = igate
            keep_ref[here, :] = keep
            states = []
            for q in range(chunk):
                kq = keep[q * SUB : (q + 1) * SUB]
                h = kq * h + driven[q * SUB : (q + 1) * SUB]
                p = kq * p
                states.append(h)
            local_ref[here, :] = jnp.concatenate(states, axis=0)
            out.append((h, p))
        return tuple(out)

    start = tuple((jnp.zeros((SUB, width), F32), jnp.ones((SUB, width), F32)) for _ in range(groups))
    done = lax.fori_loop(0, steps // chunk, step, start)
    for g in range(groups):
        h, p = done[g]
        segp_ref[g * SUB : (g + 1) * SUB, :] = p
        a, b = jnp.ones((1, width), F32), jnp.zeros((1, width), F32)
        for s in range(SUB):
            b = p[s : s + 1] * b + h[s : s + 1]
            a = p[s : s + 1] * a
        agg_ref[2 * g : 2 * g + 1, :] = a
        agg_ref[2 * g + 1 : 2 * g + 2, :] = b


def recur_in(x, halo, gain, w_in, first, gate_a, gate_i, vec, masks, groups, length):
    rows, dim = x.shape
    recur = vec.shape[1]
    width = 512
    blocks = recur // width
    block_f32 = columns(rows, width)
    heads = width // LANES
    ext_len = length + 3 * SUB
    return call(
        functools.partial(recur_in_kernel, groups, length),
        (blocks,),
        [
            whole(x.shape), whole(halo.shape), whole(gain.shape),
            columns(dim, width, (first + recur) // width),
            pl.BlockSpec((heads, LANES, LANES), lambda c: (c, 0, 0)),
            pl.BlockSpec((heads, LANES, LANES), lambda c: (c, 0, 0)),
            columns(8, width), whole(masks.shape),
        ],
        [
            whole((rows, dim)),
            pl.BlockSpec((groups, ext_len, width), lambda c: (0, 0, c)),
            block_f32, block_f32, block_f32, block_f32,
            columns(SUB * groups, width), columns(2 * groups, width),
        ],
        [
            struct((rows, dim), BF16), struct((groups, ext_len, recur), F32),
            struct((rows, recur), F32), struct((rows, recur), F32), struct((rows, recur), F32),
            struct((rows, recur), F32), struct((SUB * groups, recur), F32), struct((2 * groups, recur), F32),
        ],
        [
            pltpu.VMEM((rows + halo.shape[0], dim), BF16), pltpu.VMEM((rows, width), F32),
            pltpu.VMEM((rows, width), F32), pltpu.VMEM((rows, width), F32),
        ],
        2 * rows * dim * recur * 2.5,
        dim * recur * 2 + rows * recur * 4 * 5,
        (x, halo, gain, w_in, gate_a, gate_i, vec, masks),
    )


def branch_kernel(x_ref, w_ref, act_ref, slope_ref):
    act, slope = gelu_both(nn_dot(x_ref[...], w_ref[...]))
    act_ref[...] = act
    slope_ref[...] = slope


def branch_in(x, w_in, first, recur):
    rows, dim = x.shape
    width = 512
    block = columns(rows, width)
    return call(
        branch_kernel,
        (recur // width,),
        [whole(x.shape), columns(dim, width, first // width)],
        [block, block],
        [struct((rows, recur), F32)] * 2,
        [],
        2 * rows * dim * recur * 1.5,
        dim * recur * 2 + rows * recur * 8,
        (x, w_in),
    )


def recur_out_kernel(
    groups, length,
    x_ref, keep_ref, local_ref, act_ref, segp_ref, hin_ref, wo_ref, gain_ref,
    hidden_ref, mixed_ref, middle_ref, normed_ref,
    acc,
):
    steps = length // SUB
    width = keep_ref.shape[1]
    chunk = 4
    c = pl.program_id(0)
    start = []
    for g in range(groups):
        ends = local_ref[(g + 1) * length - SUB : (g + 1) * length, :]
        prods = segp_ref[g * SUB : (g + 1) * SUB, :]
        state = hin_ref[g : g + 1, :]
        entering = []
        for s in range(SUB):
            entering.append(state)
            state = prods[s : s + 1] * state + ends[s : s + 1]
        start.append(jnp.concatenate(entering, axis=0))

    def step(i, carry):
        out = []
        for g in range(groups):
            q = carry[g]
            at = pl.multiple_of(g * length + i * (chunk * SUB), chunk * SUB)
            here = pl.ds(at, chunk * SUB)
            keep = keep_ref[here, :]
            moved = []
            for r in range(chunk):
                q = keep[r * SUB : (r + 1) * SUB] * q
                moved.append(q)
            hidden = local_ref[here, :] + jnp.concatenate(moved, axis=0)
            hidden_ref[here, :] = hidden
            mixed_ref[here, :] = (hidden * act_ref[here, :]).astype(BF16)
            out.append(q)
        return tuple(out)

    lax.fori_loop(0, steps // chunk, step, tuple(start))
    part = nn_dot(mixed_ref[...], wo_ref[...])

    @pl.when(c == 0)
    def _():
        acc[...] = x_ref[...].astype(F32) + part

    @pl.when(c > 0)
    def _():
        acc[...] += part

    @pl.when(c == pl.num_programs(0) - 1)
    def _():
        m = acc[...]
        middle_ref[...] = m
        r = lax.rsqrt(jnp.mean(m * m, axis=-1, keepdims=True) + EPS)
        normed_ref[...] = (m * r * gain_ref[...]).astype(BF16)


def recur_out(x, keep, local, act, segp, hin, w_out, gain, groups, length):
    rows, dim = x.shape
    recur = keep.shape[1]
    width = 512
    block = columns(rows, width)
    return call(
        functools.partial(recur_out_kernel, groups, length),
        (recur // width,),
        [
            whole(x.shape), block, block, block, columns(SUB * groups, width), columns(groups, width),
            pl.BlockSpec((width, dim), lambda c: (c, 0)), whole(gain.shape),
        ],
        [block, block, whole((rows, dim)), whole((rows, dim))],
        [
            struct((rows, recur), F32), struct((rows, recur), BF16),
            struct((rows, dim), F32), struct((rows, dim), BF16),
        ],
        [pltpu.VMEM((rows, dim), F32)],
        2 * rows * dim * recur * 1.5,
        dim * recur * 2 + rows * recur * 18,
        (x, keep, local, act, segp, hin, w_out, gain),
    )


def ff_kernel(save, x_ref, mid_ref, wg_ref, wu_ref, wd_ref, *refs):
    c = pl.program_id(0)
    out_ref, acc = refs[-2:]
    x = x_ref[...]
    gate = nn_dot(x, wg_ref[...])
    up = nn_dot(x, wu_ref[...])
    if save:
        act_ref, slope_ref, product_ref = refs[:3]
        act, slope = gelu_both(gate)
        act_ref[...] = act.astype(BF16)
        slope_ref[...] = (up * slope).astype(BF16)
        product = (act * up).astype(BF16)
        product_ref[...] = product.T
    else:
        product = (gelu(gate) * up).astype(BF16)
    part = nn_dot(product, wd_ref[...])

    @pl.when(c == 0)
    def _():
        acc[...] = mid_ref[...] + part

    @pl.when(c > 0)
    def _():
        acc[...] += part

    @pl.when(c == pl.num_programs(0) - 1)
    def _():
        out_ref[...] = acc[...].astype(BF16)


def feed_forward(x, middle, w_gu, w_down, save):
    rows, dim = x.shape
    hidden = w_down.shape[0]
    width = 512
    blocks = hidden // width
    block = columns(rows, width)
    return call(
        functools.partial(ff_kernel, save),
        (blocks,),
        [
            whole(x.shape), whole(middle.shape), columns(dim, width), columns(dim, width, blocks),
            pl.BlockSpec((width, dim), lambda c: (c, 0)),
        ],
        ([block] * 2 + [pl.BlockSpec((width, rows), lambda c: (c, 0))] if save else []) + [whole((rows, dim))],
        ([struct((rows, hidden), BF16)] * 2 + [struct((hidden, rows), BF16)] if save else [])
        + [struct((rows, dim), BF16)],
        [pltpu.VMEM((rows, dim), F32)],
        6 * rows * dim * hidden * 1.5,
        6 * dim * hidden,
        (x, middle, w_gu, w_gu, w_down),
    )


def norm_back(values, gain, grad):
    q = lax.rsqrt(jnp.mean(values * values, axis=-1, keepdims=True) + EPS)
    t = gain * grad
    back = q * t - values * (q * q * q * jnp.mean(values * t, axis=-1, keepdims=True))
    return back, jnp.sum(values * q * grad, axis=0, keepdims=True)


def down_back_kernel(dout_ref, wd_ref, dproduct_ref):
    dproduct_ref[...] = nt_dot(dout_ref[...], wd_ref[...]).astype(BF16)


def down_back(dout, w_down):
    rows, dim = dout.shape
    hidden = w_down.shape[0]
    width = 512
    return call(
        down_back_kernel,
        (hidden // width,),
        [whole((rows, dim)), pl.BlockSpec((width, dim), lambda c: (c, 0))],
        columns(rows, width),
        struct((rows, hidden), BF16),
        [],
        2 * rows * dim * hidden,
        2 * dim * hidden + 4 * rows * hidden,
        (dout, w_down),
    )


def ff_back_kernel(
    ready,
    dout_ref, mid_ref, gain_ref, act_ref, slope_ref, wg_ref, wu_ref, wd_ref,
    dgu_ref, dmid_ref, low_ref, dgain_ref,
    acc,
):
    c = pl.program_id(0)
    dproduct = wd_ref[...].astype(F32) if ready else nt_dot(dout_ref[...], wd_ref[...])
    dgate = (dproduct * slope_ref[...].astype(F32)).astype(BF16)
    dup = (dproduct * act_ref[...].astype(F32)).astype(BF16)
    dgu_ref[0] = dgate
    dgu_ref[1] = dup
    part = nt_dot(dgate, wg_ref[...]) + nt_dot(dup, wu_ref[...])

    @pl.when(c == 0)
    def _():
        acc[...] = part

    @pl.when(c > 0)
    def _():
        acc[...] += part

    @pl.when(c == pl.num_programs(0) - 1)
    def _():
        back, dgain = norm_back(mid_ref[...], gain_ref[...], acc[...])
        dmid = dout_ref[...].astype(F32) + back
        dmid_ref[...] = dmid
        low_ref[...] = dmid.astype(BF16)
        dgain_ref[...] = dgain


def feed_forward_back(dout, middle, gain, act, slope, w_gu, w_down, dproduct=None):
    rows, dim = dout.shape
    hidden = w_down.shape[0]
    width = 512
    blocks = hidden // width
    block = columns(rows, width)
    full = whole((rows, dim))
    return call(
        functools.partial(ff_back_kernel, dproduct is not None),
        (blocks,),
        [
            full, full, whole(gain.shape), block, block, columns(dim, width), columns(dim, width, blocks),
            pl.BlockSpec((width, dim), lambda c: (c, 0)) if dproduct is None else block,
        ],
        [pl.BlockSpec((2, rows, width), lambda c: (0, 0, c)), full, full, whole((1, dim))],
        [
            struct((2, rows, hidden), BF16), struct((rows, dim), F32),
            struct((rows, dim), BF16), struct((1, dim), F32),
        ],
        [pltpu.VMEM((rows, dim), F32)],
        6 * rows * dim * hidden * 1.2,
        6 * dim * hidden,
        (dout, middle, gain, act, slope, w_gu, w_gu, w_down if dproduct is None else dproduct),
    )


def mix_back_kernel(
    groups, length,
    low_ref, wo_ref, act_ref, slope_ref, hidden_ref, keep_ref,
    dbranch_ref, local_ref, sege_ref, segf_ref, agg_ref,
    dmixed,
):
    steps = length // SUB
    width = keep_ref.shape[1]
    chunk = 4
    dmixed[...] = nt_dot(low_ref[...], wo_ref[...])

    def step(i, carry):
        out = []
        for g in range(groups):
            s, p, after = carry[g]
            at = pl.multiple_of(g * length + (steps // chunk - 1 - i) * (chunk * SUB), chunk * SUB)
            here = pl.ds(at, chunk * SUB)
            d = dmixed[here, :]
            dbranch_ref[here, :] = (d * hidden_ref[here, :] * slope_ref[here, :]).astype(BF16)
            dhidden = d * act_ref[here, :]
            keep = keep_ref[here, :]
            states = [None] * chunk
            for r in reversed(range(chunk)):
                s = dhidden[r * SUB : (r + 1) * SUB] + after * s
                p = after * p
                after = keep[r * SUB : (r + 1) * SUB]
                states[r] = s
            local_ref[here, :] = jnp.concatenate(states, axis=0)
            out.append((s, p, after))
        return tuple(out)

    one = jnp.ones((SUB, width), F32)
    start = tuple((jnp.zeros((SUB, width), F32), one, one) for _ in range(groups))
    done = lax.fori_loop(0, steps // chunk, step, start)
    for g in range(groups):
        s, p, after = done[g]
        e, f = after * s, after * p
        sege_ref[g * SUB : (g + 1) * SUB, :] = e
        segf_ref[g * SUB : (g + 1) * SUB, :] = f
        a, b = jnp.ones((1, width), F32), jnp.zeros((1, width), F32)
        for r in reversed(range(SUB)):
            b = e[r : r + 1] + f[r : r + 1] * b
            a = f[r : r + 1] * a
        agg_ref[2 * g : 2 * g + 1, :] = a
        agg_ref[2 * g + 1 : 2 * g + 2, :] = b


def mix_back(low, w_out, act, slope, hidden, keep, groups, length):
    rows, dim = low.shape
    recur = keep.shape[1]
    width = 512
    block = columns(rows, width)
    return call(
        functools.partial(mix_back_kernel, groups, length),
        (recur // width,),
        [whole(low.shape), pl.BlockSpec((width, dim), lambda c: (c, 0)), block, block, block, block],
        [block, block, columns(SUB * groups, width), columns(SUB * groups, width), columns(2 * groups, width)],
        [
            struct((rows, recur), BF16), struct((rows, recur), F32), struct((SUB * groups, recur), F32),
            struct((SUB * groups, recur), F32), struct((2 * groups, recur), F32),
        ],
        [pltpu.VMEM((rows, width), F32)],
        2 * rows * dim * recur * 2,
        dim * recur * 2 + rows * recur * 18,
        (low, w_out, act, slope, hidden, keep),
    )


def gates_back_kernel(
    groups, length,
    local_ref, keep_ref, hidden_ref, ext_ref, rate_ref, igate_ref, sege_ref, segf_ref, gin_ref, hin_ref,
    ga_ref, gi_ref, vec_ref, mask_ref,
    din_ref, head_ref, dga_ref, dgi_ref, dvec_ref,
    dconv, low_a, low_i, rounded,
):
    steps = length // SUB
    width = keep_ref.shape[1]
    chunk = 8
    sub = lax.broadcasted_iota(jnp.int32, (SUB, width), 0)
    taps = [vec_ref[k : k + 1, :] for k in range(CONV)]
    conv_bias, scale = vec_ref[4:5, :], vec_ref[7:8, :]
    start = []
    for g in range(groups):
        e = sege_ref[g * SUB : (g + 1) * SUB, :]
        f = segf_ref[g * SUB : (g + 1) * SUB, :]
        y = gin_ref[g : g + 1, :]
        entering = [None] * SUB
        for s in reversed(range(SUB)):
            entering[s] = y
            y = e[s : s + 1] + f[s : s + 1] * y
        start.append((jnp.concatenate(entering, axis=0), jnp.ones((SUB, width), F32)))
    zero = jnp.zeros((SUB, width), F32)

    def fold(v):
        return functools.reduce(jnp.add, [v[q * SUB : (q + 1) * SUB] for q in range(v.shape[0] // SUB)])

    def step(i, carry):
        chains, sum_a, sum_i, sum_d = carry
        out = []
        j = steps // chunk - 1 - i
        for g in range(groups):
            r, after = chains[g]
            at = pl.multiple_of(g * length + j * (chunk * SUB), chunk * SUB)
            here = pl.ds(at, chunk * SUB)
            keep = keep_ref[here, :]
            parts = [None] * chunk
            for q in reversed(range(chunk)):
                r = after * r
                after = keep[q * SUB : (q + 1) * SUB]
                parts[q] = r
            state = local_ref[here, :] + jnp.concatenate(parts, axis=0)
            last = hidden_ref[(g + 1) * length - SUB : (g + 1) * length, :]
            wrapped = jnp.where(sub == 0, hin_ref[g : g + 1, :], pltpu.roll(last, 1, 0))
            before = pl.multiple_of(jnp.maximum(at - SUB, g * length), SUB)
            first = jnp.where(j == 0, wrapped, hidden_ref[pl.ds(before, SUB), :])
            rest = hidden_ref[pl.ds(at, (chunk - 1) * SUB), :]
            previous = jnp.concatenate([first, rest], axis=0)
            inner = pl.multiple_of(j * (chunk * SUB), chunk * SUB)
            conv = conv_bias + taps[0] * ext_ref[g, pl.ds(inner + 3 * SUB, chunk * SUB), :]
            for k in range(1, CONV):
                link = lanes(mask_ref[k, here, :], width)
                conv = conv + taps[k] * (link * ext_ref[g, pl.ds(inner + (3 - k) * SUB, chunk * SUB), :])
            rate, igate = rate_ref[here, :], igate_ref[here, :]
            space = 1.0 + 0.0001 - keep * keep
            inverse = lax.rsqrt(space)
            scaling = space * inverse
            both = state * igate
            dconv[here, :] = both * scaling
            with_conv = both * conv
            dlog = (state * previous - with_conv * (keep * inverse)) * keep
            dpre_a = (dlog * scale) * (rate * (1.0 - rate))
            dpre_i = (with_conv * scaling) * (1.0 - igate)
            low_a[here, :] = dpre_a.astype(BF16)
            low_i[here, :] = dpre_i.astype(BF16)
            rounded[here, :] = conv.astype(BF16)
            sum_a = sum_a + fold(dpre_a)
            sum_i = sum_i + fold(dpre_i)
            sum_d = sum_d + fold(dlog * rate)
            out.append((r, after))
        return tuple(out), sum_a, sum_i, sum_d

    _, sum_a, sum_i, sum_d = lax.fori_loop(0, steps // chunk, step, (tuple(start), zero, zero, zero))
    dvec_ref[5:6, :] = jnp.sum(sum_a, axis=0, keepdims=True)
    dvec_ref[6:7, :] = jnp.sum(sum_i, axis=0, keepdims=True)
    dvec_ref[7:8, :] = jnp.sum(sum_d, axis=0, keepdims=True)
    for h in range(width // LANES):
        col = slice(h * LANES, (h + 1) * LANES)
        dga_ref[h] = tn_dot(rounded[:, col], low_a[:, col])
        dgi_ref[h] = tn_dot(rounded[:, col], low_i[:, col])
        dconv[:, col] += nt_dot(low_a[:, col], ga_ref[h]) + nt_dot(low_i[:, col], gi_ref[h])

    sums = [zero] * (CONV + 1)
    for g in range(groups):

        def conv_step(i, carry, g=g):
            carry = list(carry)
            inner = pl.multiple_of(i * (chunk * SUB), chunk * SUB)
            here = pl.ds(pl.multiple_of(g * length + inner, chunk * SUB), chunk * SUB)
            d = dconv[here, :]
            carry[4] = carry[4] + fold(d)
            for k in range(CONV):
                masked = d if k == 0 else d * lanes(mask_ref[k, here, :], width)
                carry[k] = carry[k] + fold(masked * ext_ref[g, pl.ds(inner + (3 - k) * SUB, chunk * SUB), :])
            return tuple(carry)

        sums = list(lax.fori_loop(0, steps // chunk, conv_step, tuple(sums)))
        base = g * length
        tail = length - 3 * SUB
        total = taps[0] * dconv[base : base + tail, :]
        for k in range(1, CONV):
            there = slice(base + k * SUB, base + k * SUB + tail)
            total = total + taps[k] * (dconv[there, :] * lanes(mask_ref[k, there, :], width))
        din_ref[base : base + tail, :] = total

        def term(k, block):
            there = slice(base + block * SUB, base + (block + 1) * SUB)
            v = taps[k] * dconv[there, :]
            return v if k == 0 else v * lanes(mask_ref[k, there, :], width)

        heads = []
        for i in (3, 2, 1):
            j = steps - i
            value = term(0, j)
            head = None
            for k in range(1, CONV):
                if j + k < steps:
                    value = value + term(k, j + k)
                else:
                    t = term(k, j + k - steps)
                    value = value + jnp.where(sub == SUB - 1, 0.0, pltpu.roll(t, SUB - 1, 0))
                    head = t if head is None else head + t
            din_ref[base + j * SUB : base + (j + 1) * SUB, :] = value
            heads.append(head[0:1])
        head_ref[g * SUB : (g + 1) * SUB, :] = jnp.concatenate(heads + [jnp.zeros((SUB - 3, width), F32)], axis=0)
    for k in range(CONV + 1):
        dvec_ref[k : k + 1, :] = jnp.sum(sums[k], axis=0, keepdims=True)


def gates_back(local, keep, hidden, ext, rate, igate, sege, segf, gin, hin, gate_a, gate_i, vec, masks, groups, length):
    rows, recur = local.shape
    width = 512
    heads = width // LANES
    block = columns(rows, width)
    seg = columns(SUB * groups, width)
    gate = pl.BlockSpec((heads, LANES, LANES), lambda c: (c, 0, 0))
    return call(
        functools.partial(gates_back_kernel, groups, length),
        (recur // width,),
        [
            block, block, block, pl.BlockSpec((groups, length + 3 * SUB, width), lambda c: (0, 0, c)),
            block, block, seg, seg, columns(groups, width), columns(groups, width),
            gate, gate, columns(8, width), whole(masks.shape),
        ],
        [block, seg, gate, gate, columns(8, width)],
        [
            struct((rows, recur), F32), struct((SUB * groups, recur), F32), struct(gate_a.shape, F32),
            struct(gate_a.shape, F32), struct((8, recur), F32),
        ],
        [
            pltpu.VMEM((rows, width), F32), pltpu.VMEM((rows, width), BF16),
            pltpu.VMEM((rows, width), BF16), pltpu.VMEM((rows, width), BF16),
        ],
        rows * recur * 128 * 8 * 4,
        rows * recur * 28,
        (local, keep, hidden, ext, rate, igate, sege, segf, gin, hin, gate_a, gate_i, vec, masks),
    )


def branch_back_kernel(dbranch_ref, w_ref, out_ref):
    part = nt_dot(dbranch_ref[...], w_ref[...])

    @pl.when(pl.program_id(0) == 0)
    def _():
        out_ref[...] = part

    @pl.when(pl.program_id(0) > 0)
    def _():
        out_ref[...] += part


def branch_back(dbranch, w_in, first, dim):
    rows, recur = dbranch.shape
    width = 512
    return call(
        branch_back_kernel,
        (recur // width,),
        [columns(rows, width), columns(dim, width, first // width)],
        whole((rows, dim)),
        struct((rows, dim), F32),
        [],
        2 * rows * dim * recur,
        dim * recur * 2,
        (dbranch, w_in),
    )


def recur_in_back_kernel(
    groups, length,
    part_ref, din_ref, back_ref, wi_ref, x_ref, gain_ref, dmid_ref,
    low_ref, dx_ref, dgain_ref,
    acc,
):
    c = pl.program_id(0)
    width = din_ref.shape[1]
    rim = 4 * SUB
    sub = lax.broadcasted_iota(jnp.int32, (SUB, width), 0)
    for g in range(groups):
        base = g * length
        if length > rim:
            low_ref[base : base + length - rim, :] = din_ref[base : base + length - rim, :].astype(BF16)
        extra = [jnp.zeros((SUB, width), F32)]
        for i in range(3):
            extra.append(jnp.where(sub == SUB - 1, back_ref[g * SUB + i : g * SUB + i + 1, :], 0.0))
        tail = slice(base + length - rim, base + length)
        low_ref[tail, :] = (din_ref[tail, :] + jnp.concatenate(extra, axis=0)).astype(BF16)
    part = nt_dot(low_ref[...], wi_ref[...])

    @pl.when(c == 0)
    def _():
        acc[...] = part_ref[...] + part

    @pl.when(c > 0)
    def _():
        acc[...] += part

    @pl.when(c == pl.num_programs(0) - 1)
    def _():
        back, dgain = norm_back(x_ref[...].astype(F32), gain_ref[...], acc[...])
        dx_ref[...] = (dmid_ref[...] + back).astype(BF16)
        dgain_ref[...] = dgain


def recur_in_back(part, din, back, w_in, first, x, gain, dmid, groups, length):
    rows, dim = x.shape
    recur = din.shape[1]
    width = 512
    block = columns(rows, width)
    full = whole((rows, dim))
    return call(
        functools.partial(recur_in_back_kernel, groups, length),
        (recur // width,),
        [
            full, block, columns(SUB * groups, width), columns(dim, width, (first + recur) // width),
            full, whole(gain.shape), full,
        ],
        [block, full, whole((1, dim))],
        [struct((rows, recur), BF16), struct((rows, dim), BF16), struct((1, dim), F32)],
        [pltpu.VMEM((rows, dim), F32)],
        2 * rows * dim * recur * 1.5,
        2 * dim * recur + rows * recur * 8,
        (part, din, back, w_in, x, gain, dmid),
    )


def outer_kernel(places, pieces, place_ref, left_a, left_b, right_a, right_b, *refs):
    outs, (keep, send) = refs[:-2], refs[-2:]
    n, fs, share = places
    rows = left_a.shape[1]
    c = pl.program_id(0)
    per = pl.num_programs(0) // pieces

    @pl.when(c == 0)
    def _():
        core, y = place_ref[0], place_ref[1]
        for at in range(n):
            there = slice(at * share, (at + 1) * share)
            for scratch, side in ((keep, y), (send, 1 - y)):
                first = pl.multiple_of((at * fs + 2 * side + core) * share, share)
                scratch[there, 0:rows] = left_a[pl.ds(first, share), :]
                scratch[there, rows : 2 * rows] = left_b[pl.ds(first, share), :]

    right = jnp.concatenate([right_a[0], right_b[0]], axis=0)
    to_keep = nn_dot(keep[...], right).astype(BF16)
    to_send = nn_dot(send[...], right).astype(BF16)
    for p in range(pieces):

        @pl.when(c // per == p)
        def _(p=p):
            outs[2 * p][...] = to_keep
            outs[2 * p + 1][...] = to_send


def outer(lefts, at, k, rights, pieces, chosen, place, n, fs):
    rows = lefts[0].shape[1]
    count, _, total = rights[0].shape
    share = k // (n * fs)
    piece = count * total // pieces
    width = next(w for w in (768, 512, 384, 256, 128, piece) if piece % w == 0)
    across, per = total // width, piece // width
    skipped, pieces = chosen[0] * per, chosen[1]

    def out_block(p):
        return pl.BlockSpec((n * share, width), lambda c, place: (0, jnp.clip(c - p * per, 0, per - 1)))

    left = pl.BlockSpec((k, rows), lambda c, place: (at // k, 0))
    right = pl.BlockSpec((1, rows, width), lambda c, place: ((c + skipped) // across, 0, (c + skipped) % across))
    outs = pl.pallas_call(
        functools.partial(outer_kernel, (n, fs, share), pieces),
        grid_spec=pltpu.PrefetchScalarGridSpec(
            num_scalar_prefetch=1,
            grid=(pieces * per,),
            in_specs=[left, left, right, right],
            out_specs=[out_block(p) for p in range(pieces) for _ in range(2)],
            scratch_shapes=[pltpu.VMEM((n * share, 2 * rows), BF16)] * 2,
        ),
        out_shape=[struct((n * share, piece), BF16)] * (2 * pieces),
        compiler_params=pltpu.CompilerParams(dimension_semantics=("arbitrary",), vmem_limit_bytes=VMEM_BYTES),
        cost_estimate=pl.CostEstimate(
            flops=8 * n * share * rows * pieces * piece // COST, bytes_accessed=1, transcendentals=0
        ),
    )(place, *lefts, *rights)
    return [(outs[2 * p], outs[2 * p + 1]) for p in range(pieces)]


def unfold_kernel(folded_ref, out_ref):
    height, width = folded_ref.shape[0], out_ref.shape[1]
    for q in range(out_ref.shape[0] // height):
        out_ref[q * height : (q + 1) * height, :] = folded_ref[:, q * width : (q + 1) * width]


def unfold_first(packed, places, height, rows, width):
    return call(
        unfold_kernel,
        (places,),
        [pl.BlockSpec((height, rows // height * width), lambda c: (c, 0))],
        pl.BlockSpec((rows, width), lambda c: (c, 0)),
        struct((places * rows, width), packed.dtype),
        [],
        0,
        places * rows * width * 4,
        (packed,),
    )


def shifted(value, axis, by):
    length = lax.axis_size(axis)
    pairs = [(i, i + by) for i in range(length) if 0 <= i + by < length]
    return lax.ppermute(value, axis, pairs)


def entering(agg, groups, reverse):
    n = lax.axis_size("seq")
    sign = -1 if reverse else 1
    got = {k: shifted(agg, "seq", sign * k) for k in range(1, n)}
    state = jnp.zeros((groups, agg.shape[1]), F32)
    for k in range(n - 1, 0, -1):
        part = got[k].reshape(groups, 2, -1)
        state = part[:, 0] * state + part[:, 1]
    return state


def add(*parts):
    return functools.reduce(jnp.add, [p.astype(F32) for p in parts])


def line_sum(slots, mine, n, send):
    def at(offset):
        return slots((mine + offset) % n)

    up, down = at(n - 1), at(1)
    for s in range(1, n):
        got_up = send(up, [(i, i + 1) for i in range(s)])
        got_down = send(down, [(i, i - 1) for i in range(n - s, n)])
        if s < n - 1:
            up = add(at(n - 1 - s), got_up).astype(BF16)
            down = add(at(s + 1), got_down).astype(BF16)
    return add(at(0), got_up, got_down)


class Scatter:
    def __init__(self):
        self.n, self.fs = lax.axis_size("seq"), lax.axis_size("fsdp")
        self.ny = self.fs // 2
        self.z, f = lax.axis_index("seq"), lax.axis_index("fsdp")
        self.y, self.core = f // 2, f % 2

    def core_swap(self, value):
        return lax.ppermute(value, "fsdp", [(i, i ^ 1) for i in range(self.fs)])

    def y_send(self, value, pairs):
        return lax.ppermute(value, "fsdp", [(2 * a + c, 2 * b + c) for a, b in pairs for c in range(2)])

    def over_y(self, keep, send, since, beside):
        return add(after(keep, beside), self.y_send(after(send, since), [(0, 1), (1, 0)])).astype(BF16)

    def over_z(self, shares):
        return lax.psum_scatter(shares, "seq", scatter_dimension=0, tiled=True)[0].astype(F32)


def pick(value, index, axis):
    return lax.dynamic_index_in_dim(value, index, axis, keepdims=False)


def reorder(v):
    length, d = v.shape[-2:]
    return jnp.swapaxes(v.reshape(-1, SUB, length // SUB, d), 1, 2).reshape(-1, d)


def restore(v, shape):
    length, d = shape[-2:]
    return jnp.swapaxes(v.reshape(-1, length // SUB, SUB, d), 1, 2).reshape(shape)


def tail_rows(v, groups, length):
    d = v.shape[1]
    last = v.reshape(groups, length // SUB, SUB, d)[:, length // SUB - 3 :, SUB - 1]
    last = jnp.pad(last, ((0, 0), (0, SUB - 3), (0, 0))).reshape(groups * SUB, d)
    return jnp.pad(last, ((0, -groups * SUB % 16), (0, 0)))


def fold_rows(v, height):
    count = -(-v.shape[0] // height)
    v = jnp.pad(v, ((0, count * height - v.shape[0]), (0, 0)))
    return jnp.concatenate([v[i * height : (i + 1) * height] for i in range(count)], axis=1)


def fold_places(v, height):
    places, rows, width = v.shape
    count = -(-rows // height)
    v = jnp.pad(v, ((0, 0), (0, count * height - rows), (0, 0))).reshape(places, count, height, width)
    return jnp.swapaxes(v, 1, 2).reshape(places, height, count * width)


def unfold_rows(v, rows, width):
    places, height, total = v.shape
    v = jnp.swapaxes(v.reshape(places, height, total // width, width), 1, 2)
    return v.reshape(places, -1, width)[:, :rows]


def after(value, *others):
    return lax.optimization_barrier((value, others))[0]


def gather(shard):
    return lax.all_gather(shard, ("seq", "fsdp"), axis=0, tiled=True)


def body(
    ends, segment_ids, norm_one, w_branch, w_input, conv_weight, conv_bias, gate_a, gate_i, bias_a, bias_i,
    decay, w_out, norm_two, w_gate, w_up, w_down,
):
    is_first = lax.axis_index("section") == 0
    z = lax.axis_index("seq")
    n, fs = lax.axis_size("seq"), lax.axis_size("fsdp")
    places = n * fs
    micro, seqs, length, dim = ends.shape[1:]
    parts_of = 1
    groups = micro * seqs // parts_of
    rows = groups * length
    recur = w_branch.shape[2]
    heads, part, block = gate_a.shape[1:]
    hidden_dim = w_gate.shape[2]

    dshare, rshare = dim // places, recur // places
    vectors = [norm_one, norm_two] + [conv_weight[:, k] for k in range(CONV)] + [conv_bias, bias_a, bias_i, decay]
    vectors = jnp.concatenate([jnp.pad(v, ((0, 0), (0, LANES - v.shape[1]))) for v in vectors], axis=0)
    vectors = jnp.pad(vectors, ((0, 2 * SUB - vectors.shape[0]), (0, 0)))
    small = jnp.concatenate([vectors, gate_a.reshape(-1, block), gate_i.reshape(-1, block)], axis=0)
    small_rows = small.shape[0]
    small = fold_rows(small, dshare)
    first = hidden_dim
    w_in = gather(
        jnp.concatenate(
            [fold_rows(w_down[0], dshare), w_branch[0], w_input[0], w_out[0].reshape(dshare, recur), small], axis=1
        )
    )
    w_gu = gather(jnp.concatenate([after(w_gate[0], small), w_up[0]], axis=1))
    w_out_all = w_in[:, first + 2 * recur : first + 3 * recur].reshape(recur, dim)
    small = unfold_rows(w_in[:, first + 3 * recur :].reshape(places, dshare, -1), small_rows, LANES)
    hshare = hidden_dim // places
    if dshare % 16 == 0:
        w_down_all = unfold_first(w_in, places, dshare, hshare, dim)
    else:
        w_down_all = unfold_rows(w_in[:, :first].reshape(places, dshare, -1), hshare, dim).reshape(hidden_dim, dim)

    def vector(row, share):
        return small[:, row, :share].reshape(1, places * share).astype(F32)

    gain_one, gain_two = vector(0, dshare), vector(1, dshare)
    decays = vector(9, rshare)
    vec = jnp.concatenate([vector(r, rshare) for r in range(2, 9)] + [-8.0 * jax.nn.softplus(decays)], axis=0)
    gates_a, gates_i = [
        jnp.swapaxes(small[:, r : r + heads * part].reshape(places, heads, part, block), 0, 1).reshape(heads, block, block)
        for r in (2 * SUB, 2 * SUB + heads * part)
    ]

    padded_ids = jnp.pad(segment_ids, ((0, 0), (0, 0), (CONV - 1, 0)), constant_values=-1)
    window = lax.dynamic_slice_in_dim(padded_ids, z * length, length + CONV - 1, axis=2)
    current = window[:, :, CONV - 1 :]
    masks = jnp.stack(
        [window[:, :, CONV - 1 - k : CONV - 1 - k + length] == current for k in (1, 1, 2, 3)]
    ).astype(F32)
    masks = jnp.swapaxes(masks.reshape(4, parts_of, groups, SUB, length // SUB), 3, 4).reshape(4, parts_of, rows, 1)
    masks = jnp.broadcast_to(masks, (4, parts_of, rows, LANES))
    masks = [masks[:, m] for m in range(parts_of)]
    micros = range(parts_of)

    def forward(xs, halos, save):
        got = []
        for m in micros:
            got.append(recur_in(xs[m], halos[m], gain_one, w_in, first, gates_a, gates_i, vec, masks[m], groups, length))
        hin = entering(jnp.concatenate([g[7] for g in got], axis=0), parts_of * groups, False)
        acts = [branch_in(after(g[0], got[-1][7]), w_in, first, recur) for g in got]
        outs, saved = [], []
        for m in micros:
            normed, ext, rate, igate, keep, local, segp, _ = got[m]
            act, slope = acts[m]
            mine = hin[m * groups : (m + 1) * groups]
            if m:
                keep = after(keep, outs[-1])
            hidden, mixed, middle, normed_two = recur_out(
                xs[m], keep, local, act, segp, mine, w_out_all, gain_two, groups, length
            )
            results = feed_forward(normed_two, middle, w_gu, w_down_all, save)
            outs.append(results[-1])
            saved.append(
                (normed, ext, rate, igate, keep, mine, hidden, mixed, middle, normed_two, act, slope) + tuple(results[:-1])
            )
        return outs, saved

    def back_ff(m, dout, saved, dproduct=None):
        return feed_forward_back(dout, saved[m][8], gain_two, saved[m][12], saved[m][13], w_gu, w_down_all, dproduct)

    def back_mix(m, low, saved):
        return mix_back(low, w_out_all, saved[m][10], saved[m][11], saved[m][6], saved[m][4], groups, length)

    def back_gates(m, mixed_back, gin, saved):
        normed, ext, rate, igate, keep, hin, hidden = saved[m][:7]
        _, local, sege, segf, _ = mixed_back
        din, head, dga, dgi, dvec = gates_back(
            local, keep, hidden, ext, rate, igate, sege, segf, gin[m * groups : (m + 1) * groups], hin,
            gates_a, gates_i, vec, masks[m], groups, length,
        )
        return din, shifted(head, "seq", -1), dga, dgi, dvec

    def back_in(m, part, gates, dmid, xs):
        return recur_in_back(part, gates[0], gates[1], w_in, first, xs[m], gain_one, dmid, groups, length)

    own = [reorder(v) for v in ends[0].reshape((parts_of, -1) + ends.shape[3:])]
    tails = [shifted(tail_rows(v, groups, length), "seq", 1) for v in own]
    outs, _ = forward(own, tails, False)
    xs, halos = [], []
    for m in micros:
        dproduct = down_back(after(own[m], outs[m]), w_down_all)
        received = after(shifted(outs[m], "section", 1), dproduct)
        received_halo = lax.ppermute(
            tail_rows(outs[m], groups, length), ("section", "seq"), [(i, n + i + 1) for i in range(n - 1)]
        )
        xs.append(jnp.where(is_first, own[m], received))
        halos.append(jnp.where(is_first, tails[m], received_halo))
    outs, saved = forward(xs, halos, True)

    scatter = Scatter()
    swap = scatter.core_swap
    place = jnp.stack([scatter.core, scatter.y]).astype(jnp.int32)

    ff = back_ff(0, own[0], saved, dproduct)
    mix = back_mix(0, ff[2], saved)
    gin = entering(mix[4], groups, True)
    product_t = saved[0][14]
    product_pair = (product_t, swap(after(product_t, mix[4])))
    gates = back_gates(0, mix, gin, saved)
    base = branch_back(after(mix[0], gates[0]), w_in, first, dim)
    dx = back_in(0, base, gates, ff[1], xs)[1]
    others = [after(saved[0][i], dx) for i in (9, 0, 7)]
    starts_at, total_rows = [], 0
    for i, v in enumerate(others):
        gap = -total_rows % v.shape[1]
        if gap:
            others[i] = jnp.concatenate([jnp.zeros((rows, gap), BF16), v], axis=1)
        starts_at.append((total_rows + gap, v.shape[1]))
        total_rows += gap + v.shape[1]
    others = jnp.concatenate([v.T for v in others], axis=0)
    received = after(shifted(dx, "section", -1), others, product_pair)
    others = after(others, received)
    others = (others, swap(others))
    lefts = {"product": (product_pair, 0, hidden_dim)}
    for name, (at, k) in zip(("two", "one", "mixed"), starts_at):
        lefts[name] = (others, at, k)
    dout = jnp.where(is_first, received, own[0])

    def pair(value):
        value = value if value.ndim == 3 else value[None]
        return value, swap(value)

    def products(name, rights, pieces=1, chosen=None):
        both, at, k = lefts[name]
        chosen = chosen or (0, pieces)
        if scatter.ny == 2:
            return outer(both, at, k, rights, pieces, chosen, place, n, fs)
        left = jnp.concatenate([v[at : at + k] for v in both], axis=1)
        right = jnp.concatenate([jnp.concatenate(list(v), axis=1) for v in rights], axis=0)
        grad = nn_dot(left, right).astype(BF16)
        grad = pick(grad.reshape(n, scatter.ny, 2, -1, grad.shape[1]), scatter.core, 2)
        return [(p,) for p in jnp.split(grad, pieces, axis=3)[chosen[0] : sum(chosen)]]

    def over_y(grads, since, *beside):
        if scatter.ny == 2:
            return scatter.over_y(*[g.reshape(n, -1, g.shape[1]) for g in grads], since, beside)
        (grad,) = grads
        return line_sum(lambda d: pick(grad, d, 1), scatter.y, scatter.ny, scatter.y_send).astype(BF16)

    down = products("product", pair(dout), 2)
    dgu, dmid, out_low, dgain_two = back_ff(0, after(dout, down), saved)
    down_sums = [over_y(down[0], (), out_low)]
    down_sums.append(None)
    gu_pair = pair(after(dgu, down_sums[0]))
    mix = back_mix(0, after(out_low, down_sums[0]), saved)
    gate_up = products("two", after(gu_pair, mix[0]), 4, (0, 1))
    down_sums[1] = over_y(down[1], out_low, gate_up[0])
    gin = entering(after(mix[4], down_sums[1]), groups, True)
    gate_up += products("two", after(gu_pair, down_sums[1]), 4, (1, 3))
    gate_up_sums = [over_y(gate_up[0], (), gate_up[1], gin)]
    gates = back_gates(0, after(mix, gate_up_sums[0]), gin, saved)
    gate_up_sums.append(over_y(gate_up[1], gin, gates[0]))
    out_low, dbranch = after((out_low, mix[0]), gate_up_sums[1])
    out_pair, branch_pair = pair(out_low), pair(dbranch)
    base = branch_back(dbranch, w_in, first, dim)
    results = back_in(0, base, gates, dmid, xs)
    gate_up_sums.append(over_y(gate_up[2], gates[0], results[1], out_pair[1], branch_pair[1]))
    input_pair = pair(after(results[0], gate_up_sums[2]))
    out = products("mixed", after(out_pair, gate_up_sums[2]))
    branch = products("one", after(branch_pair, out))
    dgain_one = results[2]
    dga, dgi, dvec = gates[2:5]
    ddecay = -8.0 * jax.nn.sigmoid(decays) * dvec[7:8]
    shares = [dgain_one, dgain_two] + [dvec[k : k + 1] for k in range(7)] + [ddecay]
    shares = [v.reshape(places, 1, -1) for v in shares]
    shares = [jnp.pad(v, ((0, 0), (0, 0), (0, LANES - v.shape[2]))) for v in shares]
    shares = jnp.pad(jnp.concatenate(shares, axis=1), ((0, 0), (0, 2 * SUB - len(shares)), (0, 0)))
    packed = jnp.concatenate(
        [shares]
        + [jnp.swapaxes(v.reshape(heads, places, part, block), 0, 1).reshape(places, -1, block) for v in (dga, dgi)],
        axis=1,
    )
    extra = fold_places(packed, dshare).reshape(n, scatter.ny, 2, dshare, -1)
    theirs = swap(pick(extra, 1 - scatter.core, 2).astype(BF16))
    extra = add(pick(extra, scatter.core, 2), theirs).astype(BF16)
    gate_up_sums.append(over_y(gate_up[3], results[1], branch, extra))
    into = products("one", after(input_pair, gate_up_sums[3]))
    out_sum = over_y(out[0], branch, into)
    if scatter.ny == 2:
        sides = (pick(extra, scatter.y, 1), pick(extra, 1 - scatter.y, 1))
        last = [
            jnp.concatenate([g.reshape(n, dshare, -1), v], axis=2).reshape(n * dshare, -1) for g, v in zip(into[0], sides)
        ]
    else:
        last = (jnp.concatenate([into[0][0], extra], axis=3),)
    branch_sum = over_y(branch[0], out_sum, last)
    input_sum = over_y(last, branch_sum)

    outputs = restore(outs[0], ends.shape)
    input_grads = restore(results[1], ends.shape)
    shares = down_sums + gate_up_sums + [out_sum, branch_sum, input_sum]
    for i in range(1, len(shares)):
        shares[i] = after(shares[i], shares[i - 1])
    totals = [scatter.over_z(v) for v in shares]
    sum_down, sum_gate, sum_up = [jnp.concatenate(totals[i : i + 2], axis=1) for i in (0, 2, 4)]
    sum_out, sum_branch, sum_input = totals[6:]
    sum_input, sums = sum_input[:, :recur], sum_input[:, recur:]
    sums = unfold_rows(sums[None], small_rows, LANES)[0]
    gate_sums = [sums[r : r + heads * part].reshape(gate_a.shape) for r in (2 * SUB, 2 * SUB + heads * part)]

    return (
        outputs,
        input_grads,
        sums[0:1, :dshare],
        sum_branch[None],
        sum_input[None],
        sums[2 : 2 + CONV, :rshare][None],
        sums[6:7, :rshare],
        gate_sums[0],
        gate_sums[1],
        sums[7:8, :rshare],
        sums[8:9, :rshare],
        sums[9:10, :rshare],
        sum_out[None],
        sums[1:2, :dshare],
        sum_gate[None],
        sum_up[None],
        sum_down[None],
    )


def solution(mesh):
    tokens = P("section", None, "fsdp", "seq", None)
    vector = P("section", ("seq", "fsdp"))
    matrix = P("section", ("seq", "fsdp"), None)
    taps = P("section", None, ("seq", "fsdp"))
    gates = P("section", None, ("seq", "fsdp"), None)
    weights = (
        vector, matrix, matrix, taps, vector, gates, gates, vector, vector, vector, matrix, vector, matrix, matrix, matrix,
    )
    return jax.shard_map(
        body,
        mesh=mesh,
        in_specs=(tokens, P(None, "fsdp", None)) + weights,
        out_specs=(tokens, tokens) + weights,
        check_vma=False,
    )
```
